32 devices in a mesh: dp: 8 (over y, x, core), seq: 4 (over z).
Axes of the slice: x: 2, y: 2, z: 4, core: 2. Of those that a mesh axis runs over, the one named last changes fastest.
Arguments:
- inputs: bfloat16 [16, 2048, 768], P('dp', 'seq'), may hold values from -6 to 6
- cotangent: bfloat16 [16, 2048, 768], P('dp', 'seq'), may hold values from -6 to 6
- rand_blocks: int32 [16, 12, 32, 3], P('dp', None, 'seq'), may hold values from 0 to 31
- global_blocks: int32 [16, 2], P('dp'), may hold values from 0 to 31
- w_query: bfloat16 [768, 768], P(('dp', 'seq')), may hold values from -0.21875 to 0.21875
- b_query: bfloat16 [768], P(('dp', 'seq')), may hold values from -3 to 3
- w_key: bfloat16 [768, 768], P(('dp', 'seq')), may hold values from -0.21875 to 0.21875
- w_value: bfloat16 [768, 768], P(('dp', 'seq')), may hold values from -0.21875 to 0.21875
- b_value: bfloat16 [768], P(('dp', 'seq')), may hold values from -3 to 3
- w_out: bfloat16 [768, 768], P(('dp', 'seq')), may hold values from -1.25 to 1.25
- b_out: bfloat16 [768], P(('dp', 'seq')), may hold values from -3 to 3
- gain_one: bfloat16 [768], P(('dp', 'seq')), may hold values from 0.5 to 1.5
- shift_one: bfloat16 [768], P(('dp', 'seq')), may hold values from -3 to 3
- w_up: bfloat16 [768, 3072], P(('dp', 'seq')), may hold values from -0.21875 to 0.21875
- b_up: bfloat16 [3072], P(('dp', 'seq')), may hold values from -3 to 3
- w_down: bfloat16 [3072, 768], P(('dp', 'seq')), may hold values from -0.109375 to 0.109375
- b_down: bfloat16 [768], P(('dp', 'seq')), may hold values from -3 to 3
- gain_two: bfloat16 [768], P(('dp', 'seq')), may hold values from 0.5 to 1.5
- shift_two: bfloat16 [768], P(('dp', 'seq')), may hold values from -3 to 3
Outputs:
- output: bfloat16 [16, 2048, 768], P('dp', 'seq')
- grad_inputs: bfloat16 [16, 2048, 768], P('dp', 'seq')
- grad_w_query: float32 [768, 768], P(('dp', 'seq'))
- grad_b_query: float32 [768], P(('dp', 'seq'))
- grad_w_key: float32 [768, 768], P(('dp', 'seq'))
- grad_w_value: float32 [768, 768], P(('dp', 'seq'))
- grad_b_value: float32 [768], P(('dp', 'seq'))
- grad_w_out: float32 [768, 768], P(('dp', 'seq'))
- grad_b_out: float32 [768], P(('dp', 'seq'))
- grad_gain_one: float32 [768], P(('dp', 'seq'))
- grad_shift_one: float32 [768], P(('dp', 'seq'))
- grad_w_up: float32 [768, 3072], P(('dp', 'seq'))
- grad_b_up: float32 [3072], P(('dp', 'seq'))
- grad_w_down: float32 [3072, 768], P(('dp', 'seq'))
- grad_b_down: float32 [768], P(('dp', 'seq'))
- grad_gain_two: float32 [768], P(('dp', 'seq'))
- grad_shift_two: float32 [768], P(('dp', 'seq'))
The draws below stay inside these ranges and needn't reach their ends.
Inputs may be any that keep to these rules, and one draw needn't show every extreme that they name: `rand_blocks`: block numbers of one sequence. `global_blocks`: block numbers of one sequence, possibly equal.
All inputs are finite; a program needn't handle non-finite values.
Results may differ from the reference program's by a relative error of at most 0.015.
Values may be sent and summed in bfloat16 or wider, within the bound.
No kernel may reach another device: no remote copies, remote signals or barrier semaphores. Data moves between devices by JAX's collectives and lax.ppermute only.
A program may use at most 384 MiB of HBM per device.

```python
import jax
import jax.numpy as jnp
from jax import lax

D = 768
HEADS = 12
HEAD = 64
FF = 3072
BLOCK = 64
RANDOM = 3
GLOBAL = 2
LENGTH = 2048
SEQS = 16
NBLOCKS = 32


def set_ends(values, own_key, least, largest):
    shape = values.shape
    index_at = [jax.random.randint(jax.random.fold_in(own_key, axis), (), 0, shape[axis]) for axis in range(len(shape))]
    values = values.at[tuple(index_at)].set(least)
    longest = shape.index(max(shape))
    index_at[longest] = (index_at[longest] + 1) % shape[longest]
    return values.at[tuple(index_at)].set(largest)


def levels(rng, shape, cuts, least, high):
    def one(axis_at, shards_of):
        draws = jax.random.uniform(jax.random.fold_in(jax.random.fold_in(rng, 6), axis_at), (shards_of,), jnp.float32, least / len(cuts), high / len(cuts))
        return jnp.repeat(jnp.exp(draws), shape[axis_at] // shards_of).reshape((-1,) + (1,) * (len(shape) - axis_at - 1))

    factor_of = one(*cuts[0])
    for cut in cuts[1:]:
        factor_of = factor_of * one(*cut)
    return factor_of


def bell_draw(key, shape, scale, reach, split=(), kind=jnp.bfloat16):
    loudness = levels(key, shape, split, -0.22, 0.18) if split else 1.0
    array = jax.random.normal(key, shape, jnp.float32) * scale * loudness
    return jnp.minimum(jnp.maximum(array, -reach), reach).astype(kind)


def setup_inputs(seed: int = 0) -> dict:
    arg_keys = jax.random.split(jax.random.key(seed), 20)
    inputs = bell_draw(arg_keys[0], (SEQS, LENGTH, D), 1.0, 6.0, ((0, 8), (1, 4)))
    cotangent = bell_draw(arg_keys[1], (SEQS, LENGTH, D), 1.0, 6.0, ((0, 8), (1, 4)))
    rand_blocks = set_ends(jax.random.randint(arg_keys[2], (SEQS, HEADS, NBLOCKS, RANDOM), 0, NBLOCKS), jax.random.fold_in(arg_keys[2], 1), 0, NBLOCKS - 1).astype(jnp.int32)
    global_blocks = set_ends(jax.random.randint(arg_keys[3], (SEQS, GLOBAL), 0, NBLOCKS), jax.random.fold_in(arg_keys[3], 1), 0, NBLOCKS - 1).astype(jnp.int32)
    w_query = bell_draw(arg_keys[4], (D, D), D ** -0.5, 0.21875, ((0, 32),))
    b_query = bell_draw(arg_keys[5], (D,), 0.5, 3.0, ((0, 32),))
    w_key = bell_draw(arg_keys[6], (D, D), D ** -0.5, 0.21875, ((0, 32),))
    w_value = bell_draw(arg_keys[7], (D, D), D ** -0.5, 0.21875, ((0, 32),))
    b_value = bell_draw(arg_keys[8], (D,), 0.5, 3.0, ((0, 32),))
    w_out = bell_draw(arg_keys[9], (D, D), (D // 32) ** -0.5, 1.25, ((0, 32),))
    b_out = bell_draw(arg_keys[10], (D,), 0.5, 3.0, ((0, 32),))
    gain_one = jnp.clip(1.0 + 0.1 * jax.random.normal(arg_keys[11], (D,), jnp.float32), 0.5, 1.5).astype(jnp.bfloat16)
    shift_one = bell_draw(arg_keys[12], (D,), 0.5, 3.0, ((0, 32),))
    w_up = bell_draw(arg_keys[13], (D, FF), D ** -0.5, 0.21875, ((0, 32),))
    b_up = bell_draw(arg_keys[14], (FF,), 0.5, 3.0, ((0, 32),))
    w_down = bell_draw(arg_keys[15], (FF, D), FF ** -0.5, 0.109375, ((0, 32),))
    b_down = bell_draw(arg_keys[16], (D,), 0.5, 3.0, ((0, 32),))
    gain_two = jnp.clip(1.0 + 0.1 * jax.random.normal(arg_keys[17], (D,), jnp.float32), 0.5, 1.5).astype(jnp.bfloat16)
    shift_two = bell_draw(arg_keys[18], (D,), 0.5, 3.0, ((0, 32),))
    return {"inputs": inputs, "cotangent": cotangent, "rand_blocks": rand_blocks, "global_blocks": global_blocks, "w_query": w_query, "b_query": b_query, "w_key": w_key, "w_value": w_value, "b_value": b_value, "w_out": w_out, "b_out": b_out, "gain_one": gain_one, "shift_one": shift_one, "w_up": w_up, "b_up": b_up, "w_down": w_down, "b_down": b_down, "gain_two": gain_two, "shift_two": shift_two}


EPS = 1e-06
NEG = -1e+30

@jax.custom_vjp
def low(v):
    return lax.optimization_barrier(v.astype(jnp.bfloat16)).astype(jnp.float32)

@jax.custom_vjp
def low_back(v):
    return v

def low_keep(v):
    return (low(v), None)

def low_pass(kept, grad):
    return (grad,)

def back_keep(v):
    return (v, None)

def back_low(kept, grad):
    return (low(grad),)
low.defvjp(low_keep, low_pass)
low_back.defvjp(back_keep, back_low)

def layer_norm(summed, gain, shift):
    center = summed - lax.optimization_barrier(jnp.mean(summed, -1, keepdims=True))
    spread = lax.optimization_barrier(jnp.mean(center * center, -1, keepdims=True))
    return center * lax.rsqrt(spread + EPS) * gain + shift

def block_mask(rand_rows, glob_ids):
    blocks = jnp.arange(NBLOCKS, dtype=jnp.int32)
    nearby = jnp.abs(blocks[:, None] - blocks[None, :]) <= 1
    glob_hit = jnp.any(blocks[:, None] == glob_ids[None, :], axis=1)
    base = nearby | glob_hit[None, :] | glob_hit[:, None]
    rand_hit = jnp.any(rand_rows[:, :, :, None] == blocks[None, None, None, :], axis=2)
    return base[None, :, :] | rand_hit

def sequence_forward(params, tokens, allowed):
    w_query, b_query, w_key, w_value, b_value, w_out, b_out, gain_one, shift_one, w_up, b_up, w_down, b_down, gain_two, shift_two = params
    highest = lax.Precision.HIGHEST
    queries = low_back(low(jnp.dot(tokens, w_query, precision=highest) + b_query))
    keys = low_back(low(jnp.dot(tokens, w_key, precision=highest)))
    values = low_back(low(jnp.dot(tokens, w_value, precision=highest) + b_value))
    q_heads = queries.reshape(LENGTH, HEADS, HEAD)
    k_heads = keys.reshape(LENGTH, HEADS, HEAD)
    v_heads = values.reshape(LENGTH, HEADS, HEAD)
    scores = jnp.einsum('qhe,khe->hqk', q_heads, k_heads, precision=highest) * HEAD ** (-0.5)
    scores = low_back(scores)
    scores = scores.reshape(HEADS, NBLOCKS, BLOCK, NBLOCKS, BLOCK)
    scores = jnp.where(allowed[:, :, None, :, None], scores, NEG).reshape(HEADS, LENGTH, LENGTH)
    highest_score = lax.optimization_barrier(jnp.max(scores, -1, keepdims=True))
    weights_exp = jnp.exp(scores - highest_score)
    prob = weights_exp / lax.optimization_barrier(jnp.sum(weights_exp, -1, keepdims=True))
    attended = jnp.einsum('hqk,khe->qhe', low(prob), v_heads, precision=highest).reshape(LENGTH, D)
    attended = low_back(low(attended))
    branch = low_back(jnp.dot(attended, w_out, precision=highest) + b_out)
    first_sum = tokens + branch
    normed = layer_norm(first_sum, gain_one, shift_one)
    hidden_pre = low_back(jnp.dot(low(normed), w_up, precision=highest) + b_up)
    hidden = low(jax.nn.gelu(hidden_pre, approximate=False))
    down = low_back(jnp.dot(hidden, w_down, precision=highest) + b_down)
    return layer_norm(normed + down, gain_two, shift_two)

def reference(inputs, cotangent, rand_blocks, global_blocks, w_query, b_query, w_key, w_value, b_value, w_out, b_out, gain_one, shift_one, w_up, b_up, w_down, b_down, gain_two, shift_two):
    params = tuple((p.astype(jnp.float32) for p in (w_query, b_query, w_key, w_value, b_value, w_out, b_out, gain_one, shift_one, w_up, b_up, w_down, b_down, gain_two, shift_two)))

    def mask_one(member):
        return block_mask(member[0], member[1])
    masks = lax.map(mask_one, (rand_blocks, global_blocks))
    step = jax.checkpoint(sequence_forward)

    def run(tokens, weights):

        def one_sequence(member):
            return step(weights, member[0], member[1])
        return lax.map(one_sequence, (tokens, masks))
    result, back = jax.vjp(run, inputs.astype(jnp.float32), params)
    grad_tokens, grads = back(cotangent.astype(jnp.float32))
    g_wq, g_bq, g_wk, g_wv, g_bv, g_wo, g_bo, g_ga, g_sa, g_wu, g_bu, g_wd, g_bd, g_gb, g_sb = grads
    return (result.astype(jnp.bfloat16), grad_tokens.astype(jnp.bfloat16), g_wq, g_bq, g_wk, g_wv, g_bv, g_wo, g_bo, g_ga, g_sa, g_wu, g_bu, g_wd, g_bd, g_gb, g_sb)
```

```python
from functools import partial

import jax
import jax.numpy as jnp
from jax import lax
from jax.experimental import pallas as pl
from jax.experimental.pallas import tpu as pltpu
from jax.sharding import PartitionSpec as P

HEADS = 12
HEAD = 64
BLOCK = 64
SLOTS = 8
EPS = 1e-06
NEG = -1e30
LOW = jnp.bfloat16
WIDE = jnp.float32

NT = (((1,), (1,)), ((), ()))
TN = (((0,), (0,)), ((), ()))
NN = (((1,), (0,)), ((), ()))


def dot(left, right, dims):
    return lax.dot_general(left, right, dims, preferred_element_type=WIDE)


def swap(array):
    size = lax.axis_size("dp")
    return lax.ppermute(array, "dp", [(i, i ^ 1) for i in range(size)])


def flip_chip(array, bit):
    size = lax.axis_size("dp")
    return lax.ppermute(array, "dp", [(i, i ^ (2 << bit)) for i in range(size)])


def flip_seq(array, k):
    size = lax.axis_size("seq")
    return lax.ppermute(array, "seq", [(i, i ^ k) for i in range(size)])


def rounds():
    dp, seq = lax.axis_size("dp"), lax.axis_size("seq")
    for a in range(2):
        for b in range(2):
            pairs = []
            for d in range(dp):
                for z in range(seq):
                    to_dp = (d & ~1) | (b ^ (z >> 1))
                    to_seq = 2 * (d & 1) + (a ^ (z & 1))
                    pairs.append((d * seq + z, to_dp * seq + to_seq))
            yield a, b, pairs


def bring(piece_of):
    z = lax.axis_index("seq")
    got = []
    for a, b, pairs in rounds():
        piece = piece_of(a ^ (z & 1), b ^ (z >> 1))
        got.append(lax.ppermute(piece, ("dp", "seq"), pairs))
    return got


def send_back(pieces):
    z = lax.axis_index("seq")
    got = []
    for at, (a, b, pairs) in enumerate(rounds()):
        got.append(lax.ppermute(pieces[at], ("dp", "seq"), [(t, s) for s, t in pairs]))
    odd, high = (z & 1) == 1, (z >> 1) == 1
    parts = []
    for s in range(2):
        for half in range(2):
            near = jnp.where(odd, got[2 * (1 - s) + half], got[2 * s + half])
            far = jnp.where(odd, got[2 * (1 - s) + 1 - half], got[2 * s + 1 - half])
            parts.append(jnp.where(high, far, near))
    return jnp.stack([jnp.concatenate(parts[:2], 0), jnp.concatenate(parts[2:], 0)])


def pick(array, index, axis):
    return lax.dynamic_slice_in_dim(array, index, 1, axis)


def gather_chips(shard):
    z = lax.axis_index("seq")
    chip = lax.axis_index("dp") >> 1
    pieces = [shard] + [flip_seq(shard, k) for k in range(1, lax.axis_size("seq"))]
    for bit in range(2):
        set_bit = ((z >> bit) & 1) == 1
        pieces = [
            jnp.where(set_bit, pieces[i ^ (1 << bit)], pieces[i]) for i in range(len(pieces))
        ]
    whole = jnp.stack(pieces, 1)[None]
    size = lax.axis_size("dp") // 2
    bit = 0
    while (1 << bit) < size:
        other = flip_chip(whole, bit)
        set_bit = ((chip >> bit) & 1) == 1
        whole = jnp.concatenate(
            [jnp.where(set_bit, other, whole), jnp.where(set_bit, whole, other)], 0
        )
        bit += 1
    return whole


def reduce_chips(parts, first):
    chip = lax.axis_index("dp") >> 1
    z = lax.axis_index("seq")
    size = parts.shape[0]
    count = size.bit_length() - 1
    tail = parts.shape[1:]
    parts = parts.reshape((2,) * count + tail)
    order = list(range(count))
    if first and count > 1:
        order = order[1:] + order[:1]
    for bit in order:
        axis = count - 1 - bit
        mine = (chip >> bit) & 1
        other = flip_chip(pick(parts, 1 - mine, axis), bit)
        parts = (pick(parts, mine, axis).astype(WIDE) + other.astype(WIDE)).astype(LOW)
    parts = parts.reshape(tail)
    total = pick(parts, z, 1).astype(WIDE)
    for k in range(1, tail[1]):
        total = total + flip_seq(pick(parts, z ^ k, 1), k).astype(WIDE)
    return total[:, 0]


def reduce_all(parts, first):
    core = lax.axis_index("dp") & 1
    other = swap(pick(parts, 1 - core, 1))
    parts = (pick(parts, core, 1).astype(WIDE) + other.astype(WIDE)).astype(LOW)
    return reduce_chips(parts, first)[0]


def block_rows(ref, block, lanes):
    return ref[pl.ds(pl.multiple_of(block * BLOCK, BLOCK), BLOCK), lanes]


def diagonal(pair_rows, low):
    zero = jnp.zeros_like(pair_rows)
    return jnp.concatenate(
        [jnp.where(low, pair_rows, zero), jnp.where(low, zero, pair_rows)], axis=0
    )


def gather_blocks(ref, ids, lanes, low):
    parts = []
    for one, two in ids:
        if two is None:
            parts.append(block_rows(ref, one, lanes))
        else:
            parts.append(
                jnp.where(low, block_rows(ref, one, lanes), block_rows(ref, two, lanes))
            )
    return jnp.concatenate(parts, axis=0)


def slot_ids(near_ref, rand_ref, globs, i, pair, blocks):
    ids = [(near_ref[i], None), (i, None), (near_ref[blocks + i], None)]
    ids += [(globs[0], None), (globs[1], None)]
    for r in range(3):
        ids.append(
            (
                rand_ref[((2 * pair) * blocks + i) * 3 + r],
                rand_ref[((2 * pair + 1) * blocks + i) * 3 + r],
            )
        )
    return ids


def lanes_of(part, pair, pairs):
    first = 128 * (part * pairs + pair)
    return slice(first, first + 128)


def attend_kernel(pairs, blocks, step, near_ref, rand_ref, glob_ref, bias_ref, qkv_ref, out_ref, log_ref):
    low = lax.broadcasted_iota(jnp.int32, (1, 2 * HEAD), 1) < HEAD
    globs = (glob_ref[0], glob_ref[1])

    def scores_of(i, pair):
        ids = slot_ids(near_ref, rand_ref, globs, i, pair, blocks)
        queries = diagonal(block_rows(qkv_ref, i, lanes_of(0, pair, pairs)), low)
        return dot(gather_blocks(qkv_ref, ids, lanes_of(1, pair, pairs), low), queries, NT)

    def softmax_of(i, pair, scores):
        highest = jnp.max(scores, axis=0, keepdims=True)
        weights = jnp.exp(scores - highest)
        total = jnp.sum(weights, axis=0, keepdims=True)
        log_ref[i, pair : pair + 1] = highest + jnp.log(total)
        return (weights * (1.0 / total)).astype(LOW)

    def put(i, pair, mixed):
        at = pl.ds(pl.multiple_of(i * BLOCK, BLOCK), BLOCK)
        out_ref[at, lanes_of(0, pair, pairs)] = jnp.where(
            low, mixed[:BLOCK], mixed[BLOCK:]
        ).astype(LOW)

    def body(at, carry):
        units = [(at * step + d, pair) for d in range(step) for pair in range(pairs)]
        scores = [scores_of(*unit) for unit in units]
        probs = []
        for (i, pair), score in zip(units, scores):
            bias = bias_ref[i, pair]
            score = jnp.concatenate(
                [score[BLOCK * j : BLOCK * j + BLOCK] + bias[j : j + 1] for j in range(SLOTS)],
                axis=0,
            )
            probs.append(softmax_of(i, pair, score))
        for (i, pair), prob in zip(units, probs):
            ids = slot_ids(near_ref, rand_ref, globs, i, pair, blocks)
            values = gather_blocks(qkv_ref, ids, lanes_of(2, pair, pairs), low)
            put(i, pair, dot(prob, values, TN))
        return carry

    lax.fori_loop(0, blocks // step, body, 0)

    def whole_row(n, carry):
        i = glob_ref[n]
        scores = []
        for pair in range(pairs):
            queries = diagonal(block_rows(qkv_ref, i, lanes_of(0, pair, pairs)), low)
            scores.append(dot(qkv_ref[:, lanes_of(1, pair, pairs)], queries, NT))
        probs = [softmax_of(i, pair, scores[pair]) for pair in range(pairs)]
        for pair in range(pairs):
            put(i, pair, dot(probs[pair], qkv_ref[:, lanes_of(2, pair, pairs)], TN))
        return carry

    lax.fori_loop(0, 2, whole_row, 0)


def attend_back_kernel(
    pairs, blocks, step, near_ref, rand_ref, glob_ref, bias_ref, log_ref, qkv_ref, grad_ref, out_ref, acc_ref
):
    low = lax.broadcasted_iota(jnp.int32, (1, 2 * HEAD), 1) < HEAD
    globs = (glob_ref[0], glob_ref[1])
    acc_ref[...] = jnp.zeros_like(acc_ref)

    def add(part, pair, block, value):
        at = pl.ds(pl.multiple_of(block * BLOCK, BLOCK), BLOCK)
        lanes = lanes_of(part, pair, pairs)
        acc_ref[at, lanes] = acc_ref[at, lanes] + value

    def operands(i, pair):
        queries = diagonal(block_rows(qkv_ref, i, lanes_of(0, pair, pairs)), low)
        grads = diagonal(block_rows(grad_ref, i, lanes_of(0, pair, pairs)), low)
        return queries, grads

    def softmax_back(prob, grad_prob):
        scaled = prob * grad_prob
        inner = jnp.sum(scaled, axis=0, keepdims=True)
        return prob.astype(LOW), (scaled - prob * inner).astype(LOW)

    def put(i, pair, mixed):
        at = pl.ds(pl.multiple_of(i * BLOCK, BLOCK), BLOCK)
        out_ref[at, lanes_of(0, pair, pairs)] = (
            jnp.where(low, mixed[:BLOCK], mixed[BLOCK:]) * HEAD ** (-0.5)
        ).astype(LOW)

    def body(at, carry):
        units = [(at * step + d, pair) for d in range(step) for pair in range(pairs)]
        first = []
        for i, pair in units:
            ids = slot_ids(near_ref, rand_ref, globs, i, pair, blocks)
            queries, grads = operands(i, pair)
            first.append(
                (
                    dot(gather_blocks(qkv_ref, ids, lanes_of(1, pair, pairs), low), queries, NT),
                    dot(gather_blocks(qkv_ref, ids, lanes_of(2, pair, pairs), low), grads, NT),
                )
            )
        second = []
        for (i, pair), (score, grad_prob) in zip(units, first):
            shift = bias_ref[i, pair] - log_ref[i, pair : pair + 1]
            prob = jnp.concatenate(
                [
                    jnp.exp(score[BLOCK * j : BLOCK * j + BLOCK] + shift[j : j + 1])
                    for j in range(SLOTS)
                ],
                axis=0,
            )
            second.append(softmax_back(prob, grad_prob))
        third = []
        for (i, pair), (prob, grad_score) in zip(units, second):
            ids = slot_ids(near_ref, rand_ref, globs, i, pair, blocks)
            queries, grads = operands(i, pair)
            keys = gather_blocks(qkv_ref, ids, lanes_of(1, pair, pairs), low)
            put(i, pair, dot(grad_score, keys, TN))
            third.append((dot(grad_score, queries, NN), dot(prob, grads, NN)))
        for (i, pair), values in zip(units, third):
            ids = slot_ids(near_ref, rand_ref, globs, i, pair, blocks)
            for j, (one, two) in enumerate(ids):
                for part, value in enumerate(values):
                    value = value[BLOCK * j : BLOCK * j + BLOCK]
                    if two is None:
                        add(part, pair, one, value)
                    else:
                        add(part, pair, one, jnp.where(low, value, 0.0))
                        add(part, pair, two, jnp.where(low, 0.0, value))
        return carry

    lax.fori_loop(0, blocks // step, body, 0)

    def whole_row(n, carry):
        i = glob_ref[n]
        first = []
        for pair in range(pairs):
            queries, grads = operands(i, pair)
            first.append(
                (
                    dot(qkv_ref[:, lanes_of(1, pair, pairs)], queries, NT),
                    dot(qkv_ref[:, lanes_of(2, pair, pairs)], grads, NT),
                )
            )
        second = []
        for pair, (score, grad_prob) in enumerate(first):
            prob = jnp.exp(score - log_ref[i, pair : pair + 1])
            second.append(softmax_back(prob, grad_prob))
        for pair, (prob, grad_score) in enumerate(second):
            queries, grads = operands(i, pair)
            acc_ref[:, lanes_of(0, pair, pairs)] += dot(grad_score, queries, NN)
            acc_ref[:, lanes_of(1, pair, pairs)] += dot(prob, grads, NN)
            put(i, pair, dot(grad_score, qkv_ref[:, lanes_of(1, pair, pairs)], TN))
        return carry

    lax.fori_loop(0, jnp.where(globs[0] == globs[1], 1, 2), whole_row, 0)
    out_ref[:, 128 * pairs :] = acc_ref[...].astype(LOW)


IN_SMEM = pl.BlockSpec(memory_space=pltpu.SMEM)
IN_VMEM = pl.BlockSpec(memory_space=pltpu.VMEM)


def attend(near, rand, globs, bias, qkv):
    length, width = qkv.shape
    pairs, blocks = width // 384, length // BLOCK
    return pl.pallas_call(
        partial(attend_kernel, pairs, blocks, 4),
        out_shape=(
            jax.ShapeDtypeStruct((length, width // 3), LOW),
            jax.ShapeDtypeStruct((blocks, 8, 128), WIDE),
        ),
        in_specs=[IN_SMEM, IN_SMEM, IN_SMEM, IN_VMEM, IN_VMEM],
        out_specs=(IN_VMEM, IN_VMEM),
        compiler_params=pltpu.CompilerParams(vmem_limit_bytes=48 << 20),
        cost_estimate=pl.CostEstimate(
            flops=20_000_000_000, bytes_accessed=8_000_000, transcendentals=0
        ),
        name="attend",
    )(near, rand, globs, bias, qkv)


def attend_back(near, rand, globs, bias, log_total, qkv, grads):
    length, width = qkv.shape
    pairs, blocks = width // 384, length // BLOCK
    return pl.pallas_call(
        partial(attend_back_kernel, pairs, blocks, 2),
        out_shape=jax.ShapeDtypeStruct((length, width), LOW),
        in_specs=[IN_SMEM, IN_SMEM, IN_SMEM, IN_VMEM, IN_VMEM, IN_VMEM, IN_VMEM],
        out_specs=IN_VMEM,
        scratch_shapes=[pltpu.VMEM((length, 2 * width // 3), WIDE)],
        compiler_params=pltpu.CompilerParams(vmem_limit_bytes=52 << 20),
        cost_estimate=pl.CostEstimate(
            flops=36_000_000_000, bytes_accessed=16_000_000, transcendentals=0
        ),
        name="attend_back",
    )(near, rand, globs, bias, log_total, qkv, grads)


def place_of(block, core, z, blocks):
    quarter, inner = block // (blocks // 4), block % (blocks // 4)
    size = blocks // 8
    half, row = inner // size, inner % size
    a = (quarter & 1) ^ (z & 1)
    b = (quarter >> 1) ^ half
    return (half ^ core) * (blocks // 2) + (2 * a + b) * size + row


def block_at(place, core, z, blocks):
    size = blocks // 8
    half = (place // (blocks // 2)) ^ core
    turn, row = (place % (blocks // 2)) // size, place % size
    quarter = 2 * ((turn & 1) ^ half) + ((turn >> 1) ^ (z & 1))
    return quarter * (blocks // 4) + half * size + row


def tables(rand, globs, blocks):
    core = lax.axis_index("dp") & 1
    z = lax.axis_index("seq")
    here = block_at(jnp.arange(blocks, dtype=jnp.int32), core, z, blocks)
    heads = rand.shape[0]
    one, two = globs[0], globs[1]

    def near(block):
        return jnp.abs(block - here) <= 1

    every = jnp.ones((heads, blocks), bool)
    ok = [every & (here > 0), every, every & (here < blocks - 1)]
    ok += [every & ~near(one), every & ~near(two) & (one != two)]
    seen = []
    for r in range(3):
        block = rand[:, :, r]
        good = ~near(block) & (block != one) & (block != two)
        for before in seen:
            good = good & (block != before)
        seen.append(block)
        ok.append(good)
    whole_row = (here == one) | (here == two)
    ok = jnp.stack(ok, -1) & ~whole_row[None, :, None]
    bias = jnp.where(ok, 0.0, NEG).astype(WIDE)
    bias = bias.reshape(heads // 2, 2, blocks, SLOTS).transpose(2, 0, 3, 1)
    bias = jnp.repeat(bias, HEAD, axis=3)
    put = partial(place_of, core=core, z=z, blocks=blocks)
    sides = jnp.concatenate([put(jnp.maximum(here - 1, 0)), put(jnp.minimum(here + 1, blocks - 1))])
    return sides, put(rand).reshape(-1), put(globs), bias


def norm_parts(summed):
    center = summed - jnp.mean(summed, -1, keepdims=True)
    spread = jnp.mean(center * center, -1, keepdims=True)
    scale = lax.rsqrt(spread + EPS)
    return center * scale, scale


def norm_back(grad, unit, scale, gain):
    grad_unit = grad * gain
    mean_one = jnp.mean(grad_unit, -1, keepdims=True)
    mean_two = jnp.mean(grad_unit * unit, -1, keepdims=True)
    return (
        scale * (grad_unit - mean_one - unit * mean_two),
        jnp.sum(grad * unit, 0),
        jnp.sum(grad, 0),
    )


def gelu_parts(x):
    size = jnp.abs(x)
    t = 1.0 / (1.0 + (0.3275911 * 0.5**0.5) * size)
    bell = jnp.exp(-0.5 * x * x)
    series = 1.061405429
    for factor in (-1.453152027, 1.421413741, -0.284496736, 0.254829592):
        series = series * t + factor
    tail = 0.5 * series * t * bell
    share = jnp.where(x >= 0, 1.0 - tail, tail)
    return x * share, share + x * bell * 0.3989422804014327


def shards(
    inputs,
    cotangent,
    rand_blocks,
    global_blocks,
    w_query,
    b_query,
    w_key,
    w_value,
    b_value,
    w_out,
    b_out,
    gain_one,
    shift_one,
    w_up,
    b_up,
    w_down,
    b_down,
    gain_two,
    shift_two,
):
    n_dp, n_seq = lax.axis_size("dp"), lax.axis_size("seq")
    chips, devices = n_dp // 2, n_dp * n_seq
    core = lax.axis_index("dp") & 1
    z = lax.axis_index("seq")
    rows_in = w_query.shape[0]
    rows_ff = w_down.shape[0]
    width = w_query.shape[1]
    wide = w_up.shape[1]
    half_width = width // 2
    _, quarter, _ = inputs.shape
    part = quarter // 2
    length = quarter * n_seq
    blocks = length // BLOCK
    own = length // 2
    own_heads = HEADS // 2

    def piece_of(s, half):
        tokens = lax.dynamic_slice(inputs, (s, half * part, 0), (1, part, width))[0]
        numbers = lax.dynamic_slice(
            rand_blocks, (s, half * own_heads, 0, 0), (1, own_heads) + rand_blocks.shape[2:]
        ).reshape(-1)
        globs = pick(global_blocks, s, 0).reshape(-1)
        numbers = jnp.concatenate([numbers, globs]).astype(LOW)
        numbers = jnp.pad(numbers, (0, 16 * width - numbers.shape[0])).reshape(16, width)
        return jnp.concatenate([tokens, numbers], 0)

    pieces = bring(piece_of)
    tokens_own = jnp.concatenate([p[:part] for p in pieces], 0)
    local_blocks = rand_blocks.shape[2]
    count = own_heads * local_blocks * 3
    rand_parts = [
        p[part, :count].astype(jnp.int32).reshape(own_heads, local_blocks, 3) for p in pieces
    ]
    globs = pieces[0][part, count : count + 2].astype(jnp.int32)
    size = local_blocks // 2
    rand_rows = []
    for side in range(2):
        for turn in range(4):
            numbers = rand_parts[turn ^ side]
            rand_rows.append(lax.dynamic_slice_in_dim(numbers, (core ^ side) * size, size, 1))
    near, rand, glob_at, bias = tables(jnp.concatenate(rand_rows, 1), globs, blocks)

    def halves(at):
        return jnp.concatenate(
            [
                lax.dynamic_slice_in_dim(w, at * half_width, half_width, 1)
                for w in (w_query, w_key, w_value)
            ],
            1,
        )

    def small_rows(*vectors):
        lines = [jnp.pad(v, (0, 3 * half_width - v.shape[0]))[None] for v in vectors]
        return jnp.pad(jnp.concatenate(lines, 0), ((0, 8 - len(lines)), (0, 0)))

    biases = small_rows(b_query, b_value)
    keep = jnp.concatenate([halves(core), biases], 0)
    come = swap(jnp.concatenate([halves(1 - core), biases], 0))
    shard = jnp.stack([jnp.where(core == 0, keep, come), jnp.where(core == 0, come, keep)])
    qkv_all = gather_chips(shard)
    w_qkv = qkv_all[:, :, :, :rows_in].reshape(width, 3 * half_width)

    def own_half(line):
        vector = qkv_all[:, :, :, rows_in + line, :rows_in].reshape(width)
        return lax.dynamic_slice_in_dim(vector, core * half_width, half_width, 0)

    b_qkv = jnp.concatenate(
        [own_half(0), jnp.zeros((half_width,), LOW), own_half(1)]
    ).astype(WIDE)

    vectors = jnp.concatenate([b_out, gain_one, shift_one, b_down, gain_two, shift_two, b_up])
    vector_rows = 8
    vectors = jnp.pad(vectors, (0, vector_rows * width - vectors.shape[0])).reshape(vector_rows, width)
    up_rows = rows_in * wide // width
    packed = jnp.concatenate([w_out, vectors, w_up.reshape(up_rows, width), w_down], 0)
    packed = lax.all_gather(packed, ("dp", "seq"), axis=0, tiled=False)
    w_out_all = packed[:, :rows_in].reshape(width, width)
    vectors = packed[:, rows_in : rows_in + vector_rows].reshape(devices, -1).astype(WIDE)
    at = rows_in + vector_rows
    w_up_all = packed[:, at : at + up_rows].reshape(width, wide)
    w_down_all = packed[:, at + up_rows :].reshape(wide, width)
    b_out_all, gain_one_all, shift_one_all, b_down_all, gain_two_all, shift_two_all = (
        vectors[:, k * rows_in : (k + 1) * rows_in].reshape(width) for k in range(6)
    )
    b_up_all = vectors[:, 6 * rows_in : 6 * rows_in + rows_ff].reshape(wide)

    tokens = jnp.concatenate([tokens_own, swap(tokens_own)], 0)
    scale = jnp.concatenate(
        [jnp.full((half_width,), HEAD ** (-0.5)), jnp.ones((2 * half_width,))]
    ).astype(LOW)
    qkv = (dot(tokens, w_qkv, NN) + b_qkv).astype(LOW) * scale
    mixed, log_total = attend(near, rand, glob_at, bias, qkv)
    other = swap(mixed[own:])
    attended = jnp.where(
        core == 0,
        jnp.concatenate([mixed[:own], other], 1),
        jnp.concatenate([other, mixed[:own]], 1),
    )
    first_sum = tokens_own.astype(WIDE) + (dot(attended, w_out_all, NN) + b_out_all)
    unit_one, scale_one = norm_parts(first_sum)
    normed = unit_one * gain_one_all + shift_one_all
    normed_low = normed.astype(LOW)
    hidden_pre = dot(normed_low, w_up_all, NN) + b_up_all
    hidden, slope = gelu_parts(hidden_pre)
    hidden, slope = hidden.astype(LOW), slope.astype(LOW)
    second_sum = normed + (dot(hidden, w_down_all, NN) + b_down_all)
    unit_two, scale_two = norm_parts(second_sum)
    result = (unit_two * gain_two_all + shift_two_all).astype(LOW)
    output = send_back(list(jnp.split(result, 4, 0)))

    def cotangent_piece(s, half):
        return lax.dynamic_slice(cotangent, (s, half * part, 0), (1, part, width))[0]

    grad_result = jnp.concatenate(bring(cotangent_piece), 0).astype(WIDE)
    grad_second, grad_gain_two, grad_shift_two = norm_back(
        grad_result, unit_two, scale_two, gain_two_all
    )
    grad_down = grad_second.astype(LOW)
    grad_b_down = jnp.sum(grad_down.astype(WIDE), 0)
    grad_w_down = dot(hidden, grad_down, TN).astype(LOW)
    own_down = reduce_all(grad_w_down.reshape(chips, 2, n_seq, rows_ff, width), 0)
    grad_pre = (dot(grad_down, w_down_all, NT) * slope.astype(WIDE)).astype(LOW)
    grad_b_up = jnp.sum(grad_pre.astype(WIDE), 0)
    grad_w_up = dot(normed_low, grad_pre, TN).astype(LOW)
    own_up = reduce_all(grad_w_up.reshape(chips, 2, n_seq, rows_in, wide), 1)
    grad_normed = grad_second + dot(grad_pre, w_up_all, NT)
    grad_first, grad_gain_one, grad_shift_one = norm_back(
        grad_normed, unit_one, scale_one, gain_one_all
    )
    grad_branch = grad_first.astype(LOW)
    grad_b_out = jnp.sum(grad_branch.astype(WIDE), 0)
    grad_w_out = dot(attended, grad_branch, TN).astype(LOW)
    grad_vectors = [
        v.reshape(devices, rows_in)
        for v in (grad_b_out, grad_gain_one, grad_shift_one, grad_b_down, grad_gain_two, grad_shift_two)
    ]
    grad_vectors = jnp.concatenate(grad_vectors + [grad_b_up.reshape(devices, rows_ff)], 1)
    grad_vectors = jnp.pad(
        grad_vectors, ((0, 0), (0, vector_rows * width - grad_vectors.shape[1]))
    ).reshape(devices, vector_rows, width)
    out_parts = jnp.concatenate(
        [grad_w_out.reshape(devices, rows_in, width), grad_vectors.astype(LOW)], 1
    )
    own_out = reduce_all(out_parts.reshape(chips, 2, n_seq, rows_in + vector_rows, width), 0)
    grad_attended = dot(grad_branch, w_out_all, NT).astype(LOW)
    mine = lax.dynamic_slice_in_dim(grad_attended, core * half_width, half_width, 1)
    theirs = lax.dynamic_slice_in_dim(grad_attended, (1 - core) * half_width, half_width, 1)
    grad_mixed = jnp.concatenate([mine, swap(theirs)], 0)
    grad_qkv = attend_back(near, rand, glob_at, bias, log_total, qkv, grad_mixed)

    grad_rows = dot(grad_qkv, w_qkv, NT)
    come = swap(grad_rows[own:].astype(LOW))
    grad_tokens = (grad_first + grad_rows[:own] + come.astype(WIDE)).astype(LOW)
    grad_inputs = send_back(list(jnp.split(grad_tokens, 4, 0)))

    grad_w_qkv = dot(tokens, grad_qkv, TN).astype(LOW)
    sums = jnp.sum(grad_qkv.astype(WIDE), 0).reshape(3, half_width)
    empty = jnp.zeros((half_width,), WIDE)

    def spread_half(vector):
        vector = jnp.where(
            core == 0, jnp.concatenate([vector, empty]), jnp.concatenate([empty, vector])
        )
        return vector.reshape(devices, 1, rows_in)

    lines = jnp.concatenate([spread_half(sums[0]), spread_half(sums[2])], 1).astype(LOW)
    lines = jnp.pad(lines, ((0, 0), (0, 6), (0, 3 * half_width - rows_in)))
    qkv_parts = jnp.concatenate(
        [grad_w_qkv.reshape(devices, rows_in, 3 * half_width), lines], 1
    ).reshape(chips, 2, n_seq, rows_in + 8, 3 * half_width)
    own_qkv = reduce_chips(qkv_parts, 0)
    come = swap(pick(own_qkv, 1 - core, 0))[0]
    keep = pick(own_qkv, core, 0)[0]
    left, right = jnp.where(core == 0, keep, come), jnp.where(core == 0, come, keep)

    def joined(k):
        lanes = slice(k * half_width, (k + 1) * half_width)
        return jnp.concatenate([left[:rows_in, lanes], right[:rows_in, lanes]], 1)

    both = keep[rows_in : rows_in + 2, :rows_in] + come[rows_in : rows_in + 2, :rows_in]
    small = own_out[rows_in:].reshape(-1)

    def vector_of(k):
        return small[k * rows_in : (k + 1) * rows_in]

    return (
        output,
        grad_inputs,
        joined(0),
        both[0],
        joined(1),
        joined(2),
        both[1],
        own_out[:rows_in],
        vector_of(0),
        vector_of(1),
        vector_of(2),
        own_up,
        small[6 * rows_in : 6 * rows_in + rows_ff],
        own_down,
        vector_of(3),
        vector_of(4),
        vector_of(5),
    )


def solution(mesh):
    both = ("dp", "seq")
    matrix, vector = P(both, None), P(both)
    tokens = P("dp", "seq", None)
    return jax.shard_map(
        shards,
        mesh=mesh,
        in_specs=(tokens, tokens, P("dp", None, "seq", None), P("dp", None))
        + (matrix, vector, matrix, matrix, vector, matrix, vector, vector, vector)
        + (matrix, vector, matrix, vector, vector, vector),
        out_specs=(tokens, tokens)
        + (matrix, vector, matrix, matrix, vector, matrix, vector, vector, vector)
        + (matrix, vector, matrix, vector, vector, vector),
        check_vma=False,
    )
```

```python
from functools import partial

import jax
import jax.numpy as jnp
from jax import lax
from jax.experimental import pallas as pl
from jax.experimental.pallas import tpu as pltpu
from jax.sharding import PartitionSpec as P

HEADS = 12
HEAD = 64
BLOCK = 64
SLOTS = 8
EPS = 1e-06
NEG = -1e30
LOW = jnp.bfloat16
WIDE = jnp.float32

NT = (((1,), (1,)), ((), ()))
TN = (((0,), (0,)), ((), ()))
NN = (((1,), (0,)), ((), ()))


def dot(left, right, dims):
    return lax.dot_general(left, right, dims, preferred_element_type=WIDE)


def swap(array):
    size = lax.axis_size("dp")
    return lax.ppermute(array, "dp", [(i, i ^ 1) for i in range(size)])


def flip_seq(array, k):
    size = lax.axis_size("seq")
    return lax.ppermute(array, "seq", [(i, i ^ k) for i in range(size)])


def rounds():
    dp, seq = lax.axis_size("dp"), lax.axis_size("seq")
    for a in range(2):
        pairs = []
        for d in range(dp):
            for z in range(seq):
                to_dp = (d & ~1) | (z >> 1)
                to_seq = 2 * (d & 1) + (a ^ (z & 1))
                pairs.append((d * seq + z, to_dp * seq + to_seq))
        yield a, pairs


def bring(piece_of):
    z = lax.axis_index("seq")
    return [lax.ppermute(piece_of(a ^ (z & 1)), ("dp", "seq"), pairs) for a, pairs in rounds()]


def send_back(rows):
    z = lax.axis_index("seq")
    size = rows.shape[0] // 2
    got = [
        lax.ppermute(rows[size * a : size * a + size], ("dp", "seq"), [(t, s) for s, t in pairs])
        for a, pairs in rounds()
    ]
    odd = (z & 1) == 1
    return jnp.stack([jnp.where(odd, got[1], got[0]), jnp.where(odd, got[0], got[1])])


def pick(array, index, axis):
    return lax.dynamic_slice_in_dim(array, index, 1, axis)


def gather_seq(shard):
    z = lax.axis_index("seq")
    mirror = flip_seq(shard, 3)
    near = flip_seq(jnp.stack([shard, mirror]), 1)
    pieces = [shard, near[0], near[1], mirror]
    for bit in range(2):
        set_bit = ((z >> bit) & 1) == 1
        pieces = [
            jnp.where(set_bit, pieces[i ^ (1 << bit)], pieces[i]) for i in range(len(pieces))
        ]
    return pieces, mirror


def chip_groups():
    count = (lax.axis_size("dp") // 2).bit_length() - 1
    return [(bit, min(2, count - bit)) for bit in range(0, count, 2)]


def flip_chip(array, away):
    size = lax.axis_size("dp")
    return lax.ppermute(array, "dp", [(i, i ^ (2 * away)) for i in range(size)])


def gather_chips(part):
    parts = [part]
    for bit, bits in chip_groups():
        parts = parts + [flip_chip(p, k << bit) for k in range(1, 1 << bits) for p in parts]
    return parts


def in_chip_order(parts):
    chip = lax.axis_index("dp") >> 1
    parts = jnp.stack(parts)
    return [pick(parts, q ^ chip, 0)[0] for q in range(parts.shape[0])]


def in_device_order(mine, theirs):
    core = lax.axis_index("dp") & 1
    parts = []
    for own, other in zip(in_chip_order(mine), in_chip_order(theirs)):
        parts += [jnp.where(core == 0, own, other), jnp.where(core == 0, other, own)]
    return jnp.concatenate(parts, 0)


def join(*values):
    return lax.optimization_barrier(values)


def tie(values, *others):
    return lax.optimization_barrier((values, others))[0]


def added(*arrays):
    return sum(array.astype(WIDE) for array in arrays).astype(LOW)


def reduce_chips(parts):
    chip = lax.axis_index("dp") >> 1
    for bit, bits in chip_groups():
        ways = 1 << bits
        parts = parts.reshape((-1, ways) + parts.shape[1:])
        mine = (chip >> bit) & (ways - 1)
        others = [flip_chip(pick(parts, mine ^ k, 1)[:, 0], k << bit) for k in range(1, ways)]
        parts = added(pick(parts, mine, 1)[:, 0], *others)
    return parts[0]


def reduce_seq(parts):
    z = lax.axis_index("seq")
    near = flip_seq(jnp.concatenate([pick(parts, z ^ 1, 0), pick(parts, z ^ 2, 0)], 0), 1)
    mirror = added(pick(parts, z ^ 3, 0)[0], near[1])
    return pick(parts, z, 0)[0].astype(WIDE) + near[0].astype(WIDE) + flip_seq(mirror, 3).astype(WIDE)


def norm_parts(summed):
    center = summed - jnp.mean(summed, -1, keepdims=True)
    spread = jnp.mean(center * center, -1, keepdims=True)
    scale = lax.rsqrt(spread + EPS)
    return center * scale, scale


def norm_back(grad, unit, scale, gain):
    grad_unit = grad * gain
    mean_one = jnp.mean(grad_unit, -1, keepdims=True)
    mean_two = jnp.mean(grad_unit * unit, -1, keepdims=True)
    return scale * (grad_unit - mean_one - unit * mean_two)


def gelu_parts(x):
    size = jnp.abs(x)
    t = 1.0 / (1.0 + (0.3275911 * 0.5**0.5) * size)
    bell = jnp.exp(-0.5 * x * x)
    series = 1.061405429
    for factor in (-1.453152027, 1.421413741, -0.284496736, 0.254829592):
        series = series * t + factor
    tail = 0.5 * series * t * bell
    share = jnp.where(x >= 0, 1.0 - tail, tail)
    return x * share, share + x * bell * 0.3989422804014327


def block_rows(ref, block, lanes):
    return ref[pl.ds(pl.multiple_of(block * BLOCK, BLOCK), BLOCK), lanes]


def diagonal(pair_rows, low):
    zero = jnp.zeros_like(pair_rows)
    return jnp.concatenate(
        [jnp.where(low, pair_rows, zero), jnp.where(low, zero, pair_rows)], axis=0
    )


def gather_blocks(ref, ids, lanes, low):
    parts = []
    for one, two in ids:
        if two is None:
            parts.append(block_rows(ref, one, lanes))
        else:
            parts.append(
                jnp.where(low, block_rows(ref, one, lanes), block_rows(ref, two, lanes))
            )
    return jnp.concatenate(parts, axis=0)


def slot_ids(near_ref, rand_ref, globs, i, head, blocks):
    ids = [(near_ref[i], None), (i, None), (near_ref[blocks + i], None)]
    ids += [(globs[0], None), (globs[1], None)]
    for r in range(3):
        ids.append(
            (
                rand_ref[(head * blocks + i) * 3 + r],
                rand_ref[((head + 1) * blocks + i) * 3 + r],
            )
        )
    return ids


def lanes_of(part, pair):
    first = 128 * (3 * pair + part)
    return slice(first, first + 128)


def flat_lanes(pair):
    return slice(128 * pair, 128 * pair + 128)


def start_copies(copies, sems):
    started = [
        pltpu.make_async_copy(source, target, sems.at[k])
        for k, (source, target) in enumerate(copies)
    ]
    for copy in started:
        copy.start()
    return started


def project_kernel(chips, direct, at_ref, tokens_ref, b_ref, *refs):
    sources, (first_ref, rest_ref, w_ref, sems) = refs[:-4], refs[-4:]
    if direct:
        span = w_ref.shape[0] // (2 * chips)
        copies = [
            (
                sources[away].at[k, :span],
                w_ref.at[pl.ds(pl.multiple_of((2 * (at_ref[0] ^ away) + k) * span, span), span)],
            )
            for away in range(chips)
            for k in range(2)
        ]
    else:
        copies = [(sources[0], w_ref)]
    for copy in start_copies(copies, sems):
        copy.wait()
    tile = 256
    lane = lax.broadcasted_iota(jnp.int32, (1, w_ref.shape[1]), 1)
    scale = jnp.where(lane % 384 < 128, HEAD ** (-0.5), 1.0)

    def body(at, carry):
        rows = pl.ds(pl.multiple_of(at * tile, tile), tile)
        values = (dot(tokens_ref[rows], w_ref[...], NN) + b_ref[...]).astype(LOW).astype(WIDE)
        values = (values * scale).astype(LOW)
        cut = first_ref.shape[1]
        first_ref[rows] = values[:, :cut]
        rest_ref[rows] = values[:, cut:]
        return carry

    lax.fori_loop(0, tokens_ref.shape[0] // tile, body, 0)


def attend_kernel(
    first_pair, pairs, blocks, step, near_ref, rand_ref, glob_ref, bias_ref, qkv_ref, out_ref, log_ref
):
    low = lax.broadcasted_iota(jnp.int32, (1, 2 * HEAD), 1) < HEAD
    globs = (glob_ref[0], glob_ref[1])

    def scores_of(i, pair):
        ids = slot_ids(near_ref, rand_ref, globs, i, 2 * (first_pair + pair), blocks)
        queries = diagonal(block_rows(qkv_ref, i, lanes_of(0, pair)), low)
        return dot(gather_blocks(qkv_ref, ids, lanes_of(1, pair), low), queries, NT)

    def softmax_of(i, pair, scores):
        highest = jnp.max(scores, axis=0, keepdims=True)
        weights = jnp.exp(scores - highest)
        total = jnp.sum(weights, axis=0, keepdims=True)
        log_ref[i, pair : pair + 1] = highest + jnp.log(total)
        return (weights * (1.0 / total)).astype(LOW)

    def put(i, pair, mixed):
        at = pl.ds(pl.multiple_of(i * BLOCK, BLOCK), BLOCK)
        out_ref[at, flat_lanes(pair)] = jnp.where(low, mixed[:BLOCK], mixed[BLOCK:]).astype(LOW)

    def body(at, carry):
        units = [(at * step + d, pair) for d in range(step) for pair in range(pairs)]
        scores = [scores_of(*unit) for unit in units]
        probs = []
        for (i, pair), score in zip(units, scores):
            bias = bias_ref[i, first_pair + pair]
            score = jnp.concatenate(
                [score[BLOCK * j : BLOCK * j + BLOCK] + bias[j : j + 1] for j in range(SLOTS)],
                axis=0,
            )
            probs.append(softmax_of(i, pair, score))
        for (i, pair), prob in zip(units, probs):
            ids = slot_ids(near_ref, rand_ref, globs, i, 2 * (first_pair + pair), blocks)
            values = gather_blocks(qkv_ref, ids, lanes_of(2, pair), low)
            put(i, pair, dot(prob, values, TN))
        return carry

    lax.fori_loop(0, blocks // step, body, 0)

    def whole_row(n, carry):
        i = glob_ref[n]
        scores = []
        for pair in range(pairs):
            queries = diagonal(block_rows(qkv_ref, i, lanes_of(0, pair)), low)
            scores.append(dot(qkv_ref[:, lanes_of(1, pair)], queries, NT))
        probs = [softmax_of(i, pair, scores[pair]) for pair in range(pairs)]
        for pair in range(pairs):
            put(i, pair, dot(probs[pair], qkv_ref[:, lanes_of(2, pair)], TN))
        return carry

    lax.fori_loop(0, 2, whole_row, 0)


def attend_back_kernel(
    first_pair,
    pairs,
    blocks,
    step,
    near_ref,
    rand_ref,
    glob_ref,
    bias_ref,
    log_ref,
    qkv_ref,
    mine_ref,
    come_ref,
    *refs,
):
    if first_pair:
        before_ref, w_ref, whole_ref, rows_own_ref, rows_other_ref, sums_ref = refs[:6]
        out_ref = whole_ref.at[:, 384 * first_pair :]
    else:
        out_ref = refs[0]
    grad_ref, acc_ref = refs[-2:]
    low = lax.broadcasted_iota(jnp.int32, (1, 2 * HEAD), 1) < HEAD
    globs = (glob_ref[0], glob_ref[1])
    acc_ref[...] = jnp.zeros_like(acc_ref)
    half = mine_ref.shape[0]
    lanes = slice(128 * first_pair, 128 * (first_pair + pairs))
    grad_ref[:half] = mine_ref[:, lanes]
    grad_ref[half:] = come_ref[:, lanes]

    def add(part, pair, block, value):
        at = pl.ds(pl.multiple_of(block * BLOCK, BLOCK), BLOCK)
        lanes = flat_lanes(2 * pair + part)
        acc_ref[at, lanes] = acc_ref[at, lanes] + value

    def operands(i, pair):
        queries = diagonal(block_rows(qkv_ref, i, lanes_of(0, pair)), low)
        grads = diagonal(block_rows(grad_ref, i, flat_lanes(pair)), low)
        return queries, grads

    def softmax_back(prob, grad_prob):
        scaled = prob * grad_prob
        inner = jnp.sum(scaled, axis=0, keepdims=True)
        return prob.astype(LOW), (scaled - prob * inner).astype(LOW)

    def put(i, pair, mixed):
        at = pl.ds(pl.multiple_of(i * BLOCK, BLOCK), BLOCK)
        out_ref[at, lanes_of(0, pair)] = (
            jnp.where(low, mixed[:BLOCK], mixed[BLOCK:]) * HEAD ** (-0.5)
        ).astype(LOW)

    def body(at, carry):
        units = [(at * step + d, pair) for d in range(step) for pair in range(pairs)]
        first = []
        for i, pair in units:
            ids = slot_ids(near_ref, rand_ref, globs, i, 2 * (first_pair + pair), blocks)
            queries, grads = operands(i, pair)
            first.append(
                (
                    dot(gather_blocks(qkv_ref, ids, lanes_of(1, pair), low), queries, NT),
                    dot(gather_blocks(qkv_ref, ids, lanes_of(2, pair), low), grads, NT),
                )
            )
        second = []
        for (i, pair), (score, grad_prob) in zip(units, first):
            shift = bias_ref[i, first_pair + pair] - log_ref[i, pair : pair + 1]
            prob = jnp.concatenate(
                [
                    jnp.exp(score[BLOCK * j : BLOCK * j + BLOCK] + shift[j : j + 1])
                    for j in range(SLOTS)
                ],
                axis=0,
            )
            second.append(softmax_back(prob, grad_prob))
        third = []
        for (i, pair), (prob, grad_score) in zip(units, second):
            ids = slot_ids(near_ref, rand_ref, globs, i, 2 * (first_pair + pair), blocks)
            queries, grads = operands(i, pair)
            keys = gather_blocks(qkv_ref, ids, lanes_of(1, pair), low)
            put(i, pair, dot(grad_score, keys, TN))
            third.append((dot(grad_score, queries, NN), dot(prob, grads, NN)))
        for (i, pair), values in zip(units, third):
            ids = slot_ids(near_ref, rand_ref, globs, i, 2 * (first_pair + pair), blocks)
            for j, (one, two) in enumerate(ids):
                for part, value in enumerate(values):
                    value = value[BLOCK * j : BLOCK * j + BLOCK]
                    if two is None:
                        add(part, pair, one, value)
                    else:
                        add(part, pair, one, jnp.where(low, value, 0.0))
                        add(part, pair, two, jnp.where(low, 0.0, value))
        return carry

    lax.fori_loop(0, blocks // step, body, 0)

    def whole_row(n, carry):
        i = glob_ref[n]
        first = []
        for pair in range(pairs):
            queries, grads = operands(i, pair)
            first.append(
                (
                    dot(qkv_ref[:, lanes_of(1, pair)], queries, NT),
                    dot(qkv_ref[:, lanes_of(2, pair)], grads, NT),
                )
            )
        second = []
        for pair, (score, grad_prob) in enumerate(first):
            prob = jnp.exp(score - log_ref[i, pair : pair + 1])
            second.append(softmax_back(prob, grad_prob))
        for pair, (prob, grad_score) in enumerate(second):
            queries, grads = operands(i, pair)
            acc_ref[:, flat_lanes(2 * pair)] += dot(grad_score, queries, NN)
            acc_ref[:, flat_lanes(2 * pair + 1)] += dot(prob, grads, NN)
            put(i, pair, dot(grad_score, qkv_ref[:, lanes_of(1, pair)], TN))
        return carry

    lax.fori_loop(0, jnp.where(globs[0] == globs[1], 1, 2), whole_row, 0)
    for pair in range(pairs):
        out_ref[:, 384 * pair + 128 : 384 * pair + 384] = acc_ref[
            :, 256 * pair : 256 * pair + 256
        ].astype(LOW)
    if first_pair:
        whole_ref[:, : 384 * first_pair] = before_ref[...]
        rows_back(256, whole_ref, w_ref, rows_own_ref, rows_other_ref, sums_ref)


def rows_back(tile, grads_ref, w_ref, own_ref, other_ref, sums_ref):
    sums_ref[...] = jnp.zeros_like(sums_ref)
    for side, rows_ref in enumerate((own_ref, other_ref)):

        def body(at, carry, side=side, rows_ref=rows_ref):
            rows = pl.ds(pl.multiple_of(side * own_ref.shape[0] + at * tile, tile), tile)
            grads = grads_ref[rows]
            sums_ref[...] += jnp.sum(grads.astype(WIDE), 0, keepdims=True)
            rows = pl.ds(pl.multiple_of(at * tile, tile), tile)
            rows_ref[rows] = dot(grads, w_ref[...], NT).astype(rows_ref.dtype)
            return carry

        lax.fori_loop(0, own_ref.shape[0] // tile, body, 0)


def token_kernel(
    tile,
    chips,
    direct,
    at_ref,
    mixed_first_ref,
    mixed_rest_ref,
    other_first_ref,
    other_rest_ref,
    tokens_ref,
    grad_ref,
    vectors_ref,
    *refs,
):
    sources, refs = refs[:-17], refs[-17:]
    output_ref, first_ref, mine_ref, theirs_ref, *grad_refs, g_vectors_ref = refs[:7]
    w_in_ref, w_down_ref, hidden_ref, pre_ref, normed_ref, down_ref, branch_ref, line_ref = refs[7:15]
    sems, out_sems = refs[15:]
    own, half = mine_ref.shape
    wide, width = w_down_ref.shape
    chunks = wide // width
    chip, core = at_ref[0], at_ref[1]
    span, span_ff = width // (2 * chips), wide // (2 * chips)
    low_rows = span * (chunks + 1)
    if direct:
        copies = []
        for k in range(2):
            for away in range(chips):
                source = sources[k * chips + away]
                place = 2 * (chip ^ away) + (core if k == 0 else 1 - core)
                rows = pl.ds(pl.multiple_of(place * span, span), span)
                copies += [
                    (source.at[span * c : span * c + span], w_in_ref.at[c, rows])
                    for c in range(chunks + 1)
                ]
                rows = pl.ds(pl.multiple_of(place * span_ff, span_ff), span_ff)
                copies.append((source.at[low_rows : low_rows + span_ff], w_down_ref.at[rows]))
    else:
        copies = [(sources[0], w_in_ref), (sources[1], w_down_ref)]
    for copy in start_copies(copies, sems):
        copy.wait()
    w_out_ref = w_in_ref.at[chunks]
    here = pl.ds(pl.multiple_of(core * half, 128), half)
    there = pl.ds(pl.multiple_of((1 - core) * half, 128), half)
    b_out, gain_one, shift_one, b_down, gain_two, shift_two = (
        vectors_ref[k : k + 1] for k in range(6)
    )
    g_vectors_ref[...] = jnp.zeros_like(g_vectors_ref)
    columns = [(c, slice(width * c, width * c + width)) for c in range(chunks)]

    def add_sums(**sums):
        for k, value in sums.items():
            k = int(k[1:])
            g_vectors_ref[k : k + 1] += jnp.sum(value, 0, keepdims=True)

    def token_tile(at, carry):
        rows = pl.ds(pl.multiple_of(at * tile, tile), tile)
        mixed = jnp.concatenate([mixed_first_ref[rows], mixed_rest_ref[rows]], 1)
        other = jnp.concatenate([other_first_ref[rows], other_rest_ref[rows]], 1)
        branch = dot(mixed, w_out_ref[here], NN) + dot(other, w_out_ref[there], NN)
        unit_one, scale_one = norm_parts(tokens_ref[rows].astype(WIDE) + (branch + b_out))
        normed = unit_one * gain_one + shift_one
        normed_low = normed.astype(LOW)
        normed_ref[rows] = normed_low
        down = b_down
        for c, lanes in columns:
            bias = vectors_ref[6 + c : 7 + c]
            hidden, slope = gelu_parts(dot(normed_low, w_in_ref[c], NN) + bias)
            hidden = hidden.astype(LOW)
            hidden_ref[rows, lanes] = hidden
            pre_ref[rows, lanes] = slope.astype(LOW)
            down = down + dot(hidden, w_down_ref[lanes], NN)
        unit_two, scale_two = norm_parts(normed + down)
        output_ref[rows] = (unit_two * gain_two + shift_two).astype(LOW)
        grad = grad_ref[rows].astype(WIDE)
        add_sums(_4=grad * unit_two, _5=grad)
        grad_second = norm_back(grad, unit_two, scale_two, gain_two)
        grad_down = grad_second.astype(LOW)
        down_ref[rows] = grad_down
        add_sums(_3=grad_down.astype(WIDE))
        grad_normed = grad_second
        for c, lanes in columns:
            grad_pre = dot(grad_down, w_down_ref[lanes], NT) * pre_ref[rows, lanes].astype(WIDE)
            grad_pre = grad_pre.astype(LOW)
            pre_ref[rows, lanes] = grad_pre
            g_vectors_ref[6 + c : 7 + c] += jnp.sum(grad_pre.astype(WIDE), 0, keepdims=True)
            grad_normed = grad_normed + dot(grad_pre, w_in_ref[c], NT)
        add_sums(_1=grad_normed * unit_one, _2=grad_normed)
        grad_first = norm_back(grad_normed, unit_one, scale_one, gain_one)
        first_ref[rows] = grad_first
        grad_branch = grad_first.astype(LOW)
        branch_ref[rows] = grad_branch
        add_sums(_0=grad_branch.astype(WIDE))
        mine_ref[rows] = dot(grad_branch, w_out_ref[here], NT).astype(LOW)
        theirs_ref[rows] = dot(grad_branch, w_out_ref[there], NT).astype(LOW)
        return carry

    lax.fori_loop(0, own // tile, token_tile, 0)
    mixed = jnp.concatenate([mixed_first_ref[:own], mixed_rest_ref[:own]], 1)
    other = jnp.concatenate([other_first_ref[...], other_rest_ref[...]], 1)
    w_out_ref[here] = dot(mixed, branch_ref[...], TN).astype(LOW)
    w_out_ref[there] = dot(other, branch_ref[...], TN).astype(LOW)
    moving = []

    def leave(copies):
        for source, target in copies:
            copy = pltpu.make_async_copy(source, target, out_sems.at[len(moving)])
            copy.start()
            moving.append(copy)

    def leave_rows(c):
        if not direct:
            return leave([(w_in_ref.at[c], grad_refs[0].at[c])])
        for k, target in enumerate(grad_refs):
            for q in range(chips):
                place = 2 * q + (core if k == 0 else 1 - core)
                rows = pl.ds(pl.multiple_of(place * span, span), span)
                leave([(w_in_ref.at[c, rows], target.at[q, span * c : span * c + span])])

    leave_rows(chunks)
    if direct:
        line_ref[...] = g_vectors_ref[...].astype(LOW)
        for target in grad_refs:
            for q in range(chips):
                leave([(line_ref, target.at[q, low_rows + span_ff : low_rows + span_ff + 16])])
    for c, lanes in columns:
        w_down_ref[lanes] = dot(hidden_ref[:, lanes], down_ref[...], TN).astype(LOW)
        if direct:
            for k, target in enumerate(grad_refs):
                place = 2 * c + (core if k == 0 else 1 - core)
                rows = pl.ds(pl.multiple_of(place * span_ff, span_ff), span_ff)
                leave([(w_down_ref.at[rows], target.at[c, low_rows : low_rows + span_ff])])
        else:
            leave([(w_down_ref.at[lanes], grad_refs[1].at[lanes])])
        w_in_ref[c] = dot(normed_ref[...], pre_ref[:, lanes], TN).astype(LOW)
        leave_rows(c)
    for copy in moving:
        copy.wait()


IN_SMEM = pl.BlockSpec(memory_space=pltpu.SMEM)
IN_VMEM = pl.BlockSpec(memory_space=pltpu.VMEM)


IN_ANY = pl.BlockSpec(memory_space=pl.ANY)


def project_tokens(at, tokens, b_qkv, weights, direct):
    length, width = tokens.shape
    half = width // 2
    chips = lax.axis_size("dp") // 2
    return pl.pallas_call(
        partial(project_kernel, chips, direct),
        out_shape=(
            jax.ShapeDtypeStruct((length, 384), LOW),
            jax.ShapeDtypeStruct((length, 3 * half - 384), LOW),
            jax.ShapeDtypeStruct((width, 3 * half), LOW),
        ),
        in_specs=[IN_SMEM] + [IN_VMEM] * 2 + [IN_ANY] * len(weights),
        out_specs=(IN_VMEM,) * 3,
        scratch_shapes=[pltpu.SemaphoreType.DMA((2 * chips,))],
        compiler_params=pltpu.CompilerParams(vmem_limit_bytes=48 << 20),
        cost_estimate=pl.CostEstimate(
            flops=4_000_000_000, bytes_accessed=12_000_000, transcendentals=0
        ),
        name="project",
    )(at, tokens, b_qkv, *weights)


def attend(first_pair, near, rand, globs, bias, qkv):
    length, width = qkv.shape
    pairs, blocks = width // 384, length // BLOCK
    return pl.pallas_call(
        partial(attend_kernel, first_pair, pairs, blocks, 8 // pairs),
        out_shape=(
            jax.ShapeDtypeStruct((length, 128 * pairs), LOW),
            jax.ShapeDtypeStruct((blocks, 8, 128), WIDE),
        ),
        in_specs=[IN_SMEM] * 3 + [IN_VMEM] * 2,
        out_specs=(IN_VMEM,) * 2,
        compiler_params=pltpu.CompilerParams(vmem_limit_bytes=48 << 20),
        cost_estimate=pl.CostEstimate(
            flops=6_000_000_000 * pairs, bytes_accessed=3_000_000 * pairs, transcendentals=0
        ),
        name="attend",
    )(near, rand, globs, bias, qkv)


def attend_back(first_pair, near, rand, globs, bias, log_total, qkv, mine, come, *more):
    length, width = qkv.shape
    pairs, blocks = width // 384, length // BLOCK
    grads = jax.ShapeDtypeStruct((length, width + 384 * first_pair), LOW)
    if more:
        rows, wide = length // 2, more[1].shape[0]
        grads = (
            grads,
            jax.ShapeDtypeStruct((rows, wide), WIDE),
            jax.ShapeDtypeStruct((rows, wide), LOW),
            jax.ShapeDtypeStruct((1, grads.shape[1]), WIDE),
        )
    return pl.pallas_call(
        partial(attend_back_kernel, first_pair, pairs, blocks, 4 // pairs),
        out_shape=grads,
        in_specs=[IN_SMEM] * 3 + [IN_VMEM] * (5 + len(more)),
        out_specs=(IN_VMEM,) * 4 if more else IN_VMEM,
        scratch_shapes=[
            pltpu.VMEM((length, 128 * pairs), LOW),
            pltpu.VMEM((length, 256 * pairs), WIDE),
        ],
        compiler_params=pltpu.CompilerParams(vmem_limit_bytes=56 << 20),
        cost_estimate=pl.CostEstimate(
            flops=12_000_000_000 * pairs, bytes_accessed=6_000_000 * pairs, transcendentals=0
        ),
        name="attend_back",
    )(near, rand, globs, bias, log_total, qkv, mine, come, *more)


def token_layer(at, mixed, other, tokens, grads, vectors, weights, direct):
    own, width = tokens.shape
    half = width // 2
    chips = lax.axis_size("dp") // 2
    wide = 4 * width
    chunks = wide // width
    if direct:
        rows = ((chunks + 1) * width + wide) // (2 * chips) + 16
        grads_like = (jax.ShapeDtypeStruct((chips, rows, width), LOW),) * 2
    else:
        grads_like = (
            jax.ShapeDtypeStruct((chunks + 1, width, width), LOW),
            jax.ShapeDtypeStruct((wide, width), LOW),
        )
    return pl.pallas_call(
        partial(token_kernel, 256, chips, direct),
        out_shape=(
            jax.ShapeDtypeStruct((own, width), LOW),
            jax.ShapeDtypeStruct((own, width), WIDE),
            jax.ShapeDtypeStruct((own, half), LOW),
            jax.ShapeDtypeStruct((own, half), LOW),
        )
        + grads_like
        + (jax.ShapeDtypeStruct((16, width), WIDE),),
        in_specs=[IN_SMEM] + [IN_VMEM] * 7 + [IN_ANY] * len(weights),
        out_specs=(IN_VMEM,) * 4 + (IN_ANY,) * 2 + (IN_VMEM,),
        scratch_shapes=[
            pltpu.VMEM((chunks + 1, width, width), LOW),
            pltpu.VMEM((wide, width), LOW),
            pltpu.VMEM((own, wide), LOW),
            pltpu.VMEM((own, wide), LOW),
            pltpu.VMEM((own, width), LOW),
            pltpu.VMEM((own, width), LOW),
            pltpu.VMEM((own, width), LOW),
            pltpu.VMEM((16, width), LOW),
            pltpu.SemaphoreType.DMA((2 * chips * (chunks + 2),)),
            pltpu.SemaphoreType.DMA((2 * chips * (chunks + 2) + 2 * chunks,)),
        ],
        compiler_params=pltpu.CompilerParams(vmem_limit_bytes=60 << 20),
        cost_estimate=pl.CostEstimate(
            flops=36_000_000_000, bytes_accessed=32_000_000, transcendentals=0
        ),
        name="token_layer",
    )(at, *mixed, *other, tokens, grads, vectors, *weights)


def place_of(block, core, z, blocks):
    quarter, row = block // (blocks // 4), block % (blocks // 4)
    a = (quarter & 1) ^ (z & 1)
    return ((quarter >> 1) ^ core) * (blocks // 2) + a * (blocks // 4) + row


def block_at(place, core, z, blocks):
    quarter = 2 * ((place // (blocks // 2)) ^ core) + ((place % (blocks // 2)) // (blocks // 4) ^ (z & 1))
    return quarter * (blocks // 4) + place % (blocks // 4)


def tables(rand, globs, blocks):
    core = lax.axis_index("dp") & 1
    z = lax.axis_index("seq")
    here = block_at(jnp.arange(blocks, dtype=jnp.int32), core, z, blocks)
    heads = rand.shape[0]
    one, two = globs[0], globs[1]

    def near(block):
        return jnp.abs(block - here) <= 1

    every = jnp.ones((heads, blocks), bool)
    ok = [every & (here > 0), every, every & (here < blocks - 1)]
    ok += [every & ~near(one), every & ~near(two) & (one != two)]
    seen = []
    for r in range(3):
        block = rand[:, :, r]
        good = ~near(block) & (block != one) & (block != two)
        for before in seen:
            good = good & (block != before)
        seen.append(block)
        ok.append(good)
    whole_row = (here == one) | (here == two)
    ok = jnp.stack(ok, -1) & ~whole_row[None, :, None]
    bias = jnp.where(ok, 0.0, NEG).astype(WIDE)
    bias = bias.reshape(heads // 2, 2, blocks, SLOTS).transpose(2, 0, 3, 1)
    bias = jnp.repeat(bias, HEAD, axis=3)
    put = partial(place_of, core=core, z=z, blocks=blocks)
    sides = jnp.concatenate([put(jnp.maximum(here - 1, 0)), put(jnp.minimum(here + 1, blocks - 1))])
    return sides, put(rand).reshape(-1), put(globs), bias


def shards(
    inputs,
    cotangent,
    rand_blocks,
    global_blocks,
    w_query,
    b_query,
    w_key,
    w_value,
    b_value,
    w_out,
    b_out,
    gain_one,
    shift_one,
    w_up,
    b_up,
    w_down,
    b_down,
    gain_two,
    shift_two,
):
    n_dp, n_seq = lax.axis_size("dp"), lax.axis_size("seq")
    chips, devices = n_dp // 2, n_dp * n_seq
    core = lax.axis_index("dp") & 1
    z = lax.axis_index("seq")
    device = lax.axis_index("dp") * n_seq + z
    rows_in, width = w_query.shape
    rows_ff, wide = w_down.shape[0], w_up.shape[1]
    chunks = wide // width
    half_width = width // 2
    _, quarter, _ = inputs.shape
    length = quarter * n_seq
    blocks = length // BLOCK
    own = length // 2
    own_heads = HEADS // 2
    span, span_ff = n_seq * rows_in, n_seq * rows_ff
    direct = span % 16 == 0 and chips == chunks

    here = jnp.arange(devices, dtype=jnp.int32)[:, None] == device

    def placed(vector):
        return jnp.where(here, vector[None], jnp.zeros((), LOW)).reshape(-1, width)

    q_line, v_line = placed(b_query), placed(b_value)

    pairs = half_width // 128

    def side(at):
        no_line = jnp.zeros((1, width), LOW)
        parts = []
        for pair in range(pairs):
            first = at * half_width + 128 * pair
            lanes = slice(first, first + 128)
            for w, line in ((w_query, q_line), (w_key, no_line), (w_value, v_line)):
                parts.append(jnp.concatenate([w[:, lanes], line[:, lanes]], 0))
        return jnp.pad(jnp.concatenate(parts, 1), ((0, 7), (0, 0)))

    left, right = side(0), side(1)
    keep = jnp.where(core == 0, left, right)
    come = swap(jnp.where(core == 0, right, left))
    shard = jnp.stack([jnp.where(core == 0, keep, come), jnp.where(core == 0, come, keep)])
    qkv_z, first_move = gather_seq(shard)

    packed = jnp.concatenate(
        [w_up[:, width * c : width * c + width] for c in range(chunks)]
        + [w_out, w_down]
        + [placed(v) for v in (b_out, gain_one, shift_one, b_down, gain_two, shift_two, b_up)]
        + [jnp.zeros((16 - 6 - chunks, width), LOW)],
        0,
    )
    wide_z, first_move = gather_seq(tie(packed, first_move))

    whole = []
    for k in range(2):
        lines = sum(p[k, rows_in:].astype(WIDE) for p in qkv_z).astype(LOW)
        whole += [p[k, :rows_in] for p in qkv_z] + [lines, jnp.zeros_like(lines)]
    qkv_parts = gather_chips(jnp.concatenate(whole, 0).reshape(2, span + 16, 3 * half_width))
    lines = sum(jnp.sum(p[:, span].astype(WIDE), 0, keepdims=True) for p in qkv_parts)

    tied_inputs = tie(inputs, first_move)

    def piece_of(s):
        tokens = pick(tied_inputs, s, 0)[0]
        numbers = pick(rand_blocks, s, 0).reshape(-1)
        globs = pick(global_blocks, s, 0).reshape(-1)
        numbers = jnp.concatenate([numbers, globs]).astype(LOW)
        numbers = jnp.pad(numbers, (0, 16 * width - numbers.shape[0])).reshape(16, width)
        return jnp.concatenate([tokens, numbers], 0)

    pieces = bring(piece_of)
    local_blocks = rand_blocks.shape[2]
    count = HEADS * local_blocks * 3
    tokens_own = jnp.concatenate([p[:quarter] for p in pieces], 0)
    numbers = jnp.stack([p[quarter] for p in pieces])
    tokens_other, other_numbers = swap(tokens_own), swap(numbers)
    numbers = jnp.concatenate([numbers, other_numbers], 0).astype(jnp.int32)
    globs = numbers[0, count : count + 2]
    rand = numbers[:, :count].reshape(4, HEADS, local_blocks, 3)
    rand = lax.dynamic_slice_in_dim(rand, core * own_heads, own_heads, 1)
    rand = rand.transpose(1, 0, 2, 3).reshape(own_heads, blocks, 3)
    near, rand, glob_at, bias = tables(rand, globs, blocks)
    tokens = jnp.concatenate([tokens_own, tokens_other], 0)

    rows_a = (chunks + 1) * rows_in
    rows = []
    for c in range(chunks + 1):
        rows += [p[c * rows_in : (c + 1) * rows_in] for p in wide_z]
    rows += [p[rows_a : rows_a + rows_ff] for p in wide_z]
    rows.append(sum(p[rows_a + rows_ff :].astype(WIDE) for p in wide_z).astype(LOW))
    parts = gather_chips(tie(jnp.concatenate(rows, 0), qkv_parts))
    rows_a, rows_b = (chunks + 1) * span, (chunks + 1) * span + span_ff
    at = jnp.stack([lax.axis_index("dp") >> 1, core]).astype(jnp.int32)
    if direct:
        qkv_weights = tuple(qkv_parts)
    else:
        ordered = in_chip_order(qkv_parts)
        qkv_weights = (jnp.concatenate([p[k, :span] for p in ordered for k in range(2)], 0),)

    qkv_first, qkv_rest, w_qkv = project_tokens(at, tokens, lines, qkv_weights, direct)
    mixed_first, log_first = attend(0, near, rand, glob_at, bias, qkv_first)
    mixed_first, qkv_rest, *parts = join(mixed_first, qkv_rest, *parts)
    other_first = swap(mixed_first[own:])
    other_parts = [swap(p) for p in parts]
    mixed_rest, log_rest = attend(1, near, rand, glob_at, bias, qkv_rest)
    vectors = sum(p[rows_b:].astype(WIDE) for p in parts + other_parts)
    if direct:
        weights = tuple(parts + other_parts)
    else:
        weights = (
            jnp.stack(
                [
                    in_device_order(
                        *([p[span * c : span * c + span] for p in ps] for ps in (parts, other_parts))
                    )
                    for c in range(chunks + 1)
                ]
            ),
            in_device_order(*([p[rows_a:rows_b] for p in ps] for ps in (parts, other_parts))),
        )
    tied_cotangent = tie(cotangent, tokens_own)
    grad_result = jnp.concatenate(bring(lambda s: pick(tied_cotangent, s, 0)[0]), 0)
    result, grad_first, mine, theirs, grad_keep, grad_send, grad_vectors = token_layer(
        at,
        (mixed_first, mixed_rest),
        (other_first, swap(mixed_rest[own:])),
        tokens_own,
        grad_result,
        vectors,
        weights,
        direct,
    )
    come = swap(theirs)
    output = send_back(result)

    if not direct:
        parts_a = grad_keep.reshape(chunks + 1, chips, 2, span, width)
        parts_b = grad_send.reshape(chips, 2, span_ff, width)
        vector_rows = jnp.broadcast_to(grad_vectors.astype(LOW), (chips, 16, width))
        grad_keep, grad_send = (
            jnp.concatenate(
                [pick(parts_a[c], which, 1)[:, 0] for c in range(chunks + 1)]
                + [pick(parts_b, which, 1)[:, 0], vector_rows],
                1,
            )
            for which in (core, 1 - core)
        )
    grad_other = swap(grad_send)

    back_first = attend_back(0, near, rand, glob_at, bias, log_first, qkv_first, mine, come)
    back_first, grad_other = join(back_first, grad_other)
    chip_sums = added(grad_keep, grad_other)
    qkv_rest, chip_sums = join(qkv_rest, chip_sums)
    own_sums = reduce_chips(chip_sums)
    grad_qkv, grad_own, grad_theirs, sums = attend_back(
        1, near, rand, glob_at, bias, log_rest, qkv_rest, mine, come, back_first, w_qkv
    )
    come = swap(grad_theirs)
    grad_qkv, own_sums = join(grad_qkv, own_sums)
    grad_tokens = (grad_first + grad_own + come.astype(WIDE)).astype(LOW)
    grad_inputs = send_back(grad_tokens)
    grad_w_qkv = dot(tokens, grad_qkv, TN).astype(LOW)
    lines = jnp.broadcast_to(sums.astype(LOW), (chips, 2, n_seq, 8, 3 * half_width))
    parts = jnp.concatenate(
        [grad_w_qkv.reshape(chips, 2, n_seq, rows_in, 3 * half_width), lines], 3
    )
    own_qkv = reduce_seq(reduce_chips(parts).transpose(1, 0, 2, 3))
    come = swap(pick(own_qkv, 1 - core, 0))[0]
    keep = pick(own_qkv, core, 0)[0]
    left, right = jnp.where(core == 0, keep, come), jnp.where(core == 0, come, keep)

    by_seq = own_sums[:rows_a].reshape(chunks + 1, n_seq, rows_in, width)
    by_seq = jnp.concatenate(
        [by_seq[c] for c in range(chunks + 1)]
        + [
            own_sums[rows_a:rows_b].reshape(n_seq, rows_ff, width),
            jnp.broadcast_to(own_sums[rows_b:], (n_seq, 16, width)),
        ],
        1,
    )
    own_sums = reduce_seq(by_seq)
    rows_a = (chunks + 1) * rows_in
    own_up = jnp.concatenate(
        [own_sums[c * rows_in : (c + 1) * rows_in] for c in range(chunks)], 1
    )
    small = own_sums[rows_a + rows_ff :]

    def joined(k, rows):
        lanes = [lanes_of(k, pair) for pair in range(pairs)]
        return jnp.concatenate([one[rows, at] for one in (left, right) for at in lanes], 1)

    def own_part(vector, size):
        return lax.dynamic_slice_in_dim(vector.reshape(-1), device * size, size, 0)

    matrix_rows, line = slice(0, rows_in), slice(rows_in, rows_in + 1)
    return (
        output,
        grad_inputs,
        joined(0, matrix_rows),
        own_part(joined(0, line), rows_in),
        joined(1, matrix_rows),
        joined(2, matrix_rows),
        own_part(joined(2, line), rows_in),
        own_sums[chunks * rows_in : rows_a],
        own_part(small[0], rows_in),
        own_part(small[1], rows_in),
        own_part(small[2], rows_in),
        own_up,
        own_part(small[6 : 6 + chunks], rows_ff),
        own_sums[rows_a : rows_a + rows_ff],
        own_part(small[3], rows_in),
        own_part(small[4], rows_in),
        own_part(small[5], rows_in),
    )


def solution(mesh):
    both = ("dp", "seq")
    matrix, vector = P(both, None), P(both)
    tokens = P("dp", "seq", None)
    return jax.shard_map(
        shards,
        mesh=mesh,
        in_specs=(tokens, tokens, P("dp", None, "seq", None), P("dp", None))
        + (matrix, vector, matrix, matrix, vector, matrix, vector, vector, vector)
        + (matrix, vector, matrix, vector, vector, vector),
        out_specs=(tokens, tokens)
        + (matrix, vector, matrix, matrix, vector, matrix, vector, vector, vector)
        + (matrix, vector, matrix, vector, vector, vector),
        check_vma=False,
    )
```

```python
from functools import partial

import jax
import jax.numpy as jnp
from jax import lax
from jax.experimental import pallas as pl
from jax.experimental.pallas import tpu as pltpu
from jax.sharding import PartitionSpec as P

HEADS = 12
HEAD = 64
BLOCK = 64
SLOTS = 8
EPS = 1e-06
NEG = -1e30
LOW = jnp.bfloat16
WIDE = jnp.float32

NT = (((1,), (1,)), ((), ()))
TN = (((0,), (0,)), ((), ()))
NN = (((1,), (0,)), ((), ()))


def dot(left, right, dims):
    return lax.dot_general(left, right, dims, preferred_element_type=WIDE)


def swap(array):
    size = lax.axis_size("dp")
    return lax.ppermute(array, "dp", [(i, i ^ 1) for i in range(size)])


def flip_seq(array, k):
    size = lax.axis_size("seq")
    return lax.ppermute(array, "seq", [(i, i ^ k) for i in range(size)])


def rounds():
    dp, seq = lax.axis_size("dp"), lax.axis_size("seq")
    for a in range(2):
        pairs = []
        for d in range(dp):
            for z in range(seq):
                to_dp = (d & ~1) | (z >> 1)
                to_seq = 2 * (d & 1) + (a ^ (z & 1))
                pairs.append((d * seq + z, to_dp * seq + to_seq))
        yield a, pairs


def bring(piece_of):
    z = lax.axis_index("seq")
    return [lax.ppermute(piece_of(a ^ (z & 1)), ("dp", "seq"), pairs) for a, pairs in rounds()]


def start_back(rows):
    size = rows.shape[0] // 2
    return [rows[size * a : size * a + size] for a in range(2)]


def finish_back(parts, which):
    a, pairs = list(rounds())[which]
    return lax.ppermute(parts[a], ("dp", "seq"), [(t, s) for s, t in pairs])


def send_back(rows):
    parts = start_back(rows)
    return [finish_back(parts, a) for a in range(2)]


def in_sequences(got):
    odd = (lax.axis_index("seq") & 1) == 1
    return jnp.stack([jnp.where(odd, got[1], got[0]), jnp.where(odd, got[0], got[1])])


def pick(array, index, axis):
    return lax.dynamic_slice_in_dim(array, index, 1, axis)


def gather_seq(shard, before=None):
    mirror = flip_seq(shard, 3)
    pair = jnp.stack([shard, mirror])
    if before is not None:
        pair = tie(pair, before)
    return shard, flip_seq(pair, 1), mirror


def in_seq_order(shard, near, mirror):
    z = lax.axis_index("seq")
    pieces = [shard, near[0], near[1], mirror]
    for bit in range(2):
        set_bit = ((z >> bit) & 1) == 1
        pieces = [
            jnp.where(set_bit, pieces[i ^ (1 << bit)], pieces[i]) for i in range(len(pieces))
        ]
    return pieces


def chip_groups():
    count = (lax.axis_size("dp") // 2).bit_length() - 1
    return [(bit, min(2, count - bit)) for bit in range(0, count, 2)]


def flip_chip(array, away):
    size = lax.axis_size("dp")
    return lax.ppermute(array, "dp", [(i, i ^ (2 * away)) for i in range(size)])


def gather_chips(part):
    parts = [part]
    for bit, bits in chip_groups():
        parts = parts + [flip_chip(p, k << bit) for k in range(1, 1 << bits) for p in parts]
    return parts


def in_chip_order(parts):
    chip = lax.axis_index("dp") >> 1
    parts = jnp.stack(parts)
    return [pick(parts, q ^ chip, 0)[0] for q in range(parts.shape[0])]


def in_device_order(mine, theirs):
    core = lax.axis_index("dp") & 1
    parts = []
    for own, other in zip(in_chip_order(mine), in_chip_order(theirs)):
        parts += [jnp.where(core == 0, own, other), jnp.where(core == 0, other, own)]
    return jnp.concatenate(parts, 0)


def join(*values):
    return lax.optimization_barrier(values)


def gather_quads(upper, lower):
    return [upper, flip_chip(upper, 1), lower, flip_chip(lower, 2)]


def finish_quads(upper, upper_x, lower, lower_y):
    upper, lower = jnp.stack([upper, upper_x]), jnp.stack([lower, lower_y])
    return [upper, flip_chip(upper, 2), lower, flip_chip(lower, 1)]


def tie(values, *others):
    return lax.optimization_barrier((values, others))[0]


def added(*arrays):
    return sum(array.astype(WIDE) for array in arrays).astype(LOW)


def reduce_chips(parts):
    chip = lax.axis_index("dp") >> 1
    for bit, bits in chip_groups():
        ways = 1 << bits
        parts = parts.reshape((-1, ways) + parts.shape[1:])
        mine = (chip >> bit) & (ways - 1)
        others = [flip_chip(pick(parts, mine ^ k, 1)[:, 0], k << bit) for k in range(1, ways)]
        parts = added(pick(parts, mine, 1)[:, 0], *others)
    return parts[0]


def reduce_seq(parts):
    z = lax.axis_index("seq")
    near = flip_seq(jnp.concatenate([pick(parts, z ^ 1, 0), pick(parts, z ^ 2, 0)], 0), 1)
    mirror = added(pick(parts, z ^ 3, 0)[0], near[1])
    return pick(parts, z, 0)[0].astype(WIDE) + near[0].astype(WIDE) + flip_seq(mirror, 3).astype(WIDE)


def norm_parts(summed):
    center = summed - jnp.mean(summed, -1, keepdims=True)
    spread = jnp.mean(center * center, -1, keepdims=True)
    scale = lax.rsqrt(spread + EPS)
    return center * scale, scale


def norm_back(grad, unit, scale, gain):
    grad_unit = grad * gain
    mean_one = jnp.mean(grad_unit, -1, keepdims=True)
    mean_two = jnp.mean(grad_unit * unit, -1, keepdims=True)
    return scale * (grad_unit - mean_one - unit * mean_two)


def gelu_parts(x):
    size = jnp.abs(x)
    t = 1.0 / (1.0 + (0.3275911 * 0.5**0.5) * size)
    bell = jnp.exp(-0.5 * x * x)
    series = 0.5 * 1.061405429
    for factor in (-1.453152027, 1.421413741, -0.284496736, 0.254829592):
        series = series * t + 0.5 * factor
    tail = series * t * bell
    share = jnp.where(x >= 0, 1.0 - tail, tail)
    return x * share, share + x * bell * 0.3989422804014327


def block_rows(ref, block, lanes):
    return ref[pl.ds(pl.multiple_of(block * BLOCK, BLOCK), BLOCK), lanes]


def diagonal(pair_rows, low):
    zero = jnp.zeros_like(pair_rows)
    return jnp.concatenate(
        [jnp.where(low, pair_rows, zero), jnp.where(low, zero, pair_rows)], axis=0
    )


def gather_blocks(ref, ids, lanes, low):
    parts = []
    for one, two in ids:
        if two is None:
            parts.append(block_rows(ref, one, lanes))
        else:
            parts.append(
                jnp.where(low, block_rows(ref, one, lanes), block_rows(ref, two, lanes))
            )
    return jnp.concatenate(parts, axis=0)


def slot_ids(near_ref, rand_ref, globs, i, head, blocks):
    ids = [(near_ref[i], None), (i, None), (near_ref[blocks + i], None)]
    ids += [(globs[0], None), (globs[1], None)]
    for r in range(3):
        ids.append(
            (
                rand_ref[(head * blocks + i) * 3 + r],
                rand_ref[((head + 1) * blocks + i) * 3 + r],
            )
        )
    return ids


def lanes_of(part, pair):
    first = 128 * (3 * pair + part)
    return slice(first, first + 128)


def flat_lanes(pair):
    return slice(128 * pair, 128 * pair + 128)


def start_copies(copies, sems):
    started = [
        pltpu.make_async_copy(source, target, sems.at[k])
        for k, (source, target) in enumerate(copies)
    ]
    for copy in started:
        copy.start()
    return started


def project_kernel(chips, direct, at_ref, *refs):
    pieces, b_ref = refs[:4], refs[4]
    sources, (first_ref, rest_ref, tokens_ref, w_ref, sems) = refs[5:-5], refs[-5:]
    if direct:
        span = w_ref.shape[0] // (2 * chips)
        copies = [
            (
                sources[away].at[k, :span],
                w_ref.at[pl.ds(pl.multiple_of((2 * (at_ref[0] ^ away) + k) * span, span), span)],
            )
            for away in range(chips)
            for k in range(2)
        ]
    else:
        copies = [(sources[0], w_ref)]
    for copy in start_copies(copies, sems):
        copy.wait()
    tile = 256
    lane = lax.broadcasted_iota(jnp.int32, (1, w_ref.shape[1]), 1)
    scale = jnp.where(lane % 384 < 128, HEAD ** (-0.5), 1.0)

    size = pieces[0].shape[0]
    for k, piece_ref in enumerate(pieces):

        def body(at, carry, k=k, piece_ref=piece_ref):
            tokens = piece_ref[pl.ds(pl.multiple_of(at * tile, tile), tile)]
            rows = pl.ds(pl.multiple_of(k * size + at * tile, tile), tile)
            tokens_ref[rows] = tokens
            values = (dot(tokens, w_ref[...], NN) + b_ref[...]).astype(LOW).astype(WIDE)
            values = (values * scale).astype(LOW)
            cut = first_ref.shape[1]
            first_ref[rows] = values[:, :cut]
            rest_ref[rows] = values[:, cut:]
            return carry

        lax.fori_loop(0, size // tile, body, 0, unroll=True)


def attend_kernel(
    first_pair, pairs, blocks, step, near_ref, rand_ref, glob_ref, bias_ref, qkv_ref, out_ref, log_ref
):
    low = lax.broadcasted_iota(jnp.int32, (1, 2 * HEAD), 1) < HEAD
    globs = (glob_ref[0], glob_ref[1])

    def scores_of(i, pair):
        ids = slot_ids(near_ref, rand_ref, globs, i, 2 * (first_pair + pair), blocks)
        queries = diagonal(block_rows(qkv_ref, i, lanes_of(0, pair)), low)
        return dot(gather_blocks(qkv_ref, ids, lanes_of(1, pair), low), queries, NT)

    def softmax_of(i, pair, scores):
        highest = jnp.max(scores, axis=0, keepdims=True)
        weights = jnp.exp(scores - highest)
        total = jnp.sum(weights, axis=0, keepdims=True)
        log_ref[i, pair : pair + 1] = highest + jnp.log(total)
        return (weights * (1.0 / total)).astype(LOW)

    def put(i, pair, mixed):
        at = pl.ds(pl.multiple_of(i * BLOCK, BLOCK), BLOCK)
        out_ref[at, flat_lanes(pair)] = jnp.where(low, mixed[:BLOCK], mixed[BLOCK:]).astype(LOW)

    def body(at, carry):
        units = [(at * step + d, pair) for d in range(step) for pair in range(pairs)]
        scores = [scores_of(*unit) for unit in units]
        probs = []
        for (i, pair), score in zip(units, scores):
            bias = bias_ref[i, first_pair + pair]
            score = jnp.concatenate(
                [score[BLOCK * j : BLOCK * j + BLOCK] + bias[j : j + 1] for j in range(SLOTS)],
                axis=0,
            )
            probs.append(softmax_of(i, pair, score))
        for (i, pair), prob in zip(units, probs):
            ids = slot_ids(near_ref, rand_ref, globs, i, 2 * (first_pair + pair), blocks)
            values = gather_blocks(qkv_ref, ids, lanes_of(2, pair), low)
            put(i, pair, dot(prob, values, TN))
        return carry

    lax.fori_loop(0, blocks // step, body, 0)

    def whole_row(n, carry):
        i = glob_ref[n]
        scores = []
        for pair in range(pairs):
            queries = diagonal(block_rows(qkv_ref, i, lanes_of(0, pair)), low)
            scores.append(dot(qkv_ref[:, lanes_of(1, pair)], queries, NT))
        probs = [softmax_of(i, pair, scores[pair]) for pair in range(pairs)]
        for pair in range(pairs):
            put(i, pair, dot(probs[pair], qkv_ref[:, lanes_of(2, pair)], TN))
        return carry

    lax.fori_loop(0, 2, whole_row, 0)


def attend_back_kernel(
    blocks,
    step,
    near_ref,
    rand_ref,
    glob_ref,
    bias_ref,
    log_first_ref,
    log_rest_ref,
    qkv_first_ref,
    qkv_rest_ref,
    mine_ref,
    come_ref,
    w_ref,
    grad_first_ref,
    out_ref,
    rows_own_ref,
    rows_other_ref,
    sums_ref,
    grad_ref,
    acc_ref,
):
    low = lax.broadcasted_iota(jnp.int32, (1, 2 * HEAD), 1) < HEAD
    globs = (glob_ref[0], glob_ref[1])
    acc_ref[...] = jnp.zeros_like(acc_ref)
    half = mine_ref.shape[0]
    grad_ref[:half] = mine_ref[...]
    grad_ref[half:] = come_ref[...]
    pairs = mine_ref.shape[1] // 128
    cut = qkv_first_ref.shape[1] // 384

    def source(pair, part):
        ref, at = (qkv_first_ref, pair) if pair < cut else (qkv_rest_ref, pair - cut)
        return ref.at[:, lanes_of(part, at)]

    def log_of(i, pair):
        ref, at = (log_first_ref, pair) if pair < cut else (log_rest_ref, pair - cut)
        return ref[i, at : at + 1]

    every = slice(None)

    def add(part, pair, block, value):
        at = pl.ds(pl.multiple_of(block * BLOCK, BLOCK), BLOCK)
        lanes = flat_lanes(2 * pair + part)
        acc_ref[at, lanes] = acc_ref[at, lanes] + value

    def operands(i, pair):
        queries = diagonal(block_rows(source(pair, 0), i, every), low)
        grads = diagonal(block_rows(grad_ref, i, flat_lanes(pair)), low)
        return queries, grads

    def softmax_back(prob, grad_prob):
        scaled = prob * grad_prob
        inner = jnp.sum(scaled, axis=0, keepdims=True)
        return prob.astype(LOW), (scaled - prob * inner).astype(LOW)

    def put(i, pair, mixed):
        at = pl.ds(pl.multiple_of(i * BLOCK, BLOCK), BLOCK)
        out_ref[at, lanes_of(0, pair)] = (
            jnp.where(low, mixed[:BLOCK], mixed[BLOCK:]) * HEAD ** (-0.5)
        ).astype(LOW)

    def body(at, carry):
        units = [(at * step + d, pair) for d in range(step) for pair in range(pairs)]
        first = []
        for i, pair in units:
            ids = slot_ids(near_ref, rand_ref, globs, i, 2 * pair, blocks)
            queries, grads = operands(i, pair)
            first.append(
                (
                    dot(gather_blocks(source(pair, 1), ids, every, low), queries, NT),
                    dot(gather_blocks(source(pair, 2), ids, every, low), grads, NT),
                )
            )
        second = []
        for (i, pair), (score, grad_prob) in zip(units, first):
            shift = bias_ref[i, pair] - log_of(i, pair)
            prob = jnp.concatenate(
                [
                    jnp.exp(score[BLOCK * j : BLOCK * j + BLOCK] + shift[j : j + 1])
                    for j in range(SLOTS)
                ],
                axis=0,
            )
            second.append(softmax_back(prob, grad_prob))
        third = []
        for (i, pair), (prob, grad_score) in zip(units, second):
            ids = slot_ids(near_ref, rand_ref, globs, i, 2 * pair, blocks)
            queries, grads = operands(i, pair)
            keys = gather_blocks(source(pair, 1), ids, every, low)
            put(i, pair, dot(grad_score, keys, TN))
            third.append((dot(grad_score, queries, NN), dot(prob, grads, NN)))
        for (i, pair), values in zip(units, third):
            ids = slot_ids(near_ref, rand_ref, globs, i, 2 * pair, blocks)
            for j, (one, two) in enumerate(ids):
                for part, value in enumerate(values):
                    value = value[BLOCK * j : BLOCK * j + BLOCK]
                    if two is None:
                        add(part, pair, one, value)
                    else:
                        add(part, pair, one, jnp.where(low, value, 0.0))
                        add(part, pair, two, jnp.where(low, 0.0, value))
        return carry

    lax.fori_loop(0, blocks // step, body, 0)

    def whole_row(n, carry):
        i = glob_ref[n]
        first = []
        for pair in range(pairs):
            queries, grads = operands(i, pair)
            first.append(
                (
                    dot(source(pair, 1)[...], queries, NT),
                    dot(source(pair, 2)[...], grads, NT),
                )
            )
        second = []
        for pair, (score, grad_prob) in enumerate(first):
            prob = jnp.exp(score - log_of(i, pair))
            second.append(softmax_back(prob, grad_prob))
        for pair, (prob, grad_score) in enumerate(second):
            queries, grads = operands(i, pair)
            acc_ref[:, flat_lanes(2 * pair)] += dot(grad_score, queries, NN)
            acc_ref[:, flat_lanes(2 * pair + 1)] += dot(prob, grads, NN)
            put(i, pair, dot(grad_score, source(pair, 1)[...], TN))
        return carry

    lax.fori_loop(0, jnp.where(globs[0] == globs[1], 1, 2), whole_row, 0)
    for pair in range(pairs):
        out_ref[:, 384 * pair + 128 : 384 * pair + 384] = acc_ref[
            :, 256 * pair : 256 * pair + 256
        ].astype(LOW)

    sums_ref[...] = jnp.zeros_like(sums_ref)
    tile = 512
    for side, rows_ref in enumerate((rows_own_ref, rows_other_ref)):

        def token_rows(at, carry, side=side, rows_ref=rows_ref):
            grads = out_ref[pl.ds(pl.multiple_of(side * half + at * tile, tile), tile)]
            sums_ref[...] += jnp.sum(grads.astype(WIDE), 0, keepdims=True)
            rows = pl.ds(pl.multiple_of(at * tile, tile), tile)
            total = dot(grads, w_ref[...], NT)
            if side == 0:
                total = total + grad_first_ref[rows].astype(WIDE)
            rows_ref[rows] = total.astype(LOW)
            return carry

        lax.fori_loop(0, half // tile, token_rows, 0)


def pack_kernel(seq, chunks, cut, at_ref, shard_ref, near_ref, mirror_ref, upper_ref, lower_ref):
    rows = shard_ref.shape[0] - 16
    rows_in = rows // (chunks + 4)
    rows_ff = rows - chunks * rows_in
    pieces = [shard_ref, near_ref.at[0], near_ref.at[1], mirror_ref]
    total = sum(piece[rows:].astype(WIDE) for piece in pieces)

    def put(first, value):
        target, first = (upper_ref, first) if first < cut else (lower_ref, first - cut)
        target[first : first + value.shape[0]] = value

    put(rows * seq, total.astype(LOW))
    for z in range(seq):

        @pl.when(at_ref[2] == z)
        def _(z=z):
            for k, piece in enumerate(pieces):
                for c in range(chunks):
                    put((c * seq + (z ^ k)) * rows_in, piece[c * rows_in : c * rows_in + rows_in])
                put(chunks * seq * rows_in + (z ^ k) * rows_ff, piece[chunks * rows_in : rows])


def unpack_kernel(seq, chunks, at_ref, in_ref, down_ref, near_ref, keep_ref):
    rows_in, rows_ff = in_ref.shape[1] // seq, down_ref.shape[0] // seq
    for z in range(seq):

        @pl.when(at_ref[2] == z)
        def _(z=z):
            for k in range(seq):
                target = (keep_ref, near_ref)[k in (1, 2)].at[int(k > 1)]
                first = (z ^ k) * rows_in
                for c in range(chunks):
                    target[c * rows_in : c * rows_in + rows_in] = in_ref[c, first : first + rows_in]
                first = (z ^ k) * rows_ff
                target[chunks * rows_in :] = down_ref[first : first + rows_ff]


def weight_copies(chips, direct, chip, core, sources, w_in_ref, w_down_ref, lines_ref):
    if not direct:
        return [(sources[0], w_in_ref), (sources[1], w_down_ref), (sources[2], lines_ref)]
    wide, width = w_down_ref.shape
    chunks = wide // width
    span, span_ff = width // (2 * chips), wide // (2 * chips)
    cut = span // 2
    copies = []
    for k in range(2):
        for away in range(chips):
            place = 2 * (chip ^ away) + (core if k == 0 else 1 - core)
            upper = sources[4 * k + (away >> 1)].at[away & 1]
            lower = sources[4 * k + 2 + (away & 1)].at[away >> 1]
            rows = pl.ds(pl.multiple_of(place * span, span), span)
            copies += [
                (upper.at[span * c : span * c + span], w_in_ref.at[c, rows]) for c in range(chunks)
            ]
            for half, source in enumerate((upper.at[span * chunks :], lower.at[:cut])):
                rows = pl.ds(pl.multiple_of(place * span + half * cut, cut), cut)
                copies.append((source, w_in_ref.at[chunks, rows]))
            rows = pl.ds(pl.multiple_of(place * span_ff, span_ff), span_ff)
            copies.append((lower.at[cut : cut + span_ff], w_down_ref.at[rows]))
            copies.append((lower.at[cut + span_ff :], lines_ref.at[k * chips + away]))
    return copies


def forward_kernel(
    chips,
    direct,
    at_ref,
    mixed_first_ref,
    mixed_rest_ref,
    other_first_ref,
    other_rest_ref,
    tokens_ref,
    grad_first_ref,
    grad_last_ref,
    *refs,
):
    sources, refs = refs[:-15], refs[-15:]
    output_ref, slope_ref, normed_ref, unit_one_ref, grad_second_ref, scale_ref, g_down_ref, sums_ref = refs[:8]
    w_in_ref, w_down_ref, lines_ref, hidden_ref, down_ref, sems, out_sems = refs[8:]
    wide, width = w_down_ref.shape
    half, chunks = width // 2, wide // width
    core = at_ref[1]
    copies = weight_copies(chips, direct, at_ref[0], core, sources, w_in_ref, w_down_ref, lines_ref)

    @pl.when(pl.program_id(0) == 0)
    def _():
        sums_ref[...] = jnp.zeros_like(sums_ref)
        for copy in start_copies(copies, sems):
            copy.wait()

    at, last = pl.program_id(0), pl.num_programs(0) - 1
    tile = tokens_ref.shape[0]
    rows = pl.ds(pl.multiple_of(at * tile, tile), tile)
    vectors = jnp.sum(lines_ref[...].astype(WIDE), 0)
    b_out, gain_one, shift_one, b_down, gain_two, shift_two = (vectors[k : k + 1] for k in range(6))
    here = pl.ds(pl.multiple_of(core * half, 128), half)
    there = pl.ds(pl.multiple_of((1 - core) * half, 128), half)
    mixed = jnp.concatenate([mixed_first_ref[...], mixed_rest_ref[...]], 1)
    other = jnp.concatenate([other_first_ref[...], other_rest_ref[...]], 1)
    branch = dot(mixed, w_in_ref[chunks, here], NN) + dot(other, w_in_ref[chunks, there], NN)
    unit_one, scale_one = norm_parts(tokens_ref[...].astype(WIDE) + (branch + b_out))
    normed = unit_one * gain_one + shift_one
    normed_low = normed.astype(LOW)
    normed_ref[...] = normed_low
    unit_one_ref[...] = unit_one
    down = b_down
    for c in range(0, chunks, 2):
        lanes = slice(width * c, width * c + 2 * width)
        weights = jnp.concatenate([w_in_ref[c], w_in_ref[c + 1]], 1)
        bias = jnp.concatenate([vectors[6 + c : 7 + c], vectors[7 + c : 8 + c]], 1)
        hidden, slope = gelu_parts(dot(normed_low, weights, NN) + bias)
        hidden = hidden.astype(LOW)
        hidden_ref[rows, lanes] = hidden
        slope_ref[:, lanes] = slope.astype(LOW)
        down = down + dot(hidden, w_down_ref[lanes], NN)
    unit_two, scale_two = norm_parts(normed + down)
    output_ref[...] = (unit_two * gain_two + shift_two).astype(LOW)
    lane = lax.broadcasted_iota(jnp.int32, (1, 128), 1)
    scale_ref[...] = jnp.where(lane < 128, scale_one, 0.0)
    grad = jnp.where(2 * at <= last, grad_first_ref[...], grad_last_ref[...]).astype(WIDE)
    sums_ref[4:5] += jnp.sum(grad * unit_two, 0, keepdims=True)
    sums_ref[5:6] += jnp.sum(grad, 0, keepdims=True)
    grad_second = norm_back(grad, unit_two, scale_two, gain_two)
    grad_second_ref[...] = grad_second
    grad_down = grad_second.astype(LOW)
    down_ref[rows] = grad_down
    sums_ref[3:4] += jnp.sum(grad_down.astype(WIDE), 0, keepdims=True)

    @pl.when(at == last)
    def _():
        moving = []
        for c in range(chunks):
            lanes = slice(width * c, width * c + width)
            w_down_ref[lanes] = dot(hidden_ref[:, lanes], down_ref[...], TN).astype(LOW)
            copy = pltpu.make_async_copy(w_down_ref.at[lanes], g_down_ref.at[lanes], out_sems.at[c])
            copy.start()
            moving.append(copy)
        for copy in moving:
            copy.wait()


def backward_kernel(
    tile,
    chips,
    direct,
    at_ref,
    mixed_first_ref,
    mixed_rest_ref,
    other_first_ref,
    other_rest_ref,
    slope_ref,
    unit_one_ref,
    grad_second_ref,
    scale_ref,
    normed_hbm,
    *refs,
):
    sources, refs = refs[:-15], refs[-15:]
    first_ref, mine_ref, theirs_ref, g_in_ref, sums_ref = refs[:5]
    w_in_ref, w_down_ref, lines_ref, vectors_ref, pre_ref, branch_ref, normed_ref = refs[5:12]
    sems, extra_sem, out_sems = refs[12:]
    own, width = normed_ref.shape
    wide = w_down_ref.shape[0]
    half, chunks = width // 2, wide // width
    chip, core = at_ref[0], at_ref[1]
    at, last = pl.program_id(0), pl.num_programs(0) - 1
    rows = pl.ds(pl.multiple_of(at * tile, tile), tile)
    copies = weight_copies(chips, direct, chip, core, sources, w_in_ref, w_down_ref, lines_ref)
    extra = pltpu.make_async_copy(normed_hbm, normed_ref, extra_sem.at[0])
    here = pl.ds(pl.multiple_of(core * half, 128), half)
    there = pl.ds(pl.multiple_of((1 - core) * half, 128), half)

    @pl.when(at == 0)
    def _():
        started = start_copies(copies, sems)
        extra.start()
        sums_ref[...] = jnp.zeros_like(sums_ref)
        for copy in started:
            copy.wait()
        vectors_ref[...] = jnp.sum(lines_ref[...].astype(WIDE), 0)

    def add_sum(k, value):
        sums_ref[k : k + 1] += jnp.sum(value, 0, keepdims=True)

    grad_normed = grad_second_ref[...]
    grad_down = grad_normed.astype(LOW)
    for c in range(chunks):
        lanes = slice(width * c, width * c + width)
        grad_pre = dot(grad_down, w_down_ref[lanes], NT) * slope_ref[:, lanes].astype(WIDE)
        grad_pre = grad_pre.astype(LOW)
        pre_ref[rows, lanes] = grad_pre
        add_sum(6 + c, grad_pre.astype(WIDE))
        grad_normed = grad_normed + dot(grad_pre, w_in_ref[c], NT)
    unit_one = unit_one_ref[...]
    add_sum(1, grad_normed * unit_one)
    add_sum(2, grad_normed)
    grad_branch = norm_back(grad_normed, unit_one, scale_ref[:, 0:1], vectors_ref[1:2]).astype(LOW)
    first_ref[...] = grad_branch
    branch_ref[rows] = grad_branch
    add_sum(0, grad_branch.astype(WIDE))
    mine_ref[...] = dot(grad_branch, w_in_ref[chunks, here], NT).astype(LOW)
    theirs_ref[...] = dot(grad_branch, w_in_ref[chunks, there], NT).astype(LOW)

    @pl.when(at == last)
    def _():
        extra.wait()
        moving = []

        def leave(c):
            copy = pltpu.make_async_copy(w_in_ref.at[c], g_in_ref.at[c], out_sems.at[c])
            copy.start()
            moving.append(copy)

        for c in range(chunks):
            lanes = slice(width * c, width * c + width)
            w_in_ref[c] = dot(normed_ref[...], pre_ref[:, lanes], TN).astype(LOW)
            leave(c)
        mixed = jnp.concatenate([mixed_first_ref[...], mixed_rest_ref[...]], 1)
        other = jnp.concatenate([other_first_ref[...], other_rest_ref[...]], 1)
        w_in_ref[chunks, here] = dot(mixed, branch_ref[...], TN).astype(LOW)
        w_in_ref[chunks, there] = dot(other, branch_ref[...], TN).astype(LOW)
        leave(chunks)
        for copy in moving:
            copy.wait()


IN_SMEM = pl.BlockSpec(memory_space=pltpu.SMEM)
IN_VMEM = pl.BlockSpec(memory_space=pltpu.VMEM)


IN_ANY = pl.BlockSpec(memory_space=pl.ANY)


def project_tokens(at, pieces, b_qkv, weights, direct):
    length, width = 4 * pieces[0].shape[0], pieces[0].shape[1]
    half = width // 2
    chips = lax.axis_size("dp") // 2
    return pl.pallas_call(
        partial(project_kernel, chips, direct),
        out_shape=(
            jax.ShapeDtypeStruct((length, 384), LOW),
            jax.ShapeDtypeStruct((length, 3 * half - 384), LOW),
            jax.ShapeDtypeStruct((length, width), LOW),
            jax.ShapeDtypeStruct((width, 3 * half), LOW),
        ),
        in_specs=[IN_SMEM] + [IN_VMEM] * 5 + [IN_ANY] * len(weights),
        out_specs=(IN_VMEM,) * 4,
        scratch_shapes=[pltpu.SemaphoreType.DMA((2 * chips,))],
        compiler_params=pltpu.CompilerParams(vmem_limit_bytes=48 << 20),
        cost_estimate=pl.CostEstimate(
            flops=4_000_000_000, bytes_accessed=12_000_000, transcendentals=0
        ),
        name="project",
    )(at, *pieces, b_qkv, *weights)


def attend(first_pair, near, rand, globs, bias, qkv):
    length, width = qkv.shape
    pairs, blocks = width // 384, length // BLOCK
    return pl.pallas_call(
        partial(attend_kernel, first_pair, pairs, blocks, 8 // pairs),
        out_shape=(
            jax.ShapeDtypeStruct((length, 128 * pairs), LOW),
            jax.ShapeDtypeStruct((blocks, 8, 128), WIDE),
        ),
        in_specs=[IN_SMEM] * 3 + [IN_VMEM] * 2,
        out_specs=(IN_VMEM,) * 2,
        compiler_params=pltpu.CompilerParams(vmem_limit_bytes=48 << 20),
        cost_estimate=pl.CostEstimate(
            flops=6_000_000_000 * pairs, bytes_accessed=3_000_000 * pairs, transcendentals=0
        ),
        name="attend",
    )(near, rand, globs, bias, qkv)


def attend_back(near, rand, globs, bias, logs, qkvs, mine, come, w_qkv, grad_first):
    length, (wide, width) = qkvs[0].shape[0], w_qkv.shape
    pairs, blocks = width // 384, length // BLOCK
    rows = jax.ShapeDtypeStruct((length // 2, wide), LOW)
    return pl.pallas_call(
        partial(attend_back_kernel, blocks, 2),
        out_shape=(
            jax.ShapeDtypeStruct((length, width), LOW),
            rows,
            rows,
            jax.ShapeDtypeStruct((1, width), WIDE),
        ),
        in_specs=[IN_SMEM] * 3 + [IN_VMEM] * 9,
        out_specs=(IN_VMEM,) * 4,
        scratch_shapes=[
            pltpu.VMEM((length, 128 * pairs), LOW),
            pltpu.VMEM((length, 256 * pairs), WIDE),
        ],
        compiler_params=pltpu.CompilerParams(vmem_limit_bytes=56 << 20),
        cost_estimate=pl.CostEstimate(
            flops=40_000_000_000, bytes_accessed=20_000_000, transcendentals=0
        ),
        name="attend_back",
    )(near, rand, globs, bias, *logs, *qkvs, mine, come, w_qkv, grad_first)


def pack_rows(at, shard, near, mirror, chunks, cut):
    rows, width = 4 * (shard.shape[0] - 16) + 16, shard.shape[1]
    return pl.pallas_call(
        partial(pack_kernel, 4, chunks, cut),
        out_shape=(
            jax.ShapeDtypeStruct((cut, width), LOW),
            jax.ShapeDtypeStruct((rows - cut, width), LOW),
        ),
        in_specs=[IN_SMEM] + [IN_VMEM] * 3,
        out_specs=(IN_VMEM, IN_VMEM),
        name="pack",
    )(at, shard, near, mirror)


TILE = 256


def tiles(width, first=0, many=None):
    if many is None:
        return pl.BlockSpec((TILE, width), lambda i: (i, 0))
    return pl.BlockSpec((TILE, width), lambda i: (jnp.clip(i - first, 0, many - 1), 0))


def weight_space(chips, direct, chunks, width):
    return [
        pltpu.VMEM((chunks + 1, width, width), LOW),
        pltpu.VMEM((chunks * width, width), LOW),
        pltpu.VMEM((2 * chips if direct else 1, 16, width), LOW),
    ]


def unpack_rows(at, rows_in, rows_down):
    chunks, span, width = rows_in.shape
    like = jax.ShapeDtypeStruct((2, (chunks * span + rows_down.shape[0]) // 4, width), LOW)
    return pl.pallas_call(
        partial(unpack_kernel, 4, chunks),
        out_shape=(like, like),
        in_specs=[IN_SMEM] + [IN_VMEM] * 2,
        out_specs=(IN_VMEM, IN_VMEM),
        name="unpack",
    )(at, rows_in, rows_down)


def layer_forward(at, mixed, other, tokens, grads, weights, direct, chunks):
    own, width = other[0].shape[0], tokens.shape[1]
    chips, wide = lax.axis_size("dp") // 2, chunks * width
    many = own // TILE // 2

    def rows(width, kind=LOW):
        return jax.ShapeDtypeStruct((own, width), kind)

    return pl.pallas_call(
        partial(forward_kernel, chips, direct),
        grid=(own // TILE,),
        out_shape=(rows(width), rows(wide), rows(width))
        + (rows(width, WIDE), rows(width, WIDE), rows(128, WIDE))
        + (jax.ShapeDtypeStruct((wide, width), LOW), jax.ShapeDtypeStruct((16, width), WIDE)),
        in_specs=[IN_SMEM]
        + [tiles(p.shape[1]) for p in (*mixed, *other, tokens)]
        + [tiles(width, 0, many), tiles(width, many, many)]
        + [IN_ANY] * len(weights),
        out_specs=tuple(tiles(w) for w in (width, wide, width, width, width, 128))
        + (IN_ANY, pl.BlockSpec((16, width), lambda i: (0, 0))),
        scratch_shapes=weight_space(chips, direct, chunks, width)
        + [
            pltpu.VMEM((own, wide), LOW),
            pltpu.VMEM((own, width), LOW),
            pltpu.SemaphoreType.DMA((2 * chips * (chunks + 4),)),
            pltpu.SemaphoreType.DMA((chunks,)),
        ],
        compiler_params=pltpu.CompilerParams(vmem_limit_bytes=58 << 20),
        cost_estimate=pl.CostEstimate(
            flops=22_000_000_000, bytes_accessed=36_000_000, transcendentals=0
        ),
        name="layer_forward",
    )(at, *mixed, *other, tokens, *grads, *weights)


def layer_backward(at, mixed, other, slope, unit_one, grad_second, scale, normed, weights, direct):
    own, width = normed.shape
    wide = slope.shape[1]
    half, chunks = width // 2, wide // width
    chips = lax.axis_size("dp") // 2
    whole = pl.BlockSpec((own, 128), lambda i: (0, 0)), pl.BlockSpec((own, half - 128), lambda i: (0, 0))
    return pl.pallas_call(
        partial(backward_kernel, TILE, chips, direct),
        grid=(own // TILE,),
        out_shape=(
            jax.ShapeDtypeStruct((own, width), LOW),
            jax.ShapeDtypeStruct((own, half), LOW),
            jax.ShapeDtypeStruct((own, half), LOW),
            jax.ShapeDtypeStruct((chunks + 1, width, width), LOW),
            jax.ShapeDtypeStruct((16, width), WIDE),
        ),
        in_specs=[IN_SMEM]
        + [whole[0], whole[1]] * 2
        + [tiles(wide), tiles(width), tiles(width), tiles(128)]
        + [IN_ANY] * (1 + len(weights)),
        out_specs=(tiles(width), tiles(half), tiles(half), IN_ANY)
        + (pl.BlockSpec((16, width), lambda i: (0, 0)),),
        scratch_shapes=weight_space(chips, direct, chunks, width)
        + [
            pltpu.VMEM((16, width), WIDE),
            pltpu.VMEM((own, wide), LOW),
            pltpu.VMEM((own, width), LOW),
            pltpu.VMEM((own, width), LOW),
            pltpu.SemaphoreType.DMA((2 * chips * (chunks + 4),)),
            pltpu.SemaphoreType.DMA((1,)),
            pltpu.SemaphoreType.DMA((chunks + 1,)),
        ],
        compiler_params=pltpu.CompilerParams(vmem_limit_bytes=58 << 20),
        cost_estimate=pl.CostEstimate(
            flops=22_000_000_000, bytes_accessed=40_000_000, transcendentals=0
        ),
        name="layer_backward",
    )(at, *mixed, *other, slope, unit_one, grad_second, scale, normed, *weights)


def place_of(block, core, z, blocks):
    quarter, row = block // (blocks // 4), block % (blocks // 4)
    a = (quarter & 1) ^ (z & 1)
    return ((quarter >> 1) ^ core) * (blocks // 2) + a * (blocks // 4) + row


def block_at(place, core, z, blocks):
    quarter = 2 * ((place // (blocks // 2)) ^ core) + ((place % (blocks // 2)) // (blocks // 4) ^ (z & 1))
    return quarter * (blocks // 4) + place % (blocks // 4)


def tables(rand, globs, blocks):
    core = lax.axis_index("dp") & 1
    z = lax.axis_index("seq")
    here = block_at(jnp.arange(blocks, dtype=jnp.int32), core, z, blocks)
    heads = rand.shape[0]
    one, two = globs[0], globs[1]

    def near(block):
        return jnp.abs(block - here) <= 1

    every = jnp.ones((heads, blocks), bool)
    ok = [every & (here > 0), every, every & (here < blocks - 1)]
    ok += [every & ~near(one), every & ~near(two) & (one != two)]
    seen = []
    for r in range(3):
        block = rand[:, :, r]
        good = ~near(block) & (block != one) & (block != two)
        for before in seen:
            good = good & (block != before)
        seen.append(block)
        ok.append(good)
    whole_row = (here == one) | (here == two)
    ok = jnp.stack(ok, -1) & ~whole_row[None, :, None]
    bias = jnp.where(ok, 0.0, NEG).astype(WIDE)
    bias = bias.reshape(heads // 2, 2, blocks, SLOTS).transpose(2, 0, 3, 1)
    bias = jnp.repeat(bias, HEAD, axis=3)
    put = partial(place_of, core=core, z=z, blocks=blocks)
    sides = jnp.concatenate([put(jnp.maximum(here - 1, 0)), put(jnp.minimum(here + 1, blocks - 1))])
    return sides, put(rand).reshape(-1), put(globs), bias


def shards(
    inputs,
    cotangent,
    rand_blocks,
    global_blocks,
    w_query,
    b_query,
    w_key,
    w_value,
    b_value,
    w_out,
    b_out,
    gain_one,
    shift_one,
    w_up,
    b_up,
    w_down,
    b_down,
    gain_two,
    shift_two,
):
    n_dp, n_seq = lax.axis_size("dp"), lax.axis_size("seq")
    chips, devices = n_dp // 2, n_dp * n_seq
    core = lax.axis_index("dp") & 1
    z = lax.axis_index("seq")
    device = lax.axis_index("dp") * n_seq + z
    rows_in, width = w_query.shape
    rows_ff, wide = w_down.shape[0], w_up.shape[1]
    chunks = wide // width
    half_width = width // 2
    _, quarter, _ = inputs.shape
    length = quarter * n_seq
    blocks = length // BLOCK
    own = length // 2
    own_heads = HEADS // 2
    span, span_ff = n_seq * rows_in, n_seq * rows_ff
    direct = span % 16 == 0 and chips == chunks

    here = jnp.arange(devices, dtype=jnp.int32)[:, None] == device

    def placed(vector):
        return jnp.where(here, vector[None], jnp.zeros((), LOW)).reshape(-1, width)

    q_line, v_line = placed(b_query), placed(b_value)

    pairs = half_width // 128

    def side(at):
        no_line = jnp.zeros((1, width), LOW)
        parts = []
        for pair in range(pairs):
            first = at * half_width + 128 * pair
            lanes = slice(first, first + 128)
            for w, line in ((w_query, q_line), (w_key, no_line), (w_value, v_line)):
                parts.append(jnp.concatenate([w[:, lanes], line[:, lanes]], 0))
        return jnp.pad(jnp.concatenate(parts, 1), ((0, 7), (0, 0)))

    left, right = side(0), side(1)
    keep = jnp.where(core == 0, left, right)
    come = swap(jnp.where(core == 0, right, left))
    shard = jnp.stack([jnp.where(core == 0, keep, come), jnp.where(core == 0, come, keep)])
    def numbers_of(s):
        numbers = pick(rand_blocks, s, 0).reshape(-1)
        numbers = jnp.concatenate([numbers, pick(global_blocks, s, 0).reshape(-1)])
        return jnp.pad(numbers, (0, -numbers.shape[0] % 128))

    numbers = jnp.stack(bring(numbers_of))
    qkv_z = gather_seq(tie(shard, numbers))

    packed = jnp.concatenate(
        [w_up[:, width * c : width * c + width] for c in range(chunks)]
        + [w_out, w_down]
        + [placed(v) for v in (b_out, gain_one, shift_one, b_down, gain_two, shift_two, b_up)]
        + [jnp.zeros((16 - 6 - chunks, width), LOW)],
        0,
    )
    wide_z = gather_seq(tie(packed, shard), qkv_z[2])
    at = jnp.stack([lax.axis_index("dp") >> 1, core, z]).astype(jnp.int32)

    numbers = tie(numbers, wide_z[2])
    numbers = jnp.concatenate([numbers, swap(numbers)], 0)
    local_blocks = rand_blocks.shape[2]
    count = HEADS * local_blocks * 3
    globs = numbers[0, count : count + 2]
    rand = numbers[:, :count].reshape(4, HEADS, local_blocks, 3)
    rand = lax.dynamic_slice_in_dim(rand, core * own_heads, own_heads, 1)
    rand = rand.transpose(1, 0, 2, 3).reshape(own_heads, blocks, 3)
    sides, rand, glob_at, bias = tables(rand, globs, blocks)

    qkv_z = in_seq_order(*qkv_z)
    whole = []
    for k in range(2):
        lines = sum(p[k, rows_in:].astype(WIDE) for p in qkv_z).astype(LOW)
        whole += [p[k, :rows_in] for p in qkv_z] + [lines, jnp.zeros_like(lines)]
    qkv_parts = gather_chips(jnp.concatenate(whole, 0).reshape(2, span + 16, 3 * half_width))

    tied_inputs = tie(inputs, qkv_z[2])
    pieces = bring(lambda s: pick(tied_inputs, s, 0)[0])

    if direct:
        cut = chunks * span + span // 2
        near, pieces[0], *qkv_parts = join(wide_z[1], pieces[0], *qkv_parts)
        whole = pack_rows(at, wide_z[0], near, wide_z[2], chunks + 1, cut)
    else:
        wide_z = in_seq_order(*wide_z)
        rows_a = (chunks + 1) * rows_in
        rows = []
        for c in range(chunks + 1):
            rows += [p[c * rows_in : (c + 1) * rows_in] for p in wide_z]
        rows += [p[rows_a : rows_a + rows_ff] for p in wide_z]
        rows.append(sum(p[rows_a + rows_ff :].astype(WIDE) for p in wide_z).astype(LOW))
        whole = jnp.concatenate(rows, 0)
    if direct:
        parts = gather_quads(*whole)
        joined_up = join(*parts, *pieces)
        parts, pieces = joined_up[:4], joined_up[4:]
    else:
        parts = gather_chips(tie(whole, qkv_parts))
    lines = sum(jnp.sum(p[:, span].astype(WIDE), 0, keepdims=True) for p in qkv_parts)
    pieces = [*pieces, *(swap(p) for p in pieces)]
    rows_a, rows_b = (chunks + 1) * span, (chunks + 1) * span + span_ff
    if direct:
        qkv_weights = tuple(qkv_parts)
    else:
        ordered = in_chip_order(qkv_parts)
        qkv_weights = (jnp.concatenate([p[k, :span] for p in ordered for k in range(2)], 0),)

    if direct:
        parts = finish_quads(*parts)
    qkv_first, qkv_rest, tokens, w_qkv = project_tokens(at, pieces, lines, qkv_weights, direct)
    mixed_first, log_first = attend(0, sides, rand, glob_at, bias, qkv_first)
    tied_cotangent = tie(cotangent, *pieces)
    grad_result = bring(lambda s: pick(tied_cotangent, s, 0)[0])
    mixed_first, qkv_rest, *parts = join(mixed_first, qkv_rest, *parts)
    other_first = swap(mixed_first[own:])
    other_parts = [swap(p) for p in parts]
    mixed_rest, log_rest = attend(1, sides, rand, glob_at, bias, qkv_rest)
    if direct:
        weights = tuple(parts + other_parts)
    else:
        weights = (
            jnp.stack(
                [
                    in_device_order(
                        *([p[span * c : span * c + span] for p in ps] for ps in (parts, other_parts))
                    )
                    for c in range(chunks + 1)
                ]
            ),
            in_device_order(*([p[rows_a:rows_b] for p in ps] for ps in (parts, other_parts))),
            sum(p[rows_b:].astype(WIDE) for p in parts + other_parts).astype(LOW)[None],
        )
    other = other_first, swap(mixed_rest[own:])
    result, slope, normed, unit_one, grad_second, scale, grad_down, down_sums = layer_forward(
        at, (mixed_first, mixed_rest), other, tokens, grad_result, weights, direct, chunks
    )
    output = send_back(result)

    grad_down = lax.psum_scatter(grad_down, "dp", scatter_dimension=0, tiled=True)
    *backward, grad_in, in_sums = layer_backward(
        at,
        (mixed_first, mixed_rest),
        other,
        slope,
        unit_one,
        grad_second,
        scale,
        normed,
        weights,
        direct,
    )
    grad_first, mine, theirs, grad_in, in_sums, *output = join(*backward, grad_in, in_sums, *output)
    grad_in = lax.psum_scatter(grad_in, "dp", scatter_dimension=1, tiled=True)

    come = swap(theirs)
    grad_qkv, grad_own, grad_theirs, sums = attend_back(
        sides,
        rand,
        glob_at,
        bias,
        (log_first, log_rest),
        (qkv_first, qkv_rest),
        mine,
        come,
        w_qkv,
        grad_first,
    )
    come = swap(grad_theirs)
    grad_w_qkv = dot(tokens, grad_qkv, TN).astype(LOW)
    grad_w_qkv, grad_own, come = join(grad_w_qkv, grad_own, come)
    grad_inputs = start_back(added(grad_own, come))
    vectors = (down_sums + in_sums)[: 6 + chunks].reshape(-1)
    vectors = jnp.pad(vectors, (0, -vectors.shape[0] % (3 * half_width))).reshape(-1, 3 * half_width)
    lines = jnp.concatenate([sums, vectors], 0).astype(LOW)
    lines = jnp.broadcast_to(lines, (chips, 2, n_seq) + lines.shape)
    parts = jnp.concatenate(
        [grad_w_qkv.reshape(chips, 2, n_seq, rows_in, 3 * half_width), lines], 3
    )
    come = swap(pick(parts, 1 - core, 1)[:, 0])
    first_back = finish_back(grad_inputs, 0)
    come, first_back = join(come, first_back)
    near_sums, keep_sums = unpack_rows(at, grad_in, grad_down)
    near_sums = flip_seq(near_sums, 1)
    parts = jnp.stack([pick(parts, core, 1)[:, 0], come], 1)
    grad_inputs, parts = tie((grad_inputs, parts), first_back)
    grad_inputs = first_back, finish_back(grad_inputs, 1)
    parts = reduce_chips(parts)
    parts, near_sums = join(parts, near_sums)
    own_qkv = reduce_seq(parts.transpose(1, 0, 2, 3))
    keep, come = own_qkv[0], own_qkv[1]
    left, right = jnp.where(core == 0, keep, come), jnp.where(core == 0, come, keep)

    mirror = flip_seq(added(keep_sums[1], near_sums[1]), 3)
    own_sums = sum(p.astype(WIDE) for p in (keep_sums[0], near_sums[0], mirror))
    rows_a = (chunks + 1) * rows_in
    own_up = jnp.concatenate(
        [own_sums[c * rows_in : (c + 1) * rows_in] for c in range(chunks)], 1
    )
    small = (keep + come)[rows_in + 1 :].reshape(-1)[: (6 + chunks) * width].reshape(-1, width)

    def joined(k, rows):
        lanes = [lanes_of(k, pair) for pair in range(pairs)]
        return jnp.concatenate([one[rows, at] for one in (left, right) for at in lanes], 1)

    def own_part(vector, size):
        return lax.dynamic_slice_in_dim(vector.reshape(-1), device * size, size, 0)

    matrix_rows, line = slice(0, rows_in), slice(rows_in, rows_in + 1)
    return (
        in_sequences(output),
        in_sequences(grad_inputs),
        joined(0, matrix_rows),
        own_part(joined(0, line), rows_in),
        joined(1, matrix_rows),
        joined(2, matrix_rows),
        own_part(joined(2, line), rows_in),
        own_sums[chunks * rows_in : rows_a],
        own_part(small[0], rows_in),
        own_part(small[1], rows_in),
        own_part(small[2], rows_in),
        own_up,
        own_part(small[6 : 6 + chunks], rows_ff),
        own_sums[rows_a : rows_a + rows_ff],
        own_part(small[3], rows_in),
        own_part(small[4], rows_in),
        own_part(small[5], rows_in),
    )


def solution(mesh):
    both = ("dp", "seq")
    matrix, vector = P(both, None), P(both)
    tokens = P("dp", "seq", None)
    return jax.shard_map(
        shards,
        mesh=mesh,
        in_specs=(tokens, tokens, P("dp", None, "seq", None), P("dp", None))
        + (matrix, vector, matrix, matrix, vector, matrix, vector, vector, vector)
        + (matrix, vector, matrix, vector, vector, vector),
        out_specs=(tokens, tokens)
        + (matrix, vector, matrix, matrix, vector, matrix, vector, vector, vector)
        + (matrix, vector, matrix, vector, vector, vector),
        check_vma=False,
    )
```

```python
from functools import partial

import jax
import jax.numpy as jnp
from jax import lax
from jax.experimental import pallas as pl
from jax.experimental.pallas import tpu as pltpu
from jax.sharding import PartitionSpec as P

HEADS = 12
HEAD = 64
BLOCK = 64
SLOTS = 8
EPS = 1e-06
NEG = -1e30
LOW = jnp.bfloat16
WIDE = jnp.float32

NT = (((1,), (1,)), ((), ()))
TN = (((0,), (0,)), ((), ()))
NN = (((1,), (0,)), ((), ()))


def dot(left, right, dims):
    return lax.dot_general(left, right, dims, preferred_element_type=WIDE)


def swap(array):
    size = lax.axis_size("dp")
    return lax.ppermute(array, "dp", [(i, i ^ 1) for i in range(size)])


def flip_seq(array, k):
    size = lax.axis_size("seq")
    return lax.ppermute(array, "seq", [(i, i ^ k) for i in range(size)])


def rounds():
    dp, seq = lax.axis_size("dp"), lax.axis_size("seq")
    for a in range(2):
        pairs = []
        for d in range(dp):
            for z in range(seq):
                to_dp = (d & ~1) | (z >> 1)
                to_seq = 2 * (d & 1) + (a ^ (z & 1))
                pairs.append((d * seq + z, to_dp * seq + to_seq))
        yield a, pairs


def bring_round(piece_of, which):
    a, pairs = list(rounds())[which]
    z = lax.axis_index("seq")
    return lax.ppermute(piece_of(a ^ (z & 1)), ("dp", "seq"), pairs)


def bring(piece_of):
    return [bring_round(piece_of, which) for which in range(2)]


def start_back(rows):
    size = rows.shape[0] // 2
    return [rows[size * a : size * a + size] for a in range(2)]


def finish_back(parts, which):
    a, pairs = list(rounds())[which]
    return lax.ppermute(parts[a], ("dp", "seq"), [(t, s) for s, t in pairs])


def send_back(rows):
    parts = start_back(rows)
    return [finish_back(parts, a) for a in range(2)]


def in_sequences(got):
    odd = (lax.axis_index("seq") & 1) == 1
    return jnp.stack([jnp.where(odd, got[1], got[0]), jnp.where(odd, got[0], got[1])])


def pick(array, index, axis):
    return lax.dynamic_slice_in_dim(array, index, 1, axis)


def gather_seq(shard, before=None):
    mirror = flip_seq(shard, 3)
    pair = jnp.stack([shard, mirror])
    if before is not None:
        pair = tie(pair, before)
    return shard, flip_seq(pair, 1), mirror


def in_seq_order(shard, near, mirror):
    z = lax.axis_index("seq")
    pieces = [shard, near[0], near[1], mirror]
    for bit in range(2):
        set_bit = ((z >> bit) & 1) == 1
        pieces = [
            jnp.where(set_bit, pieces[i ^ (1 << bit)], pieces[i]) for i in range(len(pieces))
        ]
    return pieces


def chip_groups():
    count = (lax.axis_size("dp") // 2).bit_length() - 1
    return [(bit, min(2, count - bit)) for bit in range(0, count, 2)]


def flip_chip(array, away):
    size = lax.axis_size("dp")
    return lax.ppermute(array, "dp", [(i, i ^ (2 * away)) for i in range(size)])


def gather_chips(part):
    parts = [part]
    for bit, bits in chip_groups():
        parts = parts + [flip_chip(p, k << bit) for k in range(1, 1 << bits) for p in parts]
    return parts


def in_chip_order(parts):
    chip = lax.axis_index("dp") >> 1
    parts = jnp.stack(parts)
    return [pick(parts, q ^ chip, 0)[0] for q in range(parts.shape[0])]


def in_device_order(mine, theirs):
    core = lax.axis_index("dp") & 1
    parts = []
    for own, other in zip(in_chip_order(mine), in_chip_order(theirs)):
        parts += [jnp.where(core == 0, own, other), jnp.where(core == 0, other, own)]
    return jnp.concatenate(parts, 0)


def join(*values):
    return lax.optimization_barrier(values)


def gather_quads(upper, lower):
    return [upper, flip_chip(upper, 1), lower, flip_chip(lower, 2)]


def tie(values, *others):
    return lax.optimization_barrier((values, others))[0]


def added(*arrays):
    return sum(array.astype(WIDE) for array in arrays).astype(LOW)


def reduce_chips(parts):
    chip = lax.axis_index("dp") >> 1
    for bit, bits in chip_groups():
        ways = 1 << bits
        parts = parts.reshape((-1, ways) + parts.shape[1:])
        mine = (chip >> bit) & (ways - 1)
        others = [flip_chip(pick(parts, mine ^ k, 1)[:, 0], k << bit) for k in range(1, ways)]
        parts = added(pick(parts, mine, 1)[:, 0], *others)
    return parts[0]


def reduce_seq(parts):
    z = lax.axis_index("seq")
    near = flip_seq(jnp.concatenate([pick(parts, z ^ 1, 0), pick(parts, z ^ 2, 0)], 0), 1)
    mirror = added(pick(parts, z ^ 3, 0)[0], near[1])
    return pick(parts, z, 0)[0].astype(WIDE) + near[0].astype(WIDE) + flip_seq(mirror, 3).astype(WIDE)


def norm_parts(summed):
    center = summed - jnp.mean(summed, -1, keepdims=True)
    spread = jnp.mean(center * center, -1, keepdims=True)
    scale = lax.rsqrt(spread + EPS)
    return center * scale, scale


def norm_back(grad, unit, scale, gain):
    grad_unit = grad * gain
    mean_one = jnp.mean(grad_unit, -1, keepdims=True)
    mean_two = jnp.mean(grad_unit * unit, -1, keepdims=True)
    return scale * (grad_unit - mean_one - unit * mean_two)


def gelu_parts(x):
    size = jnp.abs(x)
    t = 1.0 / (1.0 + (0.3275911 * 0.5**0.5) * size)
    bell = jnp.exp(-0.5 * x * x)
    series = 0.5 * 1.061405429
    for factor in (-1.453152027, 1.421413741, -0.284496736, 0.254829592):
        series = series * t + 0.5 * factor
    tail = series * t * bell
    share = jnp.where(x >= 0, 1.0 - tail, tail)
    return x * share, share + x * bell * 0.3989422804014327


def block_rows(ref, block, lanes):
    return ref[pl.ds(pl.multiple_of(block * BLOCK, BLOCK), BLOCK), lanes]


def diagonal(pair_rows, low):
    zero = jnp.zeros_like(pair_rows)
    return jnp.concatenate(
        [jnp.where(low, pair_rows, zero), jnp.where(low, zero, pair_rows)], axis=0
    )


def gather_blocks(ref, ids, lanes, low):
    parts = []
    for one, two in ids:
        if two is None:
            parts.append(block_rows(ref, one, lanes))
        else:
            parts.append(
                jnp.where(low, block_rows(ref, one, lanes), block_rows(ref, two, lanes))
            )
    return jnp.concatenate(parts, axis=0)


def slot_ids(near_ref, rand_ref, globs, i, head, blocks):
    ids = [(near_ref[i], None), (i, None), (near_ref[blocks + i], None)]
    ids += [(globs[0], None), (globs[1], None)]
    for r in range(3):
        ids.append(
            (
                rand_ref[(head * blocks + i) * 3 + r],
                rand_ref[((head + 1) * blocks + i) * 3 + r],
            )
        )
    return ids


def lanes_of(part, pair):
    first = 128 * (3 * pair + part)
    return slice(first, first + 128)


def flat_lanes(pair):
    return slice(128 * pair, 128 * pair + 128)


def start_copies(copies, sems):
    started = [
        pltpu.make_async_copy(source, target, sems.at[k])
        for k, (source, target) in enumerate(copies)
    ]
    for copy in started:
        copy.start()
    return started


def project_kernel(chips, direct, at_ref, *refs):
    pieces, b_ref = refs[:4], refs[4]
    sources, (qkv_ref, tokens_ref, w_ref, sems) = refs[5:-4], refs[-4:]
    if direct:
        span = w_ref.shape[0] // (2 * chips)
        copies = [
            (
                sources[away].at[k, :span],
                w_ref.at[pl.ds(pl.multiple_of((2 * (at_ref[0] ^ away) + k) * span, span), span)],
            )
            for away in range(chips)
            for k in range(2)
        ]
    else:
        copies = [(sources[0], w_ref)]

    @pl.when(pl.program_id(0) == 0)
    def _():
        for copy in start_copies(copies, sems):
            copy.wait()

    lane = lax.broadcasted_iota(jnp.int32, (1, w_ref.shape[1]), 1)
    scale = jnp.where(lane % 384 < 128, HEAD ** (-0.5), 1.0)
    at = pl.program_id(0) * len(pieces) // pl.num_programs(0)
    rows = pieces[0][...]
    for k in range(1, len(pieces)):
        rows = jnp.where(at == k, pieces[k][...], rows)
    tokens_ref[...] = rows
    values = (dot(rows, w_ref[...], NN) + b_ref[...]).astype(LOW).astype(WIDE)
    qkv_ref[...] = (values * scale).astype(LOW)


def with_sems(groups, sems):
    done, copies = 0, []
    for group in groups:
        copies.append([pltpu.make_async_copy(*pair, sems.at[done + k]) for k, pair in enumerate(group)])
        done += len(group)
    return copies


def attend_kernel(
    pairs, blocks, step, near_ref, rand_ref, glob_ref, bias_ref, qkv_ref, out_ref, log_ref
):
    low = lax.broadcasted_iota(jnp.int32, (1, 2 * HEAD), 1) < HEAD
    globs = (glob_ref[0], glob_ref[1])

    def scores_of(i, pair):
        ids = slot_ids(near_ref, rand_ref, globs, i, 2 * pair, blocks)
        queries = diagonal(block_rows(qkv_ref, i, lanes_of(0, pair)), low)
        return dot(gather_blocks(qkv_ref, ids, lanes_of(1, pair), low), queries, NT)

    def softmax_of(i, pair, scores):
        highest = jnp.max(scores, axis=0, keepdims=True)
        weights = jnp.exp(scores - highest)
        total = jnp.sum(weights, axis=0, keepdims=True)
        log_ref[i, pair : pair + 1] = highest + jnp.log(total)
        return (weights * (1.0 / total)).astype(LOW)

    def put(i, pair, mixed):
        at = pl.ds(pl.multiple_of(i * BLOCK, BLOCK), BLOCK)
        out_ref[at, flat_lanes(pair)] = jnp.where(low, mixed[:BLOCK], mixed[BLOCK:]).astype(LOW)

    def body(at, carry):
        units = [(at * step + d, pair) for d in range(step) for pair in range(pairs)]
        scores = [scores_of(*unit) for unit in units]
        probs = []
        for (i, pair), score in zip(units, scores):
            bias = bias_ref[i, pair]
            score = jnp.concatenate(
                [score[BLOCK * j : BLOCK * j + BLOCK] + bias[j : j + 1] for j in range(SLOTS)],
                axis=0,
            )
            probs.append(softmax_of(i, pair, score))
        for (i, pair), prob in zip(units, probs):
            ids = slot_ids(near_ref, rand_ref, globs, i, 2 * pair, blocks)
            values = gather_blocks(qkv_ref, ids, lanes_of(2, pair), low)
            put(i, pair, dot(prob, values, TN))
        return carry

    lax.fori_loop(0, blocks // step, body, 0)

    def whole_row(n, carry):
        i = glob_ref[n]
        scores = []
        for pair in range(pairs):
            queries = diagonal(block_rows(qkv_ref, i, lanes_of(0, pair)), low)
            scores.append(dot(qkv_ref[:, lanes_of(1, pair)], queries, NT))
        probs = [softmax_of(i, pair, scores[pair]) for pair in range(pairs)]
        for pair in range(pairs):
            put(i, pair, dot(probs[pair], qkv_ref[:, lanes_of(2, pair)], TN))
        return carry

    lax.fori_loop(0, 2, whole_row, 0)


def attend_back_kernel(
    blocks,
    step,
    near_ref,
    rand_ref,
    glob_ref,
    bias_ref,
    log_ref,
    qkv_ref,
    mine_ref,
    come_ref,
    w_ref,
    grad_first_ref,
    out_ref,
    rows_own_ref,
    rows_other_ref,
    sums_ref,
    grad_ref,
    acc_ref,
):
    low = lax.broadcasted_iota(jnp.int32, (1, 2 * HEAD), 1) < HEAD
    globs = (glob_ref[0], glob_ref[1])
    acc_ref[...] = jnp.zeros_like(acc_ref)
    half = mine_ref.shape[0]
    grad_ref[:half] = mine_ref[...]
    grad_ref[half:] = come_ref[...]
    pairs = mine_ref.shape[1] // 128

    def source(pair, part):
        return qkv_ref.at[:, lanes_of(part, pair)]

    def log_of(i, pair):
        return log_ref[i, pair : pair + 1]

    every = slice(None)

    def add(part, pair, block, value):
        at = pl.ds(pl.multiple_of(block * BLOCK, BLOCK), BLOCK)
        lanes = flat_lanes(2 * pair + part)
        acc_ref[at, lanes] = acc_ref[at, lanes] + value

    def operands(i, pair):
        queries = diagonal(block_rows(source(pair, 0), i, every), low)
        grads = diagonal(block_rows(grad_ref, i, flat_lanes(pair)), low)
        return queries, grads

    def softmax_back(prob, grad_prob):
        scaled = prob * grad_prob
        inner = jnp.sum(scaled, axis=0, keepdims=True)
        return prob.astype(LOW), (scaled - prob * inner).astype(LOW)

    def put(i, pair, mixed):
        at = pl.ds(pl.multiple_of(i * BLOCK, BLOCK), BLOCK)
        out_ref[at, lanes_of(0, pair)] = (
            jnp.where(low, mixed[:BLOCK], mixed[BLOCK:]) * HEAD ** (-0.5)
        ).astype(LOW)

    def body(at, carry):
        units = [(at * step + d, pair) for d in range(step) for pair in range(pairs)]
        first = []
        for i, pair in units:
            ids = slot_ids(near_ref, rand_ref, globs, i, 2 * pair, blocks)
            queries, grads = operands(i, pair)
            first.append(
                (
                    dot(gather_blocks(source(pair, 1), ids, every, low), queries, NT),
                    dot(gather_blocks(source(pair, 2), ids, every, low), grads, NT),
                )
            )
        second = []
        for (i, pair), (score, grad_prob) in zip(units, first):
            shift = bias_ref[i, pair] - log_of(i, pair)
            prob = jnp.concatenate(
                [
                    jnp.exp(score[BLOCK * j : BLOCK * j + BLOCK] + shift[j : j + 1])
                    for j in range(SLOTS)
                ],
                axis=0,
            )
            second.append(softmax_back(prob, grad_prob))
        third = []
        for (i, pair), (prob, grad_score) in zip(units, second):
            ids = slot_ids(near_ref, rand_ref, globs, i, 2 * pair, blocks)
            queries, grads = operands(i, pair)
            keys = gather_blocks(source(pair, 1), ids, every, low)
            put(i, pair, dot(grad_score, keys, TN))
            third.append((dot(grad_score, queries, NN), dot(prob, grads, NN)))
        for (i, pair), values in zip(units, third):
            ids = slot_ids(near_ref, rand_ref, globs, i, 2 * pair, blocks)
            for j, (one, two) in enumerate(ids):
                for part, value in enumerate(values):
                    value = value[BLOCK * j : BLOCK * j + BLOCK]
                    if two is None:
                        add(part, pair, one, value)
                    else:
                        add(part, pair, one, jnp.where(low, value, 0.0))
                        add(part, pair, two, jnp.where(low, 0.0, value))
        return carry

    lax.fori_loop(0, blocks // step, body, 0)

    def whole_row(n, carry):
        i = glob_ref[n]
        first = []
        for pair in range(pairs):
            queries, grads = operands(i, pair)
            first.append(
                (
                    dot(source(pair, 1)[...], queries, NT),
                    dot(source(pair, 2)[...], grads, NT),
                )
            )
        second = []
        for pair, (score, grad_prob) in enumerate(first):
            prob = jnp.exp(score - log_of(i, pair))
            second.append(softmax_back(prob, grad_prob))
        for pair, (prob, grad_score) in enumerate(second):
            queries, grads = operands(i, pair)
            acc_ref[:, flat_lanes(2 * pair)] += dot(grad_score, queries, NN)
            acc_ref[:, flat_lanes(2 * pair + 1)] += dot(prob, grads, NN)
            put(i, pair, dot(grad_score, source(pair, 1)[...], TN))
        return carry

    lax.fori_loop(0, jnp.where(globs[0] == globs[1], 1, 2), whole_row, 0)
    for pair in range(pairs):
        out_ref[:, 384 * pair + 128 : 384 * pair + 384] = acc_ref[
            :, 256 * pair : 256 * pair + 256
        ].astype(LOW)

    sums_ref[...] = jnp.zeros_like(sums_ref)
    tile = 512
    for side, rows_ref in enumerate((rows_own_ref, rows_other_ref)):

        def token_rows(at, carry, side=side, rows_ref=rows_ref):
            grads = out_ref[pl.ds(pl.multiple_of(side * half + at * tile, tile), tile)]
            sums_ref[...] += jnp.sum(grads.astype(WIDE), 0, keepdims=True)
            rows = pl.ds(pl.multiple_of(at * tile, tile), tile)
            total = dot(grads, w_ref[...], NT)
            if side == 0:
                total = total + grad_first_ref[rows].astype(WIDE)
            rows_ref[rows] = total.astype(LOW)
            return carry

        lax.fori_loop(0, half // tile, token_rows, 0)


def pack_kernel(seq, chunks, cut, at_ref, shard_ref, near_ref, mirror_ref, upper_ref, lower_ref):
    rows = shard_ref.shape[0] - 16
    rows_in = rows // (chunks + 4)
    rows_ff = rows - chunks * rows_in
    pieces = [shard_ref, near_ref.at[0], near_ref.at[1], mirror_ref]
    total = sum(piece[rows:].astype(WIDE) for piece in pieces)

    def put(first, value):
        target, first = (upper_ref, first) if first < cut else (lower_ref, first - cut)
        target[first : first + value.shape[0]] = value

    put(rows * seq, total.astype(LOW))
    for z in range(seq):

        @pl.when(at_ref[2] == z)
        def _(z=z):
            for k, piece in enumerate(pieces):
                for c in range(chunks):
                    put((c * seq + (z ^ k)) * rows_in, piece[c * rows_in : c * rows_in + rows_in])
                put(chunks * seq * rows_in + (z ^ k) * rows_ff, piece[chunks * rows_in : rows])


def pack_columns_kernel(seq, rows_in, at_ref, shard_ref, near_ref, mirror_ref, out_ref):
    pieces = [shard_ref, near_ref.at[0], near_ref.at[1], mirror_ref]
    total = sum(piece[:, rows_in:].astype(WIDE) for piece in pieces).astype(LOW)
    out_ref[:, seq * rows_in :] = jnp.concatenate([total, jnp.zeros_like(total)], 1)
    for z in range(seq):

        @pl.when(at_ref[2] == z)
        def _(z=z):
            for k, piece in enumerate(pieces):
                first = (z ^ k) * rows_in
                out_ref[:, first : first + rows_in] = piece[:, :rows_in]


def unpack_kernel(seq, chunks, many, at_ref, *refs):
    sources, (near_ref, keep_ref) = refs[:-2], refs[-2:]
    rows = near_ref.shape[1]
    rows_in = rows // (chunks + 4)
    rows_ff = rows - chunks * rows_in

    cut = sources[0].shape[0]

    def total(first, size):
        refs, first = (sources[:many], first) if first < cut else (sources[many:], first - cut)
        return sum(ref[first : first + size].astype(WIDE) for ref in refs).astype(LOW)

    for z in range(seq):

        @pl.when(at_ref[2] == z)
        def _(z=z):
            for k in range(seq):
                target = (keep_ref, near_ref)[k in (1, 2)].at[int(k > 1)]
                for c in range(chunks):
                    part = total((c * seq + (z ^ k)) * rows_in, rows_in)
                    target[c * rows_in : c * rows_in + rows_in] = part
                target[chunks * rows_in :] = total(chunks * seq * rows_in + (z ^ k) * rows_ff, rows_ff)


def weight_copies(chips, direct, chip, core, sources, w_in_ref, w_down_ref, lines_ref):
    if not direct:
        return [(sources[0], w_in_ref), (sources[2], lines_ref)], [], [(sources[1], w_down_ref)]
    wide, width = w_down_ref.shape
    chunks = wide // width
    span, span_ff = width // (2 * chips), wide // (2 * chips)
    cut = span // 2
    groups = [], [], []
    for k in range(2):
        for away in range(chips):
            place = 2 * (chip ^ away) + (core if k == 0 else 1 - core)
            upper = sources[4 * k + (away >> 1)].at[away & 1]
            lower = sources[4 * k + 2 + (away & 1)].at[away >> 1]
            rows = pl.ds(pl.multiple_of(place * span, span), span)
            groups[1].extend(
                (upper.at[span * c : span * c + span], w_in_ref.at[c, rows]) for c in range(chunks)
            )
            for half, source in enumerate((upper.at[span * chunks :], lower.at[:cut])):
                rows = pl.ds(pl.multiple_of(place * span + half * cut, cut), cut)
                groups[0].append((source, w_in_ref.at[chunks, rows]))
            rows = pl.ds(pl.multiple_of(place * span_ff, span_ff), span_ff)
            groups[2].append((lower.at[cut : cut + span_ff], w_down_ref.at[rows]))
            groups[0].append((lower.at[cut + span_ff :], lines_ref.at[k * chips + away]))
    return groups


def forward_kernel(
    chips,
    direct,
    at_ref,
    mixed_ref,
    other_ref,
    tokens_ref,
    *refs,
):
    sources, refs = refs[:-11], refs[-11:]
    output_ref, hidden_ref, slope_ref, normed_ref, unit_one_ref, unit_two_ref, scales_ref = refs[:7]
    w_in_ref, w_down_ref, lines_ref, sems = refs[7:]
    wide, width = w_down_ref.shape
    half, chunks = width // 2, wide // width
    core = at_ref[1]
    groups = weight_copies(chips, direct, at_ref[0], core, sources, w_in_ref, w_down_ref, lines_ref)
    groups = with_sems(groups, sems)

    @pl.when(pl.program_id(0) == 0)
    def _():
        for copy in sum(groups, []):
            copy.start()
        for copy in groups[0]:
            copy.wait()

    vectors = jnp.sum(lines_ref[...].astype(WIDE), 0)
    b_out, gain_one, shift_one, b_down, gain_two, shift_two = (vectors[k : k + 1] for k in range(6))
    here = pl.ds(pl.multiple_of(core * half, 128), half)
    there = pl.ds(pl.multiple_of((1 - core) * half, 128), half)
    branch = dot(mixed_ref[...], w_in_ref[chunks, here], NN) + dot(other_ref[...], w_in_ref[chunks, there], NN)
    unit_one, scale_one = norm_parts(tokens_ref[...].astype(WIDE) + (branch + b_out))
    normed = unit_one * gain_one + shift_one
    normed_low = normed.astype(LOW)
    normed_ref[...] = normed_low
    unit_one_ref[...] = unit_one

    @pl.when(pl.program_id(0) == 0)
    def _():
        for copy in groups[1] + groups[2]:
            copy.wait()

    down = b_down
    for c in range(0, chunks, 2):
        lanes = slice(width * c, width * c + 2 * width)
        weights = jnp.concatenate([w_in_ref[c], w_in_ref[c + 1]], 1)
        bias = jnp.concatenate([vectors[6 + c : 7 + c], vectors[7 + c : 8 + c]], 1)
        hidden, slope = gelu_parts(dot(normed_low, weights, NN) + bias)
        hidden = hidden.astype(LOW)
        hidden_ref[:, lanes] = hidden
        slope_ref[:, lanes] = slope.astype(LOW)
        down = down + dot(hidden, w_down_ref[lanes], NN)
    unit_two, scale_two = norm_parts(normed + down)
    output_ref[...] = (unit_two * gain_two + shift_two).astype(LOW)
    lane = lax.broadcasted_iota(jnp.int32, (1, 128), 1)
    scales_ref[...] = jnp.where(lane < 64, scale_one, scale_two)
    unit_two_ref[...] = unit_two


def backward_kernel(
    tile,
    chips,
    direct,
    at_ref,
    mixed_ref,
    other_ref,
    grad_first_ref,
    grad_last_ref,
    slope_ref,
    unit_one_ref,
    unit_two_ref,
    scales_ref,
    hidden_hbm,
    normed_hbm,
    *refs,
):
    sources, refs = refs[:-18], refs[-18:]
    first_ref, mine_ref, theirs_ref, sums_ref, *grad_refs = refs[:6]
    w_in_ref, w_down_ref, lines_ref, vectors_ref, pre_ref, branch_ref = refs[6:12]
    normed_ref, hidden_ref, down_ref, sems, extra_sems, out_sems = refs[12:]
    own, width = normed_ref.shape
    wide = w_down_ref.shape[0]
    half, chunks = width // 2, wide // width
    chip, core = at_ref[0], at_ref[1]
    at, last = pl.program_id(0), pl.num_programs(0) - 1
    rows = pl.ds(pl.multiple_of(at * tile, tile), tile)
    groups = weight_copies(chips, direct, chip, core, sources, w_in_ref, w_down_ref, lines_ref)
    groups = with_sems(groups, sems)
    extra = [
        pltpu.make_async_copy(hidden_hbm, hidden_ref, extra_sems.at[0]),
        pltpu.make_async_copy(normed_hbm, normed_ref, extra_sems.at[1]),
    ]
    here = pl.ds(pl.multiple_of(core * half, 128), half)
    there = pl.ds(pl.multiple_of((1 - core) * half, 128), half)

    @pl.when(at == 0)
    def _():
        for copy in groups[2] + groups[1] + groups[0]:
            copy.start()
        for copy in extra:
            copy.start()
        sums_ref[...] = jnp.zeros_like(sums_ref)
        for copy in groups[2] + groups[1] + groups[0]:
            copy.wait()
        vectors_ref[...] = jnp.sum(lines_ref[...].astype(WIDE), 0)

    def add_sum(k, value):
        sums_ref[k : k + 1] += jnp.sum(value, 0, keepdims=True)

    grad = jnp.where(2 * at <= last, grad_first_ref[...], grad_last_ref[...]).astype(WIDE)
    unit_two = unit_two_ref[...]
    add_sum(4, grad * unit_two)
    add_sum(5, grad)
    grad_normed = norm_back(grad, unit_two, scales_ref[:, 64:65], vectors_ref[4:5])
    grad_down = grad_normed.astype(LOW)
    down_ref[rows] = grad_down
    add_sum(3, grad_down.astype(WIDE))
    for c in range(chunks):
        lanes = slice(width * c, width * c + width)
        grad_pre = dot(grad_down, w_down_ref[lanes], NT) * slope_ref[:, lanes].astype(WIDE)
        grad_pre = grad_pre.astype(LOW)
        pre_ref[rows, lanes] = grad_pre
        add_sum(6 + c, grad_pre.astype(WIDE))
        grad_normed = grad_normed + dot(grad_pre, w_in_ref[c], NT)
    unit_one = unit_one_ref[...]
    add_sum(1, grad_normed * unit_one)
    add_sum(2, grad_normed)
    grad_branch = norm_back(grad_normed, unit_one, scales_ref[:, 0:1], vectors_ref[1:2]).astype(LOW)
    first_ref[...] = grad_branch
    branch_ref[rows] = grad_branch
    add_sum(0, grad_branch.astype(WIDE))
    mine_ref[...] = dot(grad_branch, w_in_ref[chunks, here], NT).astype(LOW)
    theirs_ref[...] = dot(grad_branch, w_in_ref[chunks, there], NT).astype(LOW)

    @pl.when(at == last)
    def _():
        for copy in extra:
            copy.wait()
        moving = []
        span, span_ff = width // (2 * chips), wide // (2 * chips)
        first = span * (chunks + 1)

        def leave(pairs):
            for source, target in pairs:
                copy = pltpu.make_async_copy(source, target, out_sems.at[len(moving)])
                copy.start()
                moving.append(copy)

        def leave_rows(c):
            if not direct:
                return leave([(w_in_ref.at[c], grad_refs[0].at[c])])
            for k, target in enumerate(grad_refs):
                for q in range(chips):
                    place = 2 * q + (core if k == 0 else 1 - core)
                    source = w_in_ref.at[c, pl.ds(pl.multiple_of(place * span, span), span)]
                    leave([(source, target.at[q, span * c : span * c + span])])

        for c in range(chunks):
            lanes = slice(width * c, width * c + width)
            w_down_ref[lanes] = dot(hidden_ref[:, lanes], down_ref[...], TN).astype(LOW)
            if direct:
                for k, target in enumerate(grad_refs):
                    place = 2 * c + (core if k == 0 else 1 - core)
                    source = w_down_ref.at[pl.ds(pl.multiple_of(place * span_ff, span_ff), span_ff)]
                    leave([(source, target.at[c, first : first + span_ff])])
            else:
                leave([(w_down_ref.at[lanes], grad_refs[1].at[lanes])])
            w_in_ref[c] = dot(normed_ref[...], pre_ref[:, lanes], TN).astype(LOW)
            leave_rows(c)
        w_in_ref[chunks, here] = dot(mixed_ref[...], branch_ref[...], TN).astype(LOW)
        w_in_ref[chunks, there] = dot(other_ref[...], branch_ref[...], TN).astype(LOW)
        leave_rows(chunks)
        for copy in moving:
            copy.wait()


IN_SMEM = pl.BlockSpec(memory_space=pltpu.SMEM)
IN_VMEM = pl.BlockSpec(memory_space=pltpu.VMEM)


IN_ANY = pl.BlockSpec(memory_space=pl.ANY)


TILE = 256


def tiles(width, first=0, many=None):
    if many is None:
        return pl.BlockSpec((TILE, width), lambda i: (i, 0))
    return pl.BlockSpec((TILE, width), lambda i: (jnp.clip(i - first, 0, many - 1), 0))


def project_tokens(at, pieces, b_qkv, weights, direct):
    length, width = 4 * pieces[0].shape[0], pieces[0].shape[1]
    half = width // 2
    chips = lax.axis_size("dp") // 2
    many = pieces[0].shape[0] // TILE

    def all_of(*shape):
        return pl.BlockSpec(shape, lambda i: (0, 0))

    return pl.pallas_call(
        partial(project_kernel, chips, direct),
        grid=(length // TILE,),
        out_shape=(
            jax.ShapeDtypeStruct((length, 3 * half), LOW),
            jax.ShapeDtypeStruct((length, width), LOW),
            jax.ShapeDtypeStruct((width, 3 * half), LOW),
        ),
        in_specs=[IN_SMEM]
        + [tiles(width, many * k, many) for k in range(4)]
        + [all_of(1, 3 * half)]
        + [IN_ANY] * len(weights),
        out_specs=(tiles(3 * half), tiles(width), all_of(width, 3 * half)),
        scratch_shapes=[pltpu.SemaphoreType.DMA((2 * chips,))],
        compiler_params=pltpu.CompilerParams(vmem_limit_bytes=48 << 20),
        cost_estimate=pl.CostEstimate(flops=1, bytes_accessed=1, transcendentals=0),
        name="project",
    )(at, *pieces, b_qkv, *weights)


def attend(near, rand, globs, bias, qkv):
    length, width = qkv.shape
    pairs, blocks = width // 384, length // BLOCK
    return pl.pallas_call(
        partial(attend_kernel, pairs, blocks, 4),
        out_shape=(
            jax.ShapeDtypeStruct((length, 128 * pairs), LOW),
            jax.ShapeDtypeStruct((blocks, 8, 128), WIDE),
        ),
        in_specs=[IN_SMEM] * 3 + [IN_VMEM] * 2,
        out_specs=(IN_VMEM,) * 2,
        compiler_params=pltpu.CompilerParams(vmem_limit_bytes=48 << 20),
        cost_estimate=pl.CostEstimate(flops=1, bytes_accessed=1, transcendentals=0),
        name="attend",
    )(near, rand, globs, bias, qkv)


def attend_back(near, rand, globs, bias, log_total, qkv, mine, come, w_qkv, grad_first):
    length, (wide, width) = qkv.shape[0], w_qkv.shape
    pairs, blocks = width // 384, length // BLOCK
    rows = jax.ShapeDtypeStruct((length // 2, wide), LOW)
    return pl.pallas_call(
        partial(attend_back_kernel, blocks, 2),
        out_shape=(
            jax.ShapeDtypeStruct((length, width), LOW),
            rows,
            rows,
            jax.ShapeDtypeStruct((1, width), WIDE),
        ),
        in_specs=[IN_SMEM] * 3 + [IN_VMEM] * 7,
        out_specs=(IN_VMEM,) * 4,
        scratch_shapes=[
            pltpu.VMEM((length, 128 * pairs), LOW),
            pltpu.VMEM((length, 256 * pairs), WIDE),
        ],
        compiler_params=pltpu.CompilerParams(vmem_limit_bytes=56 << 20),
        cost_estimate=pl.CostEstimate(flops=1, bytes_accessed=1, transcendentals=0),
        name="attend_back",
    )(near, rand, globs, bias, log_total, qkv, mine, come, w_qkv, grad_first)


def pack_columns(at, shard, near, mirror, rows_in):
    two, rows, width = shard.shape
    rows = 4 * rows_in + 2 * (rows - rows_in)
    return pl.pallas_call(
        partial(pack_columns_kernel, 4, rows_in),
        out_shape=jax.ShapeDtypeStruct((two, rows, width), LOW),
        in_specs=[IN_SMEM] + [IN_VMEM] * 3,
        out_specs=IN_VMEM,
        cost_estimate=pl.CostEstimate(flops=1, bytes_accessed=1, transcendentals=0),
        name="pack_columns",
    )(at, shard, near, mirror)


def pack_rows(at, shard, near, mirror, chunks, cut):
    rows, width = 4 * (shard.shape[0] - 16) + 16, shard.shape[1]
    return pl.pallas_call(
        partial(pack_kernel, 4, chunks, cut),
        out_shape=(
            jax.ShapeDtypeStruct((cut, width), LOW),
            jax.ShapeDtypeStruct((rows - cut, width), LOW),
        ),
        in_specs=[IN_SMEM] + [IN_VMEM] * 3,
        out_specs=(IN_VMEM, IN_VMEM),
        cost_estimate=pl.CostEstimate(flops=1, bytes_accessed=1, transcendentals=0),
        name="pack",
    )(at, shard, near, mirror)


def weight_space(chips, direct, chunks, width):
    return [
        pltpu.VMEM((chunks + 1, width, width), LOW),
        pltpu.VMEM((chunks * width, width), LOW),
        pltpu.VMEM((2 * chips if direct else 1, 16, width), LOW),
    ]


def unpack_rows(at, upper, lower, chunks):
    rows, width = upper[0].shape[0] + lower[0].shape[0], upper[0].shape[1]
    like = jax.ShapeDtypeStruct((2, rows // 4, width), LOW)
    return pl.pallas_call(
        partial(unpack_kernel, 4, chunks, len(upper)),
        out_shape=(like, like),
        in_specs=[IN_SMEM] + [IN_VMEM] * (len(upper) + len(lower)),
        out_specs=(IN_VMEM, IN_VMEM),
        cost_estimate=pl.CostEstimate(flops=1, bytes_accessed=1, transcendentals=0),
        name="unpack",
    )(at, *upper, *lower)


def layer_forward(at, mixed, other, tokens, weights, direct, chunks):
    own, width = other.shape[0], tokens.shape[1]
    chips, wide = lax.axis_size("dp") // 2, chunks * width

    def rows(width, kind=LOW):
        return jax.ShapeDtypeStruct((own, width), kind)

    return pl.pallas_call(
        partial(forward_kernel, chips, direct),
        grid=(own // TILE,),
        out_shape=(rows(width), rows(wide), rows(wide), rows(width))
        + (rows(width, WIDE), rows(width, WIDE), rows(128, WIDE)),
        in_specs=[IN_SMEM]
        + [tiles(p.shape[1]) for p in (mixed, other, tokens)]
        + [IN_ANY] * len(weights),
        out_specs=tuple(tiles(w) for w in (width, wide, wide, width, width, width, 128)),
        scratch_shapes=weight_space(chips, direct, chunks, width)
        + [pltpu.SemaphoreType.DMA((2 * chips * (chunks + 4),))],
        compiler_params=pltpu.CompilerParams(vmem_limit_bytes=58 << 20),
        cost_estimate=pl.CostEstimate(flops=1, bytes_accessed=1, transcendentals=0),
        name="layer_forward",
    )(at, mixed, other, tokens, *weights)


def layer_backward(at, mixed, other, grads, slope, units, scales, hidden, normed, weights, direct):
    own, width = normed.shape
    wide = slope.shape[1]
    half, chunks = width // 2, wide // width
    chips = lax.axis_size("dp") // 2
    many = own // TILE // 2
    whole = pl.BlockSpec((own, half), lambda i: (0, 0))
    if direct:
        rows = ((chunks + 1) * width + wide) // (2 * chips)
        grads_like = (jax.ShapeDtypeStruct((chips, rows, width), LOW),) * 2
    else:
        grads_like = (
            jax.ShapeDtypeStruct((chunks + 1, width, width), LOW),
            jax.ShapeDtypeStruct((wide, width), LOW),
        )
    return pl.pallas_call(
        partial(backward_kernel, TILE, chips, direct),
        grid=(own // TILE,),
        out_shape=(
            jax.ShapeDtypeStruct((own, width), LOW),
            jax.ShapeDtypeStruct((own, half), LOW),
            jax.ShapeDtypeStruct((own, half), LOW),
            jax.ShapeDtypeStruct((16, width), WIDE),
        )
        + grads_like,
        in_specs=[IN_SMEM]
        + [whole, whole]
        + [tiles(width, 0, many), tiles(width, many, many)]
        + [tiles(wide), tiles(width), tiles(width), tiles(128)]
        + [IN_ANY] * (2 + len(weights)),
        out_specs=(tiles(width), tiles(half), tiles(half))
        + (pl.BlockSpec((16, width), lambda i: (0, 0)),)
        + (IN_ANY,) * 2,
        scratch_shapes=weight_space(chips, direct, chunks, width)
        + [
            pltpu.VMEM((16, width), WIDE),
            pltpu.VMEM((own, wide), LOW),
            pltpu.VMEM((own, width), LOW),
            pltpu.VMEM((own, width), LOW),
            pltpu.VMEM((own, wide), LOW),
            pltpu.VMEM((own, width), LOW),
            pltpu.SemaphoreType.DMA((2 * chips * (chunks + 4),)),
            pltpu.SemaphoreType.DMA((2,)),
            pltpu.SemaphoreType.DMA((2 * chips * (chunks + 1) + 2 * chunks,)),
        ],
        compiler_params=pltpu.CompilerParams(vmem_limit_bytes=58 << 20),
        cost_estimate=pl.CostEstimate(flops=1, bytes_accessed=1, transcendentals=0),
        name="layer_backward",
    )(at, mixed, other, *grads, slope, *units, scales, hidden, normed, *weights)


def place_of(block, core, z, blocks):
    quarter, row = block // (blocks // 4), block % (blocks // 4)
    a = (quarter & 1) ^ (z & 1)
    return ((quarter >> 1) ^ core) * (blocks // 2) + a * (blocks // 4) + row


def block_at(place, core, z, blocks):
    quarter = 2 * ((place // (blocks // 2)) ^ core) + ((place % (blocks // 2)) // (blocks // 4) ^ (z & 1))
    return quarter * (blocks // 4) + place % (blocks // 4)


def tables(rand, globs, blocks):
    core = lax.axis_index("dp") & 1
    z = lax.axis_index("seq")
    here = block_at(jnp.arange(blocks, dtype=jnp.int32), core, z, blocks)
    heads = rand.shape[0]
    one, two = globs[0], globs[1]

    def near(block):
        return jnp.abs(block - here) <= 1

    every = jnp.ones((heads, blocks), bool)
    ok = [every & (here > 0), every, every & (here < blocks - 1)]
    ok += [every & ~near(one), every & ~near(two) & (one != two)]
    seen = []
    for r in range(3):
        block = rand[:, :, r]
        good = ~near(block) & (block != one) & (block != two)
        for before in seen:
            good = good & (block != before)
        seen.append(block)
        ok.append(good)
    whole_row = (here == one) | (here == two)
    ok = jnp.stack(ok, -1) & ~whole_row[None, :, None]
    bias = jnp.where(ok, 0.0, NEG).astype(WIDE)
    bias = bias.reshape(heads // 2, 2, blocks, SLOTS).transpose(2, 0, 3, 1)
    bias = jnp.repeat(bias, HEAD, axis=3)
    put = partial(place_of, core=core, z=z, blocks=blocks)
    sides = jnp.concatenate([put(jnp.maximum(here - 1, 0)), put(jnp.minimum(here + 1, blocks - 1))])
    return sides, put(rand).reshape(-1), put(globs), bias


def shards(
    inputs,
    cotangent,
    rand_blocks,
    global_blocks,
    w_query,
    b_query,
    w_key,
    w_value,
    b_value,
    w_out,
    b_out,
    gain_one,
    shift_one,
    w_up,
    b_up,
    w_down,
    b_down,
    gain_two,
    shift_two,
):
    n_dp, n_seq = lax.axis_size("dp"), lax.axis_size("seq")
    chips, devices = n_dp // 2, n_dp * n_seq
    core = lax.axis_index("dp") & 1
    z = lax.axis_index("seq")
    device = lax.axis_index("dp") * n_seq + z
    rows_in, width = w_query.shape
    rows_ff, wide = w_down.shape[0], w_up.shape[1]
    chunks = wide // width
    half_width = width // 2
    _, quarter, _ = inputs.shape
    length = quarter * n_seq
    blocks = length // BLOCK
    own = length // 2
    own_heads = HEADS // 2
    span, span_ff = n_seq * rows_in, n_seq * rows_ff
    direct = span % 16 == 0 and chips == chunks

    here = jnp.arange(devices, dtype=jnp.int32)[:, None] == device

    def placed(vector):
        return jnp.where(here, vector[None], jnp.zeros((), LOW)).reshape(-1, width)

    q_line, v_line = placed(b_query), placed(b_value)

    pairs = half_width // 128

    def side(at):
        no_line = jnp.zeros((1, width), LOW)
        parts = []
        for pair in range(pairs):
            first = at * half_width + 128 * pair
            lanes = slice(first, first + 128)
            for w, line in ((w_query, q_line), (w_key, no_line), (w_value, v_line)):
                parts.append(jnp.concatenate([w[:, lanes], line[:, lanes]], 0))
        return jnp.pad(jnp.concatenate(parts, 1), ((0, 7), (0, 0)))

    left, right = side(0), side(1)
    keep = jnp.where(core == 0, left, right)
    come = swap(jnp.where(core == 0, right, left))
    shard = jnp.stack([jnp.where(core == 0, keep, come), jnp.where(core == 0, come, keep)])
    def numbers_of(s):
        numbers = pick(rand_blocks, s, 0).reshape(-1)
        numbers = jnp.concatenate([numbers, pick(global_blocks, s, 0).reshape(-1)])
        return jnp.pad(numbers, (0, -numbers.shape[0] % 128))

    numbers = jnp.stack(bring(numbers_of))
    qkv_z = gather_seq(tie(shard, numbers))

    packed = jnp.concatenate(
        [w_up[:, width * c : width * c + width] for c in range(chunks)]
        + [w_out, w_down]
        + [placed(v) for v in (b_out, gain_one, shift_one, b_down, gain_two, shift_two, b_up)]
        + [jnp.zeros((16 - 6 - chunks, width), LOW)],
        0,
    )
    wide_z = gather_seq(tie(packed, shard), qkv_z[2])
    at = jnp.stack([lax.axis_index("dp") >> 1, core, z]).astype(jnp.int32)

    direct = span % 16 == 0 and chips == chunks
    if direct:
        whole = pack_columns(at, *qkv_z, rows_in)
    else:
        qkv_z = in_seq_order(*qkv_z)
        whole = []
        for k in range(2):
            lines = sum(p[k, rows_in:].astype(WIDE) for p in qkv_z).astype(LOW)
            whole += [p[k, :rows_in] for p in qkv_z] + [lines, jnp.zeros_like(lines)]
        whole = jnp.concatenate(whole, 0).reshape(2, span + 16, 3 * half_width)
    qkv_parts = gather_chips(whole)
    numbers = tie(numbers, whole)
    numbers = jnp.concatenate([numbers, swap(numbers)], 0)
    local_blocks = rand_blocks.shape[2]
    count = HEADS * local_blocks * 3
    globs = numbers[0, count : count + 2]
    rand = numbers[:, :count].reshape(4, HEADS, local_blocks, 3)
    rand = lax.dynamic_slice_in_dim(rand, core * own_heads, own_heads, 1)
    rand = rand.transpose(1, 0, 2, 3).reshape(own_heads, blocks, 3)
    sides, rand, glob_at, bias = tables(rand, globs, blocks)


    tied_inputs = tie(inputs, qkv_z[2])
    pieces = bring(lambda s: pick(tied_inputs, s, 0)[0])

    if direct:
        cut = chunks * span + span // 2
        near, pieces[0], bias, sides, rand, glob_at, *qkv_parts = join(
            wide_z[1], pieces[0], bias, sides, rand, glob_at, *qkv_parts
        )
        whole = pack_rows(at, wide_z[0], near, wide_z[2], chunks + 1, cut)
    else:
        wide_z = in_seq_order(*wide_z)
        rows_a = (chunks + 1) * rows_in
        rows = []
        for c in range(chunks + 1):
            rows += [p[c * rows_in : (c + 1) * rows_in] for p in wide_z]
        rows += [p[rows_a : rows_a + rows_ff] for p in wide_z]
        rows.append(sum(p[rows_a + rows_ff :].astype(WIDE) for p in wide_z).astype(LOW))
        whole = jnp.concatenate(rows, 0)
    if direct:
        lines = sum(jnp.sum(p[:, span].astype(WIDE), 0, keepdims=True) for p in qkv_parts)
        *parts, lines, pieces[0], pieces[1] = join(*gather_quads(*whole), lines, *pieces)
    else:
        parts = gather_chips(tie(whole, qkv_parts))
        lines = sum(jnp.sum(p[:, span].astype(WIDE), 0, keepdims=True) for p in qkv_parts)
    pieces = [*pieces, *(swap(p) for p in pieces)]
    rows_a, rows_b = (chunks + 1) * span, (chunks + 1) * span + span_ff
    if direct:
        qkv_weights = tuple(qkv_parts)
    else:
        ordered = in_chip_order(qkv_parts)
        qkv_weights = (jnp.concatenate([p[k, :span] for p in ordered for k in range(2)], 0),)

    if direct:
        upper, lower = jnp.stack(parts[:2]), jnp.stack(parts[2:])
        parts = [upper, flip_chip(upper, 2), lower, flip_chip(lower, 1)]
        other_parts = [swap(upper), None, swap(lower), None]
    qkv, tokens, w_qkv = project_tokens(at, pieces, lines, qkv_weights, direct)
    mixed, log_total = attend(sides, rand, glob_at, bias, qkv)
    tied = tie(cotangent, qkv)
    first_grads = bring_round(lambda s: pick(tied, s, 0)[0], 0)
    mixed, log_total, first_grads, *parts = join(mixed, log_total, first_grads, *parts)
    other = swap(mixed[own:])
    if direct:
        other_parts[1], other_parts[3] = swap(parts[1]), swap(parts[3])
    else:
        other_parts = [swap(p) for p in parts]
    if direct:
        weights = tuple(parts + other_parts)
    else:
        weights = (
            jnp.stack(
                [
                    in_device_order(
                        *([p[span * c : span * c + span] for p in ps] for ps in (parts, other_parts))
                    )
                    for c in range(chunks + 1)
                ]
            ),
            in_device_order(*([p[rows_a:rows_b] for p in ps] for ps in (parts, other_parts))),
            sum(p[rows_b:].astype(WIDE) for p in parts + other_parts).astype(LOW)[None],
        )
    tied = tie(cotangent, mixed)
    grad_result = first_grads, bring_round(lambda s: pick(tied, s, 0)[0], 1)
    forward = layer_forward(at, mixed, other, tokens, weights, direct, chunks)
    forward, grad_result = join(forward, grad_result)
    result, hidden, slope, normed, unit_one, unit_two, scales = forward
    output = send_back(result)
    backward = layer_backward(
        at,
        mixed,
        other,
        grad_result,
        slope,
        (unit_one, unit_two),
        scales,
        hidden,
        normed,
        weights,
        direct,
    )
    backward, output = join(backward, output)
    grad_first, mine, theirs, in_sums, grad_in, grad_down = backward

    come = swap(theirs)
    if direct:
        chip = lax.axis_index("dp") >> 1
        x, y = chip & 1, chip >> 1
        grad_other, come = join(swap(grad_down), come)
        sums = added(grad_in, grad_other).reshape(2, 2, -1, width)
        cut = chunks * span + span // 2
        upper, lower = sums[:, :, :cut], sums[:, :, cut:]
        moves = [pick(upper, x, 1), pick(upper, 1 - x, 1), pick(lower, y, 0), pick(lower, 1 - y, 0)]
        mine, come, *moves = join(mine, come, *moves)
        moves[1], moves[3] = flip_chip(moves[1], 1), flip_chip(moves[3], 2)
    grad_qkv, grad_own, grad_theirs, sums = attend_back(
        sides,
        rand,
        glob_at,
        bias,
        log_total,
        qkv,
        mine,
        come,
        w_qkv,
        grad_first,
    )
    if direct:
        grad_qkv, grad_own, grad_theirs, sums, *moves = join(grad_qkv, grad_own, grad_theirs, sums, *moves)
    come_rows = swap(grad_theirs)
    grad_w_qkv = dot(tokens, grad_qkv, TN).astype(LOW)
    vectors = in_sums[: 6 + chunks].reshape(-1)
    vectors = jnp.pad(vectors, (0, -vectors.shape[0] % (3 * half_width))).reshape(-1, 3 * half_width)
    lines = jnp.concatenate([sums, vectors], 0).astype(LOW)
    lines = jnp.broadcast_to(lines, (chips, 2, n_seq) + lines.shape)
    parts = jnp.concatenate(
        [grad_w_qkv.reshape(chips, 2, n_seq, rows_in, 3 * half_width), lines], 3
    )
    keep, come = (pick(parts, which, 1)[:, 0] for which in (core, 1 - core))
    if direct:
        keep, come, *moves = join(keep, come, *moves)
        upper, lower = added(*moves[:2]), added(*moves[2:])
        moves = [pick(upper, y, 0), pick(upper, 1 - y, 0), pick(lower, x, 1), pick(lower, 1 - x, 1)]
        grad_own, *moves = join(grad_own, *(move.reshape(-1, width) for move in moves))
        moves[1], moves[3] = flip_chip(moves[1], 2), flip_chip(moves[3], 1)
    come = swap(come)
    grad_tokens = added(grad_own, come_rows)
    parts = jnp.stack([keep, come], 1)
    grad_inputs = start_back(grad_tokens)
    first_back = finish_back(grad_inputs, 0)
    if direct:
        first_back, *moves = join(first_back, *moves)
        near_sums, keep_sums = unpack_rows(at, moves[:2], moves[2:], chunks + 1)
    else:
        rows = lax.psum_scatter(grad_in, "dp", scatter_dimension=1, tiled=True)
        rows = rows.reshape((chunks + 1) * span, width)
        down = lax.psum_scatter(grad_down, "dp", scatter_dimension=0, tiled=True)
        near_sums, keep_sums = unpack_rows(at, [rows], [down], chunks + 1)
    grad_inputs = first_back, finish_back(tie(grad_inputs, near_sums), 1)
    near_sums = flip_seq(near_sums, 1)
    parts = reduce_chips(parts)
    parts, near_sums = join(parts, near_sums)
    own_qkv = reduce_seq(parts.transpose(1, 0, 2, 3))
    keep, come = own_qkv[0], own_qkv[1]
    left, right = jnp.where(core == 0, keep, come), jnp.where(core == 0, come, keep)

    mirror = flip_seq(added(keep_sums[1], near_sums[1]), 3)
    own_sums = sum(p.astype(WIDE) for p in (keep_sums[0], near_sums[0], mirror))
    rows_a = (chunks + 1) * rows_in
    own_up = jnp.concatenate(
        [own_sums[c * rows_in : (c + 1) * rows_in] for c in range(chunks)], 1
    )
    small = (keep + come)[rows_in + 1 :].reshape(-1)[: (6 + chunks) * width].reshape(-1, width)

    def joined(k, rows):
        lanes = [lanes_of(k, pair) for pair in range(pairs)]
        return jnp.concatenate([one[rows, at] for one in (left, right) for at in lanes], 1)

    def own_part(vector, size):
        return lax.dynamic_slice_in_dim(vector.reshape(-1), device * size, size, 0)

    matrix_rows, line = slice(0, rows_in), slice(rows_in, rows_in + 1)
    return (
        in_sequences(output),
        in_sequences(grad_inputs),
        joined(0, matrix_rows),
        own_part(joined(0, line), rows_in),
        joined(1, matrix_rows),
        joined(2, matrix_rows),
        own_part(joined(2, line), rows_in),
        own_sums[chunks * rows_in : rows_a],
        own_part(small[0], rows_in),
        own_part(small[1], rows_in),
        own_part(small[2], rows_in),
        own_up,
        own_part(small[6 : 6 + chunks], rows_ff),
        own_sums[rows_a : rows_a + rows_ff],
        own_part(small[3], rows_in),
        own_part(small[4], rows_in),
        own_part(small[5], rows_in),
    )


def solution(mesh):
    both = ("dp", "seq")
    matrix, vector = P(both, None), P(both)
    tokens = P("dp", "seq", None)
    return jax.shard_map(
        shards,
        mesh=mesh,
        in_specs=(tokens, tokens, P("dp", None, "seq", None), P("dp", None))
        + (matrix, vector, matrix, matrix, vector, matrix, vector, vector, vector)
        + (matrix, vector, matrix, vector, vector, vector),
        out_specs=(tokens, tokens)
        + (matrix, vector, matrix, matrix, vector, matrix, vector, vector, vector)
        + (matrix, vector, matrix, vector, vector, vector),
        check_vma=False,
    )
```

```python
from functools import partial

import jax
import jax.numpy as jnp
from jax import lax
from jax.experimental import pallas as pl
from jax.experimental.pallas import tpu as pltpu
from jax.sharding import PartitionSpec as P

HEADS = 12
HEAD = 64
BLOCK = 64
SLOTS = 8
EPS = 1e-06
NEG = -1e30
LOW = jnp.bfloat16
WIDE = jnp.float32

NT = (((1,), (1,)), ((), ()))
TN = (((0,), (0,)), ((), ()))
NN = (((1,), (0,)), ((), ()))


def dot(left, right, dims):
    return lax.dot_general(left, right, dims, preferred_element_type=WIDE)


def swap(array):
    size = lax.axis_size("dp")
    return lax.ppermute(array, "dp", [(i, i ^ 1) for i in range(size)])


def flip_seq(array, k):
    size = lax.axis_size("seq")
    return lax.ppermute(array, "seq", [(i, i ^ k) for i in range(size)])


def rounds():
    dp, seq = lax.axis_size("dp"), lax.axis_size("seq")
    for a in range(2):
        pairs = []
        for d in range(dp):
            for z in range(seq):
                to_dp = (d & ~1) | (z >> 1)
                to_seq = 2 * (d & 1) + (a ^ (z & 1))
                pairs.append((d * seq + z, to_dp * seq + to_seq))
        yield a, pairs


def bring_round(piece_of, which):
    a, pairs = list(rounds())[which]
    z = lax.axis_index("seq")
    return lax.ppermute(piece_of(a ^ (z & 1)), ("dp", "seq"), pairs)


def bring(piece_of):
    return [bring_round(piece_of, which) for which in range(2)]


def start_back(rows):
    size = rows.shape[0] // 2
    return [rows[size * a : size * a + size] for a in range(2)]


def finish_back(parts, which):
    a, pairs = list(rounds())[which]
    return lax.ppermute(parts[a], ("dp", "seq"), [(t, s) for s, t in pairs])


def send_back(rows):
    parts = start_back(rows)
    return [finish_back(parts, a) for a in range(2)]


def in_sequences(got):
    odd = (lax.axis_index("seq") & 1) == 1
    return jnp.stack([jnp.where(odd, got[1], got[0]), jnp.where(odd, got[0], got[1])])


def pick(array, index, axis):
    return lax.dynamic_slice_in_dim(array, index, 1, axis)


def gather_seq(shard, before=None):
    mirror = flip_seq(shard, 3)
    pair = jnp.stack([shard, mirror])
    if before is not None:
        pair = tie(pair, before)
    return shard, flip_seq(pair, 1), mirror


def in_seq_order(shard, near, mirror):
    z = lax.axis_index("seq")
    pieces = [shard, near[0], near[1], mirror]
    for bit in range(2):
        set_bit = ((z >> bit) & 1) == 1
        pieces = [
            jnp.where(set_bit, pieces[i ^ (1 << bit)], pieces[i]) for i in range(len(pieces))
        ]
    return pieces


def chip_groups():
    count = (lax.axis_size("dp") // 2).bit_length() - 1
    return [(bit, min(2, count - bit)) for bit in range(0, count, 2)]


def flip_chip(array, away):
    size = lax.axis_size("dp")
    return lax.ppermute(array, "dp", [(i, i ^ (2 * away)) for i in range(size)])


def gather_chips(part):
    parts = [part]
    for bit, bits in chip_groups():
        parts = parts + [flip_chip(p, k << bit) for k in range(1, 1 << bits) for p in parts]
    return parts


def in_chip_order(parts):
    chip = lax.axis_index("dp") >> 1
    parts = jnp.stack(parts)
    return [pick(parts, q ^ chip, 0)[0] for q in range(parts.shape[0])]


def in_device_order(mine, theirs):
    core = lax.axis_index("dp") & 1
    parts = []
    for own, other in zip(in_chip_order(mine), in_chip_order(theirs)):
        parts += [jnp.where(core == 0, own, other), jnp.where(core == 0, other, own)]
    return jnp.concatenate(parts, 0)


def join(*values):
    return lax.optimization_barrier(values)


def gather_quads(upper, lower):
    return [upper, flip_chip(upper, 1), lower, flip_chip(lower, 2)]


def tie(values, *others):
    return lax.optimization_barrier((values, others))[0]


def added(*arrays):
    return sum(array.astype(WIDE) for array in arrays).astype(LOW)


def reduce_chips(parts):
    chip = lax.axis_index("dp") >> 1
    for bit, bits in chip_groups():
        ways = 1 << bits
        parts = parts.reshape((-1, ways) + parts.shape[1:])
        mine = (chip >> bit) & (ways - 1)
        others = [flip_chip(pick(parts, mine ^ k, 1)[:, 0], k << bit) for k in range(1, ways)]
        parts = added(pick(parts, mine, 1)[:, 0], *others)
    return parts[0]


def reduce_seq(parts):
    z = lax.axis_index("seq")
    near = flip_seq(jnp.concatenate([pick(parts, z ^ 1, 0), pick(parts, z ^ 2, 0)], 0), 1)
    mirror = added(pick(parts, z ^ 3, 0)[0], near[1])
    return pick(parts, z, 0)[0].astype(WIDE) + near[0].astype(WIDE) + flip_seq(mirror, 3).astype(WIDE)


def norm_parts(summed):
    center = summed - jnp.mean(summed, -1, keepdims=True)
    spread = jnp.mean(center * center, -1, keepdims=True)
    scale = lax.rsqrt(spread + EPS)
    return center * scale, scale


def norm_back(grad, unit, scale, gain):
    grad_unit = grad * gain
    mean_one = jnp.mean(grad_unit, -1, keepdims=True)
    mean_two = jnp.mean(grad_unit * unit, -1, keepdims=True)
    return scale * (grad_unit - mean_one - unit * mean_two)


def gelu_parts(x):
    size = jnp.abs(x)
    t = 1.0 / (1.0 + (0.3275911 * 0.5**0.5) * size)
    bell = jnp.exp(-0.5 * x * x)
    series = 0.5 * 1.061405429
    for factor in (-1.453152027, 1.421413741, -0.284496736, 0.254829592):
        series = series * t + 0.5 * factor
    tail = series * t * bell
    share = jnp.where(x >= 0, 1.0 - tail, tail)
    return x * share, share + x * bell * 0.3989422804014327


def block_rows(ref, block, lanes):
    return ref[pl.ds(pl.multiple_of(block * BLOCK, BLOCK), BLOCK), lanes]


def diagonal(pair_rows, low):
    zero = jnp.zeros_like(pair_rows)
    return jnp.concatenate(
        [jnp.where(low, pair_rows, zero), jnp.where(low, zero, pair_rows)], axis=0
    )


def gather_blocks(ref, ids, lanes, low):
    parts = []
    for one, two in ids:
        if two is None:
            parts.append(block_rows(ref, one, lanes))
        else:
            parts.append(
                jnp.where(low, block_rows(ref, one, lanes), block_rows(ref, two, lanes))
            )
    return jnp.concatenate(parts, axis=0)


def slot_ids(near_ref, rand_ref, globs, i, head, blocks):
    ids = [(near_ref[i], None), (i, None), (near_ref[blocks + i], None)]
    ids += [(globs[0], None), (globs[1], None)]
    for r in range(3):
        ids.append(
            (
                rand_ref[(head * blocks + i) * 3 + r],
                rand_ref[((head + 1) * blocks + i) * 3 + r],
            )
        )
    return ids


def lanes_of(part, pair):
    first = 128 * (3 * pair + part)
    return slice(first, first + 128)


def flat_lanes(pair):
    return slice(128 * pair, 128 * pair + 128)


def start_copies(copies, sems):
    started = [
        pltpu.make_async_copy(source, target, sems.at[k])
        for k, (source, target) in enumerate(copies)
    ]
    for copy in started:
        copy.start()
    return started


def project_kernel(chips, direct, at_ref, *refs):
    pieces, b_ref = refs[:4], refs[4]
    sources, (qkv_ref, tokens_ref, w_ref, sems) = refs[5:-4], refs[-4:]
    if direct:
        span = w_ref.shape[0] // (2 * chips)
        copies = [
            (
                sources[away].at[k, :span],
                w_ref.at[pl.ds(pl.multiple_of((2 * (at_ref[0] ^ away) + k) * span, span), span)],
            )
            for away in range(chips)
            for k in range(2)
        ]
    else:
        copies = [(sources[0], w_ref)]

    @pl.when(pl.program_id(0) == 0)
    def _():
        for copy in start_copies(copies, sems):
            copy.wait()

    lane = lax.broadcasted_iota(jnp.int32, (1, w_ref.shape[1]), 1)
    scale = jnp.where(lane % 384 < 128, HEAD ** (-0.5), 1.0)
    at = pl.program_id(0) * len(pieces) // pl.num_programs(0)
    rows = pieces[0][...]
    for k in range(1, len(pieces)):
        rows = jnp.where(at == k, pieces[k][...], rows)
    tokens_ref[...] = rows
    values = (dot(rows, w_ref[...], NN) + b_ref[...]).astype(LOW).astype(WIDE)
    qkv_ref[...] = (values * scale).astype(LOW)


def with_sems(groups, sems):
    done, copies = 0, []
    for group in groups:
        copies.append([pltpu.make_async_copy(*pair, sems.at[done + k]) for k, pair in enumerate(group)])
        done += len(group)
    return copies


def attend_kernel(
    pairs, blocks, step, near_ref, rand_ref, glob_ref, bias_ref, qkv_ref, out_ref, log_ref
):
    low = lax.broadcasted_iota(jnp.int32, (1, 2 * HEAD), 1) < HEAD
    globs = (glob_ref[0], glob_ref[1])

    def scores_of(i, pair):
        ids = slot_ids(near_ref, rand_ref, globs, i, 2 * pair, blocks)
        queries = diagonal(block_rows(qkv_ref, i, lanes_of(0, pair)), low)
        return dot(gather_blocks(qkv_ref, ids, lanes_of(1, pair), low), queries, NT)

    def softmax_of(i, pair, scores):
        highest = jnp.max(scores, axis=0, keepdims=True)
        weights = jnp.exp(scores - highest)
        total = jnp.sum(weights, axis=0, keepdims=True)
        log_ref[i, pair : pair + 1] = highest + jnp.log(total)
        return (weights * (1.0 / total)).astype(LOW)

    def put(i, pair, mixed):
        at = pl.ds(pl.multiple_of(i * BLOCK, BLOCK), BLOCK)
        out_ref[at, flat_lanes(pair)] = jnp.where(low, mixed[:BLOCK], mixed[BLOCK:]).astype(LOW)

    def body(at, carry):
        units = [(at * step + d, pair) for d in range(step) for pair in range(pairs)]
        scores = [scores_of(*unit) for unit in units]
        probs = []
        for (i, pair), score in zip(units, scores):
            bias = bias_ref[i, pair]
            score = jnp.concatenate(
                [score[BLOCK * j : BLOCK * j + BLOCK] + bias[j : j + 1] for j in range(SLOTS)],
                axis=0,
            )
            probs.append(softmax_of(i, pair, score))
        for (i, pair), prob in zip(units, probs):
            ids = slot_ids(near_ref, rand_ref, globs, i, 2 * pair, blocks)
            values = gather_blocks(qkv_ref, ids, lanes_of(2, pair), low)
            put(i, pair, dot(prob, values, TN))
        return carry

    lax.fori_loop(0, blocks // step, body, 0)

    def whole_row(n, carry):
        i = glob_ref[n]
        scores = []
        for pair in range(pairs):
            queries = diagonal(block_rows(qkv_ref, i, lanes_of(0, pair)), low)
            scores.append(dot(qkv_ref[:, lanes_of(1, pair)], queries, NT))
        probs = [softmax_of(i, pair, scores[pair]) for pair in range(pairs)]
        for pair in range(pairs):
            put(i, pair, dot(probs[pair], qkv_ref[:, lanes_of(2, pair)], TN))
        return carry

    lax.fori_loop(0, 2, whole_row, 0)


def attend_back_kernel(
    blocks,
    step,
    near_ref,
    rand_ref,
    glob_ref,
    bias_ref,
    log_ref,
    qkv_ref,
    mine_ref,
    come_ref,
    w_ref,
    grad_first_ref,
    out_ref,
    rows_own_ref,
    rows_other_ref,
    sums_ref,
    grad_ref,
    acc_ref,
):
    low = lax.broadcasted_iota(jnp.int32, (1, 2 * HEAD), 1) < HEAD
    globs = (glob_ref[0], glob_ref[1])
    acc_ref[...] = jnp.zeros_like(acc_ref)
    half = mine_ref.shape[0]
    grad_ref[:half] = mine_ref[...]
    grad_ref[half:] = come_ref[...]
    pairs = mine_ref.shape[1] // 128

    def source(pair, part):
        return qkv_ref.at[:, lanes_of(part, pair)]

    def log_of(i, pair):
        return log_ref[i, pair : pair + 1]

    every = slice(None)

    def add(part, pair, block, value):
        at = pl.ds(pl.multiple_of(block * BLOCK, BLOCK), BLOCK)
        lanes = flat_lanes(2 * pair + part)
        acc_ref[at, lanes] = acc_ref[at, lanes] + value

    def operands(i, pair):
        queries = diagonal(block_rows(source(pair, 0), i, every), low)
        grads = diagonal(block_rows(grad_ref, i, flat_lanes(pair)), low)
        return queries, grads

    def softmax_back(prob, grad_prob):
        scaled = prob * grad_prob
        inner = jnp.sum(scaled, axis=0, keepdims=True)
        return prob.astype(LOW), (scaled - prob * inner).astype(LOW)

    def put(i, pair, mixed):
        at = pl.ds(pl.multiple_of(i * BLOCK, BLOCK), BLOCK)
        out_ref[at, lanes_of(0, pair)] = (
            jnp.where(low, mixed[:BLOCK], mixed[BLOCK:]) * HEAD ** (-0.5)
        ).astype(LOW)

    def body(at, carry):
        units = [(at * step + d, pair) for d in range(step) for pair in range(pairs)]
        first = []
        for i, pair in units:
            ids = slot_ids(near_ref, rand_ref, globs, i, 2 * pair, blocks)
            queries, grads = operands(i, pair)
            first.append(
                (
                    dot(gather_blocks(source(pair, 1), ids, every, low), queries, NT),
                    dot(gather_blocks(source(pair, 2), ids, every, low), grads, NT),
                )
            )
        second = []
        for (i, pair), (score, grad_prob) in zip(units, first):
            shift = bias_ref[i, pair] - log_of(i, pair)
            prob = jnp.concatenate(
                [
                    jnp.exp(score[BLOCK * j : BLOCK * j + BLOCK] + shift[j : j + 1])
                    for j in range(SLOTS)
                ],
                axis=0,
            )
            second.append(softmax_back(prob, grad_prob))
        third = []
        for (i, pair), (prob, grad_score) in zip(units, second):
            ids = slot_ids(near_ref, rand_ref, globs, i, 2 * pair, blocks)
            queries, grads = operands(i, pair)
            keys = gather_blocks(source(pair, 1), ids, every, low)
            put(i, pair, dot(grad_score, keys, TN))
            third.append((dot(grad_score, queries, NN), dot(prob, grads, NN)))
        for (i, pair), values in zip(units, third):
            ids = slot_ids(near_ref, rand_ref, globs, i, 2 * pair, blocks)
            for j, (one, two) in enumerate(ids):
                for part, value in enumerate(values):
                    value = value[BLOCK * j : BLOCK * j + BLOCK]
                    if two is None:
                        add(part, pair, one, value)
                    else:
                        add(part, pair, one, jnp.where(low, value, 0.0))
                        add(part, pair, two, jnp.where(low, 0.0, value))
        return carry

    lax.fori_loop(0, blocks // step, body, 0)

    def whole_row(n, carry):
        i = glob_ref[n]
        first = []
        for pair in range(pairs):
            queries, grads = operands(i, pair)
            first.append(
                (
                    dot(source(pair, 1)[...], queries, NT),
                    dot(source(pair, 2)[...], grads, NT),
                )
            )
        second = []
        for pair, (score, grad_prob) in enumerate(first):
            prob = jnp.exp(score - log_of(i, pair))
            second.append(softmax_back(prob, grad_prob))
        for pair, (prob, grad_score) in enumerate(second):
            queries, grads = operands(i, pair)
            acc_ref[:, flat_lanes(2 * pair)] += dot(grad_score, queries, NN)
            acc_ref[:, flat_lanes(2 * pair + 1)] += dot(prob, grads, NN)
            put(i, pair, dot(grad_score, source(pair, 1)[...], TN))
        return carry

    lax.fori_loop(0, jnp.where(globs[0] == globs[1], 1, 2), whole_row, 0)
    for pair in range(pairs):
        out_ref[:, 384 * pair + 128 : 384 * pair + 384] = acc_ref[
            :, 256 * pair : 256 * pair + 256
        ].astype(LOW)

    sums_ref[...] = jnp.zeros_like(sums_ref)
    tile = 512
    for side, rows_ref in enumerate((rows_own_ref, rows_other_ref)):

        def token_rows(at, carry, side=side, rows_ref=rows_ref):
            grads = out_ref[pl.ds(pl.multiple_of(side * half + at * tile, tile), tile)]
            sums_ref[...] += jnp.sum(grads.astype(WIDE), 0, keepdims=True)
            rows = pl.ds(pl.multiple_of(at * tile, tile), tile)
            total = dot(grads, w_ref[...], NT)
            if side == 0:
                total = total + grad_first_ref[rows].astype(WIDE)
            rows_ref[rows] = total.astype(LOW)
            return carry

        lax.fori_loop(0, half // tile, token_rows, 0)


def pack_kernel(seq, chunks, cut, at_ref, shard_ref, near_ref, mirror_ref, upper_ref, lower_ref):
    rows = shard_ref.shape[0] - 16
    rows_in = rows // (chunks + 4)
    rows_ff = rows - chunks * rows_in
    pieces = [shard_ref, near_ref.at[0], near_ref.at[1], mirror_ref]
    total = sum(piece[rows:].astype(WIDE) for piece in pieces)

    def put(first, value):
        target, first = (upper_ref, first) if first < cut else (lower_ref, first - cut)
        target[first : first + value.shape[0]] = value

    put(rows * seq, total.astype(LOW))
    for z in range(seq):

        @pl.when(at_ref[2] == z)
        def _(z=z):
            for k, piece in enumerate(pieces):
                for c in range(chunks):
                    put((c * seq + (z ^ k)) * rows_in, piece[c * rows_in : c * rows_in + rows_in])
                put(chunks * seq * rows_in + (z ^ k) * rows_ff, piece[chunks * rows_in : rows])


def pack_columns_kernel(seq, rows_in, at_ref, shard_ref, near_ref, mirror_ref, out_ref):
    pieces = [shard_ref, near_ref.at[0], near_ref.at[1], mirror_ref]
    total = sum(piece[:, rows_in:].astype(WIDE) for piece in pieces).astype(LOW)
    out_ref[:, seq * rows_in :] = jnp.concatenate([total, jnp.zeros_like(total)], 1)
    for z in range(seq):

        @pl.when(at_ref[2] == z)
        def _(z=z):
            for k, piece in enumerate(pieces):
                first = (z ^ k) * rows_in
                out_ref[:, first : first + rows_in] = piece[:, :rows_in]


def unpack_kernel(seq, chunks, many, at_ref, *refs):
    sources, (near_ref, keep_ref) = refs[:-2], refs[-2:]
    rows = near_ref.shape[1]
    rows_in = rows // (chunks + 4)
    rows_ff = rows - chunks * rows_in

    cut = sources[0].shape[0]

    def total(first, size):
        refs, first = (sources[:many], first) if first < cut else (sources[many:], first - cut)
        return sum(ref[first : first + size].astype(WIDE) for ref in refs).astype(LOW)

    for z in range(seq):

        @pl.when(at_ref[2] == z)
        def _(z=z):
            for k in range(seq):
                target = (keep_ref, near_ref)[k in (1, 2)].at[int(k > 1)]
                for c in range(chunks):
                    part = total((c * seq + (z ^ k)) * rows_in, rows_in)
                    target[c * rows_in : c * rows_in + rows_in] = part
                target[chunks * rows_in :] = total(chunks * seq * rows_in + (z ^ k) * rows_ff, rows_ff)


def weight_copies(chips, direct, chip, core, sources, w_in_ref, w_down_ref, lines_ref):
    if not direct:
        return [(sources[0], w_in_ref), (sources[2], lines_ref)], [], [(sources[1], w_down_ref)]
    wide, width = w_down_ref.shape
    chunks = wide // width
    span, span_ff = width // (2 * chips), wide // (2 * chips)
    cut = span // 2
    groups = [], [], []
    for k in range(2):
        for away in range(chips):
            place = 2 * (chip ^ away) + (core if k == 0 else 1 - core)
            upper = sources[4 * k + (away >> 1)].at[away & 1]
            lower = sources[4 * k + 2 + (away & 1)].at[away >> 1]
            rows = pl.ds(pl.multiple_of(place * span, span), span)
            groups[1].extend(
                (upper.at[span * c : span * c + span], w_in_ref.at[c, rows]) for c in range(chunks)
            )
            for half, source in enumerate((upper.at[span * chunks :], lower.at[:cut])):
                rows = pl.ds(pl.multiple_of(place * span + half * cut, cut), cut)
                groups[0].append((source, w_in_ref.at[chunks, rows]))
            rows = pl.ds(pl.multiple_of(place * span_ff, span_ff), span_ff)
            groups[2].append((lower.at[cut : cut + span_ff], w_down_ref.at[rows]))
            groups[0].append((lower.at[cut + span_ff :], lines_ref.at[k * chips + away]))
    return groups


def forward_kernel(
    chips,
    direct,
    at_ref,
    mixed_ref,
    other_ref,
    tokens_ref,
    *refs,
):
    sources, refs = refs[:-11], refs[-11:]
    output_ref, hidden_ref, slope_ref, normed_ref, unit_one_ref, unit_two_ref, scales_ref = refs[:7]
    w_in_ref, w_down_ref, lines_ref, sems = refs[7:]
    wide, width = w_down_ref.shape
    half, chunks = width // 2, wide // width
    core = at_ref[1]
    groups = weight_copies(chips, direct, at_ref[0], core, sources, w_in_ref, w_down_ref, lines_ref)
    groups = with_sems(groups, sems)

    @pl.when(pl.program_id(0) == 0)
    def _():
        for copy in sum(groups, []):
            copy.start()
        for copy in groups[0]:
            copy.wait()

    vectors = jnp.sum(lines_ref[...].astype(WIDE), 0)
    b_out, gain_one, shift_one, b_down, gain_two, shift_two = (vectors[k : k + 1] for k in range(6))
    here = pl.ds(pl.multiple_of(core * half, 128), half)
    there = pl.ds(pl.multiple_of((1 - core) * half, 128), half)
    branch = dot(mixed_ref[...], w_in_ref[chunks, here], NN) + dot(other_ref[...], w_in_ref[chunks, there], NN)
    unit_one, scale_one = norm_parts(tokens_ref[...].astype(WIDE) + (branch + b_out))
    normed = unit_one * gain_one + shift_one
    normed_low = normed.astype(LOW)
    normed_ref[...] = normed_low
    unit_one_ref[...] = unit_one

    @pl.when(pl.program_id(0) == 0)
    def _():
        for copy in groups[1] + groups[2]:
            copy.wait()

    down = b_down
    for c in range(0, chunks, 2):
        lanes = slice(width * c, width * c + 2 * width)
        weights = jnp.concatenate([w_in_ref[c], w_in_ref[c + 1]], 1)
        bias = jnp.concatenate([vectors[6 + c : 7 + c], vectors[7 + c : 8 + c]], 1)
        hidden, slope = gelu_parts(dot(normed_low, weights, NN) + bias)
        hidden = hidden.astype(LOW)
        hidden_ref[:, lanes] = hidden
        slope_ref[:, lanes] = slope.astype(LOW)
        down = down + dot(hidden, w_down_ref[lanes], NN)
    unit_two, scale_two = norm_parts(normed + down)
    output_ref[...] = (unit_two * gain_two + shift_two).astype(LOW)
    lane = lax.broadcasted_iota(jnp.int32, (1, 128), 1)
    scales_ref[...] = jnp.where(lane < 64, scale_one, scale_two)
    unit_two_ref[...] = unit_two


def backward_kernel(
    tile,
    chips,
    direct,
    at_ref,
    mixed_ref,
    other_ref,
    grad_first_ref,
    grad_last_ref,
    slope_ref,
    unit_one_ref,
    unit_two_ref,
    scales_ref,
    hidden_hbm,
    normed_hbm,
    *refs,
):
    sources, refs = refs[:-18], refs[-18:]
    first_ref, mine_ref, theirs_ref, sums_ref, *grad_refs = refs[:6]
    w_in_ref, w_down_ref, lines_ref, vectors_ref, pre_ref, branch_ref = refs[6:12]
    normed_ref, hidden_ref, down_ref, sems, extra_sems, out_sems = refs[12:]
    own, width = normed_ref.shape
    wide = w_down_ref.shape[0]
    half, chunks = width // 2, wide // width
    chip, core = at_ref[0], at_ref[1]
    at, last = pl.program_id(0), pl.num_programs(0) - 1
    rows = pl.ds(pl.multiple_of(at * tile, tile), tile)
    groups = weight_copies(chips, direct, chip, core, sources, w_in_ref, w_down_ref, lines_ref)
    groups = with_sems(groups, sems)
    extra = [
        pltpu.make_async_copy(hidden_hbm, hidden_ref, extra_sems.at[0]),
        pltpu.make_async_copy(normed_hbm, normed_ref, extra_sems.at[1]),
    ]
    here = pl.ds(pl.multiple_of(core * half, 128), half)
    there = pl.ds(pl.multiple_of((1 - core) * half, 128), half)

    @pl.when(at == 0)
    def _():
        for copy in groups[2] + groups[1] + groups[0]:
            copy.start()
        for copy in extra:
            copy.start()
        sums_ref[...] = jnp.zeros_like(sums_ref)
        for copy in groups[2] + groups[1] + groups[0]:
            copy.wait()
        vectors_ref[...] = jnp.sum(lines_ref[...].astype(WIDE), 0)

    def add_sum(k, value):
        sums_ref[k : k + 1] += jnp.sum(value, 0, keepdims=True)

    grad = jnp.where(2 * at <= last, grad_first_ref[...], grad_last_ref[...]).astype(WIDE)
    unit_two = unit_two_ref[...]
    add_sum(4, grad * unit_two)
    add_sum(5, grad)
    grad_normed = norm_back(grad, unit_two, scales_ref[:, 64:65], vectors_ref[4:5])
    grad_down = grad_normed.astype(LOW)
    down_ref[rows] = grad_down
    add_sum(3, grad_down.astype(WIDE))
    for c in range(chunks):
        lanes = slice(width * c, width * c + width)
        grad_pre = dot(grad_down, w_down_ref[lanes], NT) * slope_ref[:, lanes].astype(WIDE)
        grad_pre = grad_pre.astype(LOW)
        pre_ref[rows, lanes] = grad_pre
        add_sum(6 + c, grad_pre.astype(WIDE))
        grad_normed = grad_normed + dot(grad_pre, w_in_ref[c], NT)
    unit_one = unit_one_ref[...]
    add_sum(1, grad_normed * unit_one)
    add_sum(2, grad_normed)
    grad_branch = norm_back(grad_normed, unit_one, scales_ref[:, 0:1], vectors_ref[1:2]).astype(LOW)
    first_ref[...] = grad_branch
    branch_ref[rows] = grad_branch
    add_sum(0, grad_branch.astype(WIDE))
    mine_ref[...] = dot(grad_branch, w_in_ref[chunks, here], NT).astype(LOW)
    theirs_ref[...] = dot(grad_branch, w_in_ref[chunks, there], NT).astype(LOW)

    @pl.when(at == last)
    def _():
        for copy in extra:
            copy.wait()
        moving = []
        span, span_ff = width // (2 * chips), wide // (2 * chips)
        first = span * (chunks + 1)

        def leave(pairs):
            for source, target in pairs:
                copy = pltpu.make_async_copy(source, target, out_sems.at[len(moving)])
                copy.start()
                moving.append(copy)

        def leave_rows(c):
            if not direct:
                return leave([(w_in_ref.at[c], grad_refs[0].at[c])])
            for k, target in enumerate(grad_refs):
                for q in range(chips):
                    place = 2 * q + (core if k == 0 else 1 - core)
                    source = w_in_ref.at[c, pl.ds(pl.multiple_of(place * span, span), span)]
                    leave([(source, target.at[q, span * c : span * c + span])])

        for c in range(chunks):
            lanes = slice(width * c, width * c + width)
            w_down_ref[lanes] = dot(hidden_ref[:, lanes], down_ref[...], TN).astype(LOW)
            if direct:
                for k, target in enumerate(grad_refs):
                    place = 2 * c + (core if k == 0 else 1 - core)
                    source = w_down_ref.at[pl.ds(pl.multiple_of(place * span_ff, span_ff), span_ff)]
                    leave([(source, target.at[c, first : first + span_ff])])
            else:
                leave([(w_down_ref.at[lanes], grad_refs[1].at[lanes])])
            w_in_ref[c] = dot(normed_ref[...], pre_ref[:, lanes], TN).astype(LOW)
            leave_rows(c)
        w_in_ref[chunks, here] = dot(mixed_ref[...], branch_ref[...], TN).astype(LOW)
        w_in_ref[chunks, there] = dot(other_ref[...], branch_ref[...], TN).astype(LOW)
        leave_rows(chunks)
        for copy in moving:
            copy.wait()


IN_SMEM = pl.BlockSpec(memory_space=pltpu.SMEM)
IN_VMEM = pl.BlockSpec(memory_space=pltpu.VMEM)


IN_ANY = pl.BlockSpec(memory_space=pl.ANY)


TILE = 256


def tiles(width, first=0, many=None):
    if many is None:
        return pl.BlockSpec((TILE, width), lambda i: (i, 0))
    return pl.BlockSpec((TILE, width), lambda i: (jnp.clip(i - first, 0, many - 1), 0))


def project_tokens(at, pieces, b_qkv, weights, direct):
    length, width = 4 * pieces[0].shape[0], pieces[0].shape[1]
    half = width // 2
    chips = lax.axis_size("dp") // 2
    many = pieces[0].shape[0] // TILE

    def all_of(*shape):
        return pl.BlockSpec(shape, lambda i: (0, 0))

    return pl.pallas_call(
        partial(project_kernel, chips, direct),
        grid=(length // TILE,),
        out_shape=(
            jax.ShapeDtypeStruct((length, 3 * half), LOW),
            jax.ShapeDtypeStruct((length, width), LOW),
            jax.ShapeDtypeStruct((width, 3 * half), LOW),
        ),
        in_specs=[IN_SMEM]
        + [tiles(width, many * k, many) for k in range(4)]
        + [all_of(1, 3 * half)]
        + [IN_ANY] * len(weights),
        out_specs=(tiles(3 * half), tiles(width), all_of(width, 3 * half)),
        scratch_shapes=[pltpu.SemaphoreType.DMA((2 * chips,))],
        compiler_params=pltpu.CompilerParams(vmem_limit_bytes=48 << 20),
        cost_estimate=pl.CostEstimate(flops=1, bytes_accessed=1, transcendentals=0),
        name="project",
    )(at, *pieces, b_qkv, *weights)


def attend(near, rand, globs, bias, qkv):
    length, width = qkv.shape
    pairs, blocks = width // 384, length // BLOCK
    return pl.pallas_call(
        partial(attend_kernel, pairs, blocks, 4),
        out_shape=(
            jax.ShapeDtypeStruct((length, 128 * pairs), LOW),
            jax.ShapeDtypeStruct((blocks, 8, 128), WIDE),
        ),
        in_specs=[IN_SMEM] * 3 + [IN_VMEM] * 2,
        out_specs=(IN_VMEM,) * 2,
        compiler_params=pltpu.CompilerParams(vmem_limit_bytes=48 << 20),
        cost_estimate=pl.CostEstimate(flops=1, bytes_accessed=1, transcendentals=0),
        name="attend",
    )(near, rand, globs, bias, qkv)


def attend_back(near, rand, globs, bias, log_total, qkv, mine, come, w_qkv, grad_first):
    length, (wide, width) = qkv.shape[0], w_qkv.shape
    pairs, blocks = width // 384, length // BLOCK
    rows = jax.ShapeDtypeStruct((length // 2, wide), LOW)
    return pl.pallas_call(
        partial(attend_back_kernel, blocks, 2),
        out_shape=(
            jax.ShapeDtypeStruct((length, width), LOW),
            rows,
            rows,
            jax.ShapeDtypeStruct((1, width), WIDE),
        ),
        in_specs=[IN_SMEM] * 3 + [IN_VMEM] * 7,
        out_specs=(IN_VMEM,) * 4,
        scratch_shapes=[
            pltpu.VMEM((length, 128 * pairs), LOW),
            pltpu.VMEM((length, 256 * pairs), WIDE),
        ],
        compiler_params=pltpu.CompilerParams(vmem_limit_bytes=56 << 20),
        cost_estimate=pl.CostEstimate(flops=1, bytes_accessed=1, transcendentals=0),
        name="attend_back",
    )(near, rand, globs, bias, log_total, qkv, mine, come, w_qkv, grad_first)


def pack_columns(at, shard, near, mirror, rows_in):
    two, rows, width = shard.shape
    rows = 4 * rows_in + 2 * (rows - rows_in)
    return pl.pallas_call(
        partial(pack_columns_kernel, 4, rows_in),
        out_shape=jax.ShapeDtypeStruct((two, rows, width), LOW),
        in_specs=[IN_SMEM] + [IN_VMEM] * 3,
        out_specs=IN_VMEM,
        cost_estimate=pl.CostEstimate(flops=1, bytes_accessed=1, transcendentals=0),
        name="pack_columns",
    )(at, shard, near, mirror)


def pack_rows(at, shard, near, mirror, chunks, cut):
    rows, width = 4 * (shard.shape[0] - 16) + 16, shard.shape[1]
    return pl.pallas_call(
        partial(pack_kernel, 4, chunks, cut),
        out_shape=(
            jax.ShapeDtypeStruct((cut, width), LOW),
            jax.ShapeDtypeStruct((rows - cut, width), LOW),
        ),
        in_specs=[IN_SMEM] + [IN_VMEM] * 3,
        out_specs=(IN_VMEM, IN_VMEM),
        cost_estimate=pl.CostEstimate(flops=1, bytes_accessed=1, transcendentals=0),
        name="pack",
    )(at, shard, near, mirror)


def weight_space(chips, direct, chunks, width):
    return [
        pltpu.VMEM((chunks + 1, width, width), LOW),
        pltpu.VMEM((chunks * width, width), LOW),
        pltpu.VMEM((2 * chips if direct else 1, 16, width), LOW),
    ]


def unpack_rows(at, upper, lower, chunks):
    rows, width = upper[0].shape[0] + lower[0].shape[0], upper[0].shape[1]
    like = jax.ShapeDtypeStruct((2, rows // 4, width), LOW)
    return pl.pallas_call(
        partial(unpack_kernel, 4, chunks, len(upper)),
        out_shape=(like, like),
        in_specs=[IN_SMEM] + [IN_VMEM] * (len(upper) + len(lower)),
        out_specs=(IN_VMEM, IN_VMEM),
        cost_estimate=pl.CostEstimate(flops=1, bytes_accessed=1, transcendentals=0),
        name="unpack",
    )(at, *upper, *lower)


def layer_forward(at, mixed, other, tokens, weights, direct, chunks):
    own, width = other.shape[0], tokens.shape[1]
    chips, wide = lax.axis_size("dp") // 2, chunks * width

    def rows(width, kind=LOW):
        return jax.ShapeDtypeStruct((own, width), kind)

    return pl.pallas_call(
        partial(forward_kernel, chips, direct),
        grid=(own // TILE,),
        out_shape=(rows(width), rows(wide), rows(wide), rows(width))
        + (rows(width, WIDE), rows(width, WIDE), rows(128, WIDE)),
        in_specs=[IN_SMEM]
        + [tiles(p.shape[1]) for p in (mixed, other, tokens)]
        + [IN_ANY] * len(weights),
        out_specs=tuple(tiles(w) for w in (width, wide, wide, width, width, width, 128)),
        scratch_shapes=weight_space(chips, direct, chunks, width)
        + [pltpu.SemaphoreType.DMA((2 * chips * (chunks + 4),))],
        compiler_params=pltpu.CompilerParams(vmem_limit_bytes=58 << 20),
        cost_estimate=pl.CostEstimate(flops=1, bytes_accessed=1, transcendentals=0),
        name="layer_forward",
    )(at, mixed, other, tokens, *weights)


def layer_backward(at, mixed, other, grads, slope, units, scales, hidden, normed, weights, direct):
    own, width = normed.shape
    wide = slope.shape[1]
    half, chunks = width // 2, wide // width
    chips = lax.axis_size("dp") // 2
    many = own // TILE // 2
    whole = pl.BlockSpec((own, half), lambda i: (0, 0))
    if direct:
        rows = ((chunks + 1) * width + wide) // (2 * chips)
        grads_like = (jax.ShapeDtypeStruct((chips, rows, width), LOW),) * 2
    else:
        grads_like = (
            jax.ShapeDtypeStruct((chunks + 1, width, width), LOW),
            jax.ShapeDtypeStruct((wide, width), LOW),
        )
    return pl.pallas_call(
        partial(backward_kernel, TILE, chips, direct),
        grid=(own // TILE,),
        out_shape=(
            jax.ShapeDtypeStruct((own, width), LOW),
            jax.ShapeDtypeStruct((own, half), LOW),
            jax.ShapeDtypeStruct((own, half), LOW),
            jax.ShapeDtypeStruct((16, width), WIDE),
        )
        + grads_like,
        in_specs=[IN_SMEM]
        + [whole, whole]
        + [tiles(width, 0, many), tiles(width, many, many)]
        + [tiles(wide), tiles(width), tiles(width), tiles(128)]
        + [IN_ANY] * (2 + len(weights)),
        out_specs=(tiles(width), tiles(half), tiles(half))
        + (pl.BlockSpec((16, width), lambda i: (0, 0)),)
        + (IN_ANY,) * 2,
        scratch_shapes=weight_space(chips, direct, chunks, width)
        + [
            pltpu.VMEM((16, width), WIDE),
            pltpu.VMEM((own, wide), LOW),
            pltpu.VMEM((own, width), LOW),
            pltpu.VMEM((own, width), LOW),
            pltpu.VMEM((own, wide), LOW),
            pltpu.VMEM((own, width), LOW),
            pltpu.SemaphoreType.DMA((2 * chips * (chunks + 4),)),
            pltpu.SemaphoreType.DMA((2,)),
            pltpu.SemaphoreType.DMA((2 * chips * (chunks + 1) + 2 * chunks,)),
        ],
        compiler_params=pltpu.CompilerParams(vmem_limit_bytes=58 << 20),
        cost_estimate=pl.CostEstimate(flops=1, bytes_accessed=1, transcendentals=0),
        name="layer_backward",
    )(at, mixed, other, *grads, slope, *units, scales, hidden, normed, *weights)


def place_of(block, core, z, blocks):
    quarter, row = block // (blocks // 4), block % (blocks // 4)
    a = (quarter & 1) ^ (z & 1)
    return ((quarter >> 1) ^ core) * (blocks // 2) + a * (blocks // 4) + row


def block_at(place, core, z, blocks):
    quarter = 2 * ((place // (blocks // 2)) ^ core) + ((place % (blocks // 2)) // (blocks // 4) ^ (z & 1))
    return quarter * (blocks // 4) + place % (blocks // 4)


def tables(rand, globs, blocks):
    core = lax.axis_index("dp") & 1
    z = lax.axis_index("seq")
    here = block_at(jnp.arange(blocks, dtype=jnp.int32), core, z, blocks)
    heads = rand.shape[0]
    one, two = globs[0], globs[1]

    def near(block):
        return jnp.abs(block - here) <= 1

    every = jnp.ones((heads, blocks), bool)
    ok = [every & (here > 0), every, every & (here < blocks - 1)]
    ok += [every & ~near(one), every & ~near(two) & (one != two)]
    seen = []
    for r in range(3):
        block = rand[:, :, r]
        good = ~near(block) & (block != one) & (block != two)
        for before in seen:
            good = good & (block != before)
        seen.append(block)
        ok.append(good)
    whole_row = (here == one) | (here == two)
    ok = jnp.stack(ok, -1) & ~whole_row[None, :, None]
    bias = jnp.where(ok, 0.0, NEG).astype(WIDE)
    bias = bias.reshape(heads // 2, 2, blocks, SLOTS).transpose(2, 0, 3, 1)
    bias = jnp.repeat(bias, HEAD, axis=3)
    put = partial(place_of, core=core, z=z, blocks=blocks)
    sides = jnp.concatenate([put(jnp.maximum(here - 1, 0)), put(jnp.minimum(here + 1, blocks - 1))])
    return sides, put(rand).reshape(-1), put(globs), bias


def shards(
    inputs,
    cotangent,
    rand_blocks,
    global_blocks,
    w_query,
    b_query,
    w_key,
    w_value,
    b_value,
    w_out,
    b_out,
    gain_one,
    shift_one,
    w_up,
    b_up,
    w_down,
    b_down,
    gain_two,
    shift_two,
):
    n_dp, n_seq = lax.axis_size("dp"), lax.axis_size("seq")
    chips, devices = n_dp // 2, n_dp * n_seq
    core = lax.axis_index("dp") & 1
    z = lax.axis_index("seq")
    device = lax.axis_index("dp") * n_seq + z
    rows_in, width = w_query.shape
    rows_ff, wide = w_down.shape[0], w_up.shape[1]
    chunks = wide // width
    half_width = width // 2
    _, quarter, _ = inputs.shape
    length = quarter * n_seq
    blocks = length // BLOCK
    own = length // 2
    own_heads = HEADS // 2
    span, span_ff = n_seq * rows_in, n_seq * rows_ff
    direct = span % 16 == 0 and chips == chunks

    here = jnp.arange(devices, dtype=jnp.int32)[:, None] == device

    def placed(vector):
        return jnp.where(here, vector[None], jnp.zeros((), LOW)).reshape(-1, width)

    q_line, v_line = placed(b_query), placed(b_value)

    pairs = half_width // 128

    def side(at):
        no_line = jnp.zeros((1, width), LOW)
        parts = []
        for pair in range(pairs):
            first = at * half_width + 128 * pair
            lanes = slice(first, first + 128)
            for w, line in ((w_query, q_line), (w_key, no_line), (w_value, v_line)):
                parts.append(jnp.concatenate([w[:, lanes], line[:, lanes]], 0))
        return jnp.pad(jnp.concatenate(parts, 1), ((0, 7), (0, 0)))

    left, right = side(0), side(1)
    keep = jnp.where(core == 0, left, right)
    come = swap(jnp.where(core == 0, right, left))
    shard = jnp.stack([jnp.where(core == 0, keep, come), jnp.where(core == 0, come, keep)])
    def numbers_of(s):
        numbers = pick(rand_blocks, s, 0).reshape(-1)
        numbers = jnp.concatenate([numbers, pick(global_blocks, s, 0).reshape(-1)])
        return jnp.pad(numbers, (0, -numbers.shape[0] % 128))

    numbers = jnp.stack(bring(numbers_of))
    qkv_z = gather_seq(tie(shard, numbers))

    packed = jnp.concatenate(
        [w_up[:, width * c : width * c + width] for c in range(chunks)]
        + [w_out, w_down]
        + [placed(v) for v in (b_out, gain_one, shift_one, b_down, gain_two, shift_two, b_up)]
        + [jnp.zeros((16 - 6 - chunks, width), LOW)],
        0,
    )
    wide_z = gather_seq(tie(packed, shard), qkv_z[2])
    at = jnp.stack([lax.axis_index("dp") >> 1, core, z]).astype(jnp.int32)

    direct = span % 16 == 0 and chips == chunks
    if direct:
        whole = pack_columns(at, *qkv_z, rows_in)
    else:
        qkv_z = in_seq_order(*qkv_z)
        whole = []
        for k in range(2):
            lines = sum(p[k, rows_in:].astype(WIDE) for p in qkv_z).astype(LOW)
            whole += [p[k, :rows_in] for p in qkv_z] + [lines, jnp.zeros_like(lines)]
        whole = jnp.concatenate(whole, 0).reshape(2, span + 16, 3 * half_width)
    qkv_parts = gather_chips(whole)
    numbers = tie(numbers, whole)
    numbers = jnp.concatenate([numbers, swap(numbers)], 0)
    local_blocks = rand_blocks.shape[2]
    count = HEADS * local_blocks * 3
    globs = numbers[0, count : count + 2]
    rand = numbers[:, :count].reshape(4, HEADS, local_blocks, 3)
    rand = lax.dynamic_slice_in_dim(rand, core * own_heads, own_heads, 1)
    rand = rand.transpose(1, 0, 2, 3).reshape(own_heads, blocks, 3)
    sides, rand, glob_at, bias = tables(rand, globs, blocks)


    tied_inputs = tie(inputs, qkv_z[2])
    pieces = bring(lambda s: pick(tied_inputs, s, 0)[0])

    if direct:
        cut = chunks * span + span // 2
        near, pieces[0], bias, sides, rand, glob_at, *qkv_parts = join(
            wide_z[1], pieces[0], bias, sides, rand, glob_at, *qkv_parts
        )
        whole = pack_rows(at, wide_z[0], near, wide_z[2], chunks + 1, cut)
    else:
        wide_z = in_seq_order(*wide_z)
        rows_a = (chunks + 1) * rows_in
        rows = []
        for c in range(chunks + 1):
            rows += [p[c * rows_in : (c + 1) * rows_in] for p in wide_z]
        rows += [p[rows_a : rows_a + rows_ff] for p in wide_z]
        rows.append(sum(p[rows_a + rows_ff :].astype(WIDE) for p in wide_z).astype(LOW))
        whole = jnp.concatenate(rows, 0)
    if direct:
        lines = sum(jnp.sum(p[:, span].astype(WIDE), 0, keepdims=True) for p in qkv_parts)
        *parts, lines, pieces[0], pieces[1] = join(*gather_quads(*whole), lines, *pieces)
    else:
        parts = gather_chips(tie(whole, qkv_parts))
        lines = sum(jnp.sum(p[:, span].astype(WIDE), 0, keepdims=True) for p in qkv_parts)
    pieces = [*pieces, *(swap(p) for p in pieces)]
    rows_a, rows_b = (chunks + 1) * span, (chunks + 1) * span + span_ff
    if direct:
        qkv_weights = tuple(qkv_parts)
    else:
        ordered = in_chip_order(qkv_parts)
        qkv_weights = (jnp.concatenate([p[k, :span] for p in ordered for k in range(2)], 0),)

    if direct:
        upper, lower = jnp.stack(parts[:2]), jnp.stack(parts[2:])
        parts = [upper, flip_chip(upper, 2), lower, flip_chip(lower, 1)]
        other_parts = [swap(upper), None, swap(lower), None]
    qkv, tokens, w_qkv = project_tokens(at, pieces, lines, qkv_weights, direct)
    mixed, log_total = attend(sides, rand, glob_at, bias, qkv)
    tied = tie(cotangent, qkv)
    first_grads = bring_round(lambda s: pick(tied, s, 0)[0], 0)
    mixed, log_total, first_grads, *parts = join(mixed, log_total, first_grads, *parts)
    other = swap(mixed[own:])
    if direct:
        other_parts[1], other_parts[3] = swap(parts[1]), swap(parts[3])
    else:
        other_parts = [swap(p) for p in parts]
    if direct:
        weights = tuple(parts + other_parts)
    else:
        weights = (
            jnp.stack(
                [
                    in_device_order(
                        *([p[span * c : span * c + span] for p in ps] for ps in (parts, other_parts))
                    )
                    for c in range(chunks + 1)
                ]
            ),
            in_device_order(*([p[rows_a:rows_b] for p in ps] for ps in (parts, other_parts))),
            sum(p[rows_b:].astype(WIDE) for p in parts + other_parts).astype(LOW)[None],
        )
    tied = tie(cotangent, mixed)
    grad_result = first_grads, bring_round(lambda s: pick(tied, s, 0)[0], 1)
    forward = layer_forward(at, mixed, other, tokens, weights, direct, chunks)
    forward, grad_result = join(forward, grad_result)
    result, hidden, slope, normed, unit_one, unit_two, scales = forward
    output = send_back(result)
    backward = layer_backward(
        at,
        mixed,
        other,
        grad_result,
        slope,
        (unit_one, unit_two),
        scales,
        hidden,
        normed,
        weights,
        direct,
    )
    backward, output = join(backward, output)
    grad_first, mine, theirs, in_sums, grad_in, grad_down = backward

    come = swap(theirs)
    if direct:
        chip = lax.axis_index("dp") >> 1
        x, y = chip & 1, chip >> 1
        grad_other, come = join(swap(grad_down), come)
        sums = added(grad_in, grad_other).reshape(2, 2, -1, width)
        cut = chunks * span + span // 2
        upper, lower = sums[:, :, :cut], sums[:, :, cut:]
        moves = [pick(upper, x, 1), pick(upper, 1 - x, 1), pick(lower, y, 0), pick(lower, 1 - y, 0)]
        mine, come, *moves = join(mine, come, *moves)
        moves[1], moves[3] = flip_chip(moves[1], 1), flip_chip(moves[3], 2)
    grad_qkv, grad_own, grad_theirs, sums = attend_back(
        sides,
        rand,
        glob_at,
        bias,
        log_total,
        qkv,
        mine,
        come,
        w_qkv,
        grad_first,
    )
    if direct:
        grad_qkv, grad_own, grad_theirs, sums, *moves = join(grad_qkv, grad_own, grad_theirs, sums, *moves)
    come_rows = swap(grad_theirs)
    if direct:
        upper, lower = added(*moves[:2]), added(*moves[2:])
        moves = [pick(upper, y, 0), pick(upper, 1 - y, 0), pick(lower, x, 1), pick(lower, 1 - x, 1)]
        grad_own, *moves = join(grad_own, *(move.reshape(-1, width) for move in moves))
        moves[1], moves[3] = flip_chip(moves[1], 2), flip_chip(moves[3], 1)
    grad_tokens = added(grad_own, come_rows)
    grad_tokens, grad_qkv = join(grad_tokens, grad_qkv)
    grad_inputs = start_back(grad_tokens)
    first_back = finish_back(grad_inputs, 0)
    grad_w_qkv = dot(tokens, grad_qkv, TN).astype(LOW)
    vectors = in_sums[: 6 + chunks].reshape(-1)
    vectors = jnp.pad(vectors, (0, -vectors.shape[0] % (3 * half_width))).reshape(-1, 3 * half_width)
    lines = jnp.concatenate([sums, vectors], 0).astype(LOW)
    lines = jnp.broadcast_to(lines, (chips, 2, n_seq) + lines.shape)
    parts = jnp.concatenate(
        [grad_w_qkv.reshape(chips, 2, n_seq, rows_in, 3 * half_width), lines], 3
    )
    keep, come = (pick(parts, which, 1)[:, 0] for which in (core, 1 - core))
    come = swap(come)
    parts = jnp.stack([keep, come], 1)
    if direct:
        first_back, *moves = join(first_back, *moves)
        near_sums, keep_sums = unpack_rows(at, moves[:2], moves[2:], chunks + 1)
    else:
        rows = lax.psum_scatter(grad_in, "dp", scatter_dimension=1, tiled=True)
        rows = rows.reshape((chunks + 1) * span, width)
        down = lax.psum_scatter(grad_down, "dp", scatter_dimension=0, tiled=True)
        near_sums, keep_sums = unpack_rows(at, [rows], [down], chunks + 1)
    grad_inputs = first_back, finish_back(grad_inputs, 1)
    near_sums = flip_seq(near_sums, 1)
    parts = reduce_chips(parts)
    parts, near_sums = join(parts, near_sums)
    own_qkv = reduce_seq(parts.transpose(1, 0, 2, 3))
    keep, come = own_qkv[0], own_qkv[1]
    left, right = jnp.where(core == 0, keep, come), jnp.where(core == 0, come, keep)

    mirror = flip_seq(added(keep_sums[1], near_sums[1]), 3)
    own_sums = sum(p.astype(WIDE) for p in (keep_sums[0], near_sums[0], mirror))
    rows_a = (chunks + 1) * rows_in
    own_up = jnp.concatenate(
        [own_sums[c * rows_in : (c + 1) * rows_in] for c in range(chunks)], 1
    )
    small = (keep + come)[rows_in + 1 :].reshape(-1)[: (6 + chunks) * width].reshape(-1, width)

    def joined(k, rows):
        lanes = [lanes_of(k, pair) for pair in range(pairs)]
        return jnp.concatenate([one[rows, at] for one in (left, right) for at in lanes], 1)

    def own_part(vector, size):
        return lax.dynamic_slice_in_dim(vector.reshape(-1), device * size, size, 0)

    six = lax.dynamic_slice_in_dim(small[:6], device * rows_in, rows_in, 1)

    matrix_rows, line = slice(0, rows_in), slice(rows_in, rows_in + 1)
    return (
        in_sequences(output),
        in_sequences(grad_inputs),
        joined(0, matrix_rows),
        own_part(joined(0, line), rows_in),
        joined(1, matrix_rows),
        joined(2, matrix_rows),
        own_part(joined(2, line), rows_in),
        own_sums[chunks * rows_in : rows_a],
        six[0],
        six[1],
        six[2],
        own_up,
        own_part(small[6 : 6 + chunks], rows_ff),
        own_sums[rows_a : rows_a + rows_ff],
        six[3],
        six[4],
        six[5],
    )


def solution(mesh):
    both = ("dp", "seq")
    matrix, vector = P(both, None), P(both)
    tokens = P("dp", "seq", None)
    return jax.shard_map(
        shards,
        mesh=mesh,
        in_specs=(tokens, tokens, P("dp", None, "seq", None), P("dp", None))
        + (matrix, vector, matrix, matrix, vector, matrix, vector, vector, vector)
        + (matrix, vector, matrix, vector, vector, vector),
        out_specs=(tokens, tokens)
        + (matrix, vector, matrix, matrix, vector, matrix, vector, vector, vector)
        + (matrix, vector, matrix, vector, vector, vector),
        check_vma=False,
    )
```

```python
from functools import partial

import jax
import jax.numpy as jnp
from jax import lax
from jax.experimental import pallas as pl
from jax.experimental.pallas import tpu as pltpu
from jax.sharding import PartitionSpec as P

HEADS = 12
HEAD = 64
BLOCK = 64
SLOTS = 8
EPS = 1e-06
NEG = -1e30
LOW = jnp.bfloat16
WIDE = jnp.float32

NT = (((1,), (1,)), ((), ()))
TN = (((0,), (0,)), ((), ()))
NN = (((1,), (0,)), ((), ()))


def dot(left, right, dims):
    return lax.dot_general(left, right, dims, preferred_element_type=WIDE)


def swap(array):
    size = lax.axis_size("dp")
    return lax.ppermute(array, "dp", [(i, i ^ 1) for i in range(size)])


def flip_seq(array, k):
    size = lax.axis_size("seq")
    return lax.ppermute(array, "seq", [(i, i ^ k) for i in range(size)])


def rounds():
    dp, seq = lax.axis_size("dp"), lax.axis_size("seq")
    for a in range(2):
        pairs = []
        for d in range(dp):
            for z in range(seq):
                to_dp = (d & ~1) | (z >> 1)
                to_seq = 2 * (d & 1) + (a ^ (z & 1))
                pairs.append((d * seq + z, to_dp * seq + to_seq))
        yield a, pairs


def bring_round(piece_of, which):
    a, pairs = list(rounds())[which]
    z = lax.axis_index("seq")
    return lax.ppermute(piece_of(a ^ (z & 1)), ("dp", "seq"), pairs)


def bring(piece_of):
    return [bring_round(piece_of, which) for which in range(2)]


def start_back(rows):
    size = rows.shape[0] // 2
    return [rows[size * a : size * a + size] for a in range(2)]


def finish_back(parts, which):
    a, pairs = list(rounds())[which]
    return lax.ppermute(parts[a], ("dp", "seq"), [(t, s) for s, t in pairs])


def send_back(rows):
    parts = start_back(rows)
    return [finish_back(parts, a) for a in range(2)]


def in_sequences(got):
    odd = (lax.axis_index("seq") & 1) == 1
    return jnp.stack([jnp.where(odd, got[1], got[0]), jnp.where(odd, got[0], got[1])])


def pick(array, index, axis):
    return lax.dynamic_slice_in_dim(array, index, 1, axis)


def gather_seq(shard, before=None):
    mirror = flip_seq(shard, 3)
    pair = jnp.stack([shard, mirror])
    if before is not None:
        pair = tie(pair, before)
    return shard, flip_seq(pair, 1), mirror


def in_seq_order(shard, near, mirror):
    z = lax.axis_index("seq")
    pieces = [shard, near[0], near[1], mirror]
    for bit in range(2):
        set_bit = ((z >> bit) & 1) == 1
        pieces = [
            jnp.where(set_bit, pieces[i ^ (1 << bit)], pieces[i]) for i in range(len(pieces))
        ]
    return pieces


def chip_groups():
    count = (lax.axis_size("dp") // 2).bit_length() - 1
    return [(bit, min(2, count - bit)) for bit in range(0, count, 2)]


def flip_chip(array, away):
    size = lax.axis_size("dp")
    return lax.ppermute(array, "dp", [(i, i ^ (2 * away)) for i in range(size)])


def gather_chips(part):
    parts = [part]
    for bit, bits in chip_groups():
        parts = parts + [flip_chip(p, k << bit) for k in range(1, 1 << bits) for p in parts]
    return parts


def in_chip_order(parts):
    chip = lax.axis_index("dp") >> 1
    parts = jnp.stack(parts)
    return [pick(parts, q ^ chip, 0)[0] for q in range(parts.shape[0])]


def in_device_order(mine, theirs):
    core = lax.axis_index("dp") & 1
    parts = []
    for own, other in zip(in_chip_order(mine), in_chip_order(theirs)):
        parts += [jnp.where(core == 0, own, other), jnp.where(core == 0, other, own)]
    return jnp.concatenate(parts, 0)


def join(*values):
    return lax.optimization_barrier(values)


def gather_quads(upper, lower):
    return [upper, flip_chip(upper, 1), lower, flip_chip(lower, 2)]


def tie(values, *others):
    return lax.optimization_barrier((values, others))[0]


def added(*arrays):
    return sum(array.astype(WIDE) for array in arrays).astype(LOW)


def reduce_chips(parts):
    chip = lax.axis_index("dp") >> 1
    for bit, bits in chip_groups():
        ways = 1 << bits
        parts = parts.reshape((-1, ways) + parts.shape[1:])
        mine = (chip >> bit) & (ways - 1)
        others = [flip_chip(pick(parts, mine ^ k, 1)[:, 0], k << bit) for k in range(1, ways)]
        parts = added(pick(parts, mine, 1)[:, 0], *others)
    return parts[0]


def reduce_seq(parts):
    z = lax.axis_index("seq")
    near = flip_seq(jnp.concatenate([pick(parts, z ^ 1, 0), pick(parts, z ^ 2, 0)], 0), 1)
    mirror = added(pick(parts, z ^ 3, 0)[0], near[1])
    return pick(parts, z, 0)[0].astype(WIDE) + near[0].astype(WIDE) + flip_seq(mirror, 3).astype(WIDE)


def norm_parts(summed):
    center = summed - jnp.mean(summed, -1, keepdims=True)
    spread = jnp.mean(center * center, -1, keepdims=True)
    scale = lax.rsqrt(spread + EPS)
    return center * scale, scale


def norm_back(grad, unit, scale, gain):
    grad_unit = grad * gain
    mean_one = jnp.mean(grad_unit, -1, keepdims=True)
    mean_two = jnp.mean(grad_unit * unit, -1, keepdims=True)
    return scale * (grad_unit - mean_one - unit * mean_two)


def gelu_parts(x):
    size = jnp.abs(x)
    t = 1.0 / (1.0 + (0.3275911 * 0.5**0.5) * size)
    bell = jnp.exp(-0.5 * x * x)
    series = 0.5 * 1.061405429
    for factor in (-1.453152027, 1.421413741, -0.284496736, 0.254829592):
        series = series * t + 0.5 * factor
    tail = series * t * bell
    share = jnp.where(x >= 0, 1.0 - tail, tail)
    return x * share, share + x * bell * 0.3989422804014327


def block_rows(ref, block, lanes):
    return ref[pl.ds(pl.multiple_of(block * BLOCK, BLOCK), BLOCK), lanes]


def diagonal(pair_rows, low):
    zero = jnp.zeros_like(pair_rows)
    return jnp.concatenate(
        [jnp.where(low, pair_rows, zero), jnp.where(low, zero, pair_rows)], axis=0
    )


def gather_blocks(ref, ids, lanes, low):
    parts = []
    for one, two in ids:
        if two is None:
            parts.append(block_rows(ref, one, lanes))
        else:
            parts.append(
                jnp.where(low, block_rows(ref, one, lanes), block_rows(ref, two, lanes))
            )
    return jnp.concatenate(parts, axis=0)


def slot_ids(near_ref, rand_ref, globs, i, head, blocks):
    ids = [(near_ref[i], None), (i, None), (near_ref[blocks + i], None)]
    ids += [(globs[0], None), (globs[1], None)]
    for r in range(3):
        ids.append(
            (
                rand_ref[(head * blocks + i) * 3 + r],
                rand_ref[((head + 1) * blocks + i) * 3 + r],
            )
        )
    return ids


def lanes_of(part, pair):
    first = 128 * (3 * pair + part)
    return slice(first, first + 128)


def flat_lanes(pair):
    return slice(128 * pair, 128 * pair + 128)


def start_copies(copies, sems):
    started = [
        pltpu.make_async_copy(source, target, sems.at[k])
        for k, (source, target) in enumerate(copies)
    ]
    for copy in started:
        copy.start()
    return started


def project_kernel(chips, direct, at_ref, *refs):
    pieces, b_ref = refs[:4], refs[4]
    sources, (qkv_ref, tokens_ref, w_ref, sems) = refs[5:-4], refs[-4:]
    if direct:
        span = w_ref.shape[0] // (2 * chips)
        copies = [
            (
                sources[away].at[k, :span],
                w_ref.at[pl.ds(pl.multiple_of((2 * (at_ref[0] ^ away) + k) * span, span), span)],
            )
            for away in range(chips)
            for k in range(2)
        ]
    else:
        copies = [(sources[0], w_ref)]

    @pl.when(pl.program_id(0) == 0)
    def _():
        for copy in start_copies(copies, sems):
            copy.wait()

    lane = lax.broadcasted_iota(jnp.int32, (1, w_ref.shape[1]), 1)
    scale = jnp.where(lane % 384 < 128, HEAD ** (-0.5), 1.0)
    at = pl.program_id(0) * len(pieces) // pl.num_programs(0)
    rows = pieces[0][...]
    for k in range(1, len(pieces)):
        rows = jnp.where(at == k, pieces[k][...], rows)
    tokens_ref[...] = rows
    values = (dot(rows, w_ref[...], NN) + b_ref[...]).astype(LOW).astype(WIDE)
    qkv_ref[...] = (values * scale).astype(LOW)


def with_sems(groups, sems):
    done, copies = 0, []
    for group in groups:
        copies.append([pltpu.make_async_copy(*pair, sems.at[done + k]) for k, pair in enumerate(group)])
        done += len(group)
    return copies


def attend_kernel(
    pairs, blocks, step, near_ref, rand_ref, glob_ref, bias_ref, qkv_ref, out_ref, log_ref
):
    low = lax.broadcasted_iota(jnp.int32, (1, 2 * HEAD), 1) < HEAD
    globs = (glob_ref[0], glob_ref[1])

    def scores_of(i, pair):
        ids = slot_ids(near_ref, rand_ref, globs, i, 2 * pair, blocks)
        queries = diagonal(block_rows(qkv_ref, i, lanes_of(0, pair)), low)
        return dot(gather_blocks(qkv_ref, ids, lanes_of(1, pair), low), queries, NT)

    def softmax_of(i, pair, scores):
        highest = jnp.max(scores, axis=0, keepdims=True)
        weights = jnp.exp(scores - highest)
        total = jnp.sum(weights, axis=0, keepdims=True)
        log_ref[i, pair : pair + 1] = highest + jnp.log(total)
        return (weights * (1.0 / total)).astype(LOW)

    def put(i, pair, mixed):
        at = pl.ds(pl.multiple_of(i * BLOCK, BLOCK), BLOCK)
        out_ref[at, flat_lanes(pair)] = jnp.where(low, mixed[:BLOCK], mixed[BLOCK:]).astype(LOW)

    def body(at, carry):
        units = [(at * step + d, pair) for d in range(step) for pair in range(pairs)]
        scores = [scores_of(*unit) for unit in units]
        probs = []
        for (i, pair), score in zip(units, scores):
            bias = bias_ref[i, pair]
            score = jnp.concatenate(
                [score[BLOCK * j : BLOCK * j + BLOCK] + bias[j : j + 1] for j in range(SLOTS)],
                axis=0,
            )
            probs.append(softmax_of(i, pair, score))
        for (i, pair), prob in zip(units, probs):
            ids = slot_ids(near_ref, rand_ref, globs, i, 2 * pair, blocks)
            values = gather_blocks(qkv_ref, ids, lanes_of(2, pair), low)
            put(i, pair, dot(prob, values, TN))
        return carry

    lax.fori_loop(0, blocks // step, body, 0)

    def whole_row(n, carry):
        i = glob_ref[n]
        scores = []
        for pair in range(pairs):
            queries = diagonal(block_rows(qkv_ref, i, lanes_of(0, pair)), low)
            scores.append(dot(qkv_ref[:, lanes_of(1, pair)], queries, NT))
        probs = [softmax_of(i, pair, scores[pair]) for pair in range(pairs)]
        for pair in range(pairs):
            put(i, pair, dot(probs[pair], qkv_ref[:, lanes_of(2, pair)], TN))
        return carry

    lax.fori_loop(0, 2, whole_row, 0)


def attend_back_kernel(
    blocks,
    step,
    near_ref,
    rand_ref,
    glob_ref,
    bias_ref,
    log_ref,
    qkv_ref,
    mine_ref,
    come_ref,
    w_ref,
    grad_first_ref,
    out_ref,
    rows_own_ref,
    rows_other_ref,
    sums_ref,
    grad_ref,
    acc_ref,
):
    low = lax.broadcasted_iota(jnp.int32, (1, 2 * HEAD), 1) < HEAD
    globs = (glob_ref[0], glob_ref[1])
    acc_ref[...] = jnp.zeros_like(acc_ref)
    half = mine_ref.shape[0]
    grad_ref[:half] = mine_ref[...]
    grad_ref[half:] = come_ref[...]
    pairs = mine_ref.shape[1] // 128

    def source(pair, part):
        return qkv_ref.at[:, lanes_of(part, pair)]

    def log_of(i, pair):
        return log_ref[i, pair : pair + 1]

    every = slice(None)

    def add(part, pair, block, value):
        at = pl.ds(pl.multiple_of(block * BLOCK, BLOCK), BLOCK)
        lanes = flat_lanes(2 * pair + part)
        acc_ref[at, lanes] = acc_ref[at, lanes] + value

    def operands(i, pair):
        queries = diagonal(block_rows(source(pair, 0), i, every), low)
        grads = diagonal(block_rows(grad_ref, i, flat_lanes(pair)), low)
        return queries, grads

    def softmax_back(prob, grad_prob):
        scaled = prob * grad_prob
        inner = jnp.sum(scaled, axis=0, keepdims=True)
        return prob.astype(LOW), (scaled - prob * inner).astype(LOW)

    def put(i, pair, mixed):
        at = pl.ds(pl.multiple_of(i * BLOCK, BLOCK), BLOCK)
        out_ref[at, lanes_of(0, pair)] = (
            jnp.where(low, mixed[:BLOCK], mixed[BLOCK:]) * HEAD ** (-0.5)
        ).astype(LOW)

    def body(at, carry):
        units = [(at * step + d, pair) for d in range(step) for pair in range(pairs)]
        first = []
        for i, pair in units:
            ids = slot_ids(near_ref, rand_ref, globs, i, 2 * pair, blocks)
            queries, grads = operands(i, pair)
            first.append(
                (
                    dot(gather_blocks(source(pair, 1), ids, every, low), queries, NT),
                    dot(gather_blocks(source(pair, 2), ids, every, low), grads, NT),
                )
            )
        second = []
        for (i, pair), (score, grad_prob) in zip(units, first):
            shift = bias_ref[i, pair] - log_of(i, pair)
            prob = jnp.concatenate(
                [
                    jnp.exp(score[BLOCK * j : BLOCK * j + BLOCK] + shift[j : j + 1])
                    for j in range(SLOTS)
                ],
                axis=0,
            )
            second.append(softmax_back(prob, grad_prob))
        third = []
        for (i, pair), (prob, grad_score) in zip(units, second):
            ids = slot_ids(near_ref, rand_ref, globs, i, 2 * pair, blocks)
            queries, grads = operands(i, pair)
            keys = gather_blocks(source(pair, 1), ids, every, low)
            put(i, pair, dot(grad_score, keys, TN))
            third.append((dot(grad_score, queries, NN), dot(prob, grads, NN)))
        for (i, pair), values in zip(units, third):
            ids = slot_ids(near_ref, rand_ref, globs, i, 2 * pair, blocks)
            for j, (one, two) in enumerate(ids):
                for part, value in enumerate(values):
                    value = value[BLOCK * j : BLOCK * j + BLOCK]
                    if two is None:
                        add(part, pair, one, value)
                    else:
                        add(part, pair, one, jnp.where(low, value, 0.0))
                        add(part, pair, two, jnp.where(low, 0.0, value))
        return carry

    lax.fori_loop(0, blocks // step, body, 0)

    def whole_row(n, carry):
        i = glob_ref[n]
        first = []
        for pair in range(pairs):
            queries, grads = operands(i, pair)
            first.append(
                (
                    dot(source(pair, 1)[...], queries, NT),
                    dot(source(pair, 2)[...], grads, NT),
                )
            )
        second = []
        for pair, (score, grad_prob) in enumerate(first):
            prob = jnp.exp(score - log_of(i, pair))
            second.append(softmax_back(prob, grad_prob))
        for pair, (prob, grad_score) in enumerate(second):
            queries, grads = operands(i, pair)
            acc_ref[:, flat_lanes(2 * pair)] += dot(grad_score, queries, NN)
            acc_ref[:, flat_lanes(2 * pair + 1)] += dot(prob, grads, NN)
            put(i, pair, dot(grad_score, source(pair, 1)[...], TN))
        return carry

    lax.fori_loop(0, jnp.where(globs[0] == globs[1], 1, 2), whole_row, 0)
    for pair in range(pairs):
        out_ref[:, 384 * pair + 128 : 384 * pair + 384] = acc_ref[
            :, 256 * pair : 256 * pair + 256
        ].astype(LOW)

    sums_ref[...] = jnp.zeros_like(sums_ref)
    tile = 512
    for side, rows_ref in enumerate((rows_own_ref, rows_other_ref)):

        def token_rows(at, carry, side=side, rows_ref=rows_ref):
            grads = out_ref[pl.ds(pl.multiple_of(side * half + at * tile, tile), tile)]
            sums_ref[...] += jnp.sum(grads.astype(WIDE), 0, keepdims=True)
            rows = pl.ds(pl.multiple_of(at * tile, tile), tile)
            total = dot(grads, w_ref[...], NT)
            if side == 0:
                total = total + grad_first_ref[rows].astype(WIDE)
            rows_ref[rows] = total.astype(LOW)
            return carry

        lax.fori_loop(0, half // tile, token_rows, 0)


def pack_kernel(seq, chunks, cut, at_ref, shard_ref, near_ref, mirror_ref, upper_ref, lower_ref):
    rows = shard_ref.shape[0] - 16
    rows_in = rows // (chunks + 4)
    rows_ff = rows - chunks * rows_in
    pieces = [shard_ref, near_ref.at[0], near_ref.at[1], mirror_ref]
    total = sum(piece[rows:].astype(WIDE) for piece in pieces)

    def put(first, value):
        target, first = (upper_ref, first) if first < cut else (lower_ref, first - cut)
        target[first : first + value.shape[0]] = value

    put(rows * seq, total.astype(LOW))
    for z in range(seq):

        @pl.when(at_ref[2] == z)
        def _(z=z):
            for k, piece in enumerate(pieces):
                for c in range(chunks):
                    put((c * seq + (z ^ k)) * rows_in, piece[c * rows_in : c * rows_in + rows_in])
                put(chunks * seq * rows_in + (z ^ k) * rows_ff, piece[chunks * rows_in : rows])


def pack_columns_kernel(seq, rows_in, at_ref, shard_ref, near_ref, mirror_ref, out_ref):
    pieces = [shard_ref, near_ref.at[0], near_ref.at[1], mirror_ref]
    total = sum(piece[:, rows_in:].astype(WIDE) for piece in pieces).astype(LOW)
    out_ref[:, seq * rows_in :] = jnp.concatenate([total, jnp.zeros_like(total)], 1)
    for z in range(seq):

        @pl.when(at_ref[2] == z)
        def _(z=z):
            for k, piece in enumerate(pieces):
                first = (z ^ k) * rows_in
                out_ref[:, first : first + rows_in] = piece[:, :rows_in]


def unpack_kernel(seq, chunks, many, at_ref, *refs):
    sources, (near_ref, keep_ref) = refs[:-2], refs[-2:]
    rows = near_ref.shape[1]
    rows_in = rows // (chunks + 4)
    rows_ff = rows - chunks * rows_in

    cut = sources[0].shape[0]

    def total(first, size):
        refs, first = (sources[:many], first) if first < cut else (sources[many:], first - cut)
        return sum(ref[first : first + size].astype(WIDE) for ref in refs).astype(LOW)

    for z in range(seq):

        @pl.when(at_ref[2] == z)
        def _(z=z):
            for k in range(seq):
                target = (keep_ref, near_ref)[k in (1, 2)].at[int(k > 1)]
                for c in range(chunks):
                    part = total((c * seq + (z ^ k)) * rows_in, rows_in)
                    target[c * rows_in : c * rows_in + rows_in] = part
                target[chunks * rows_in :] = total(chunks * seq * rows_in + (z ^ k) * rows_ff, rows_ff)


def weight_copies(chips, direct, chip, core, sources, w_in_ref, w_down_ref, lines_ref):
    if not direct:
        return [(sources[0], w_in_ref), (sources[2], lines_ref)], [], [(sources[1], w_down_ref)]
    wide, width = w_down_ref.shape
    chunks = wide // width
    span, span_ff = width // (2 * chips), wide // (2 * chips)
    cut = span // 2
    groups = [], [], []
    for k in range(2):
        for away in range(chips):
            place = 2 * (chip ^ away) + (core if k == 0 else 1 - core)
            upper = sources[4 * k + (away >> 1)].at[away & 1]
            lower = sources[4 * k + 2 + (away & 1)].at[away >> 1]
            rows = pl.ds(pl.multiple_of(place * span, span), span)
            groups[1].extend(
                (upper.at[span * c : span * c + span], w_in_ref.at[c, rows]) for c in range(chunks)
            )
            for half, source in enumerate((upper.at[span * chunks :], lower.at[:cut])):
                rows = pl.ds(pl.multiple_of(place * span + half * cut, cut), cut)
                groups[0].append((source, w_in_ref.at[chunks, rows]))
            rows = pl.ds(pl.multiple_of(place * span_ff, span_ff), span_ff)
            groups[2].append((lower.at[cut : cut + span_ff], w_down_ref.at[rows]))
            groups[0].append((lower.at[cut + span_ff :], lines_ref.at[k * chips + away]))
    return groups


def forward_kernel(
    chips,
    direct,
    at_ref,
    mixed_ref,
    other_ref,
    tokens_ref,
    *refs,
):
    sources, refs = refs[:-11], refs[-11:]
    output_ref, hidden_ref, slope_ref, normed_ref, unit_one_ref, unit_two_ref, scales_ref = refs[:7]
    w_in_ref, w_down_ref, lines_ref, sems = refs[7:]
    wide, width = w_down_ref.shape
    half, chunks = width // 2, wide // width
    core = at_ref[1]
    groups = weight_copies(chips, direct, at_ref[0], core, sources, w_in_ref, w_down_ref, lines_ref)
    groups = with_sems(groups, sems)

    @pl.when(pl.program_id(0) == 0)
    def _():
        for copy in sum(groups, []):
            copy.start()
        for copy in groups[0]:
            copy.wait()

    vectors = jnp.sum(lines_ref[...].astype(WIDE), 0)
    b_out, gain_one, shift_one, b_down, gain_two, shift_two = (vectors[k : k + 1] for k in range(6))
    here = pl.ds(pl.multiple_of(core * half, 128), half)
    there = pl.ds(pl.multiple_of((1 - core) * half, 128), half)
    branch = dot(mixed_ref[...], w_in_ref[chunks, here], NN) + dot(other_ref[...], w_in_ref[chunks, there], NN)
    unit_one, scale_one = norm_parts(tokens_ref[...].astype(WIDE) + (branch + b_out))
    normed = unit_one * gain_one + shift_one
    normed_low = normed.astype(LOW)
    normed_ref[...] = normed_low
    unit_one_ref[...] = unit_one

    @pl.when(pl.program_id(0) == 0)
    def _():
        for copy in groups[1] + groups[2]:
            copy.wait()

    down = b_down
    for c in range(0, chunks, 2):
        lanes = slice(width * c, width * c + 2 * width)
        weights = jnp.concatenate([w_in_ref[c], w_in_ref[c + 1]], 1)
        bias = jnp.concatenate([vectors[6 + c : 7 + c], vectors[7 + c : 8 + c]], 1)
        hidden, slope = gelu_parts(dot(normed_low, weights, NN) + bias)
        hidden = hidden.astype(LOW)
        hidden_ref[:, lanes] = hidden
        slope_ref[:, lanes] = slope.astype(LOW)
        down = down + dot(hidden, w_down_ref[lanes], NN)
    unit_two, scale_two = norm_parts(normed + down)
    output_ref[...] = (unit_two * gain_two + shift_two).astype(LOW)
    lane = lax.broadcasted_iota(jnp.int32, (1, 128), 1)
    scales_ref[...] = jnp.where(lane < 64, scale_one, scale_two)
    unit_two_ref[...] = unit_two


def backward_kernel(
    tile,
    chips,
    direct,
    at_ref,
    mixed_ref,
    other_ref,
    grad_first_ref,
    grad_last_ref,
    slope_ref,
    unit_one_ref,
    unit_two_ref,
    scales_ref,
    hidden_hbm,
    normed_hbm,
    *refs,
):
    sources, refs = refs[:-18], refs[-18:]
    first_ref, mine_ref, theirs_ref, sums_ref, *grad_refs = refs[:6]
    w_in_ref, w_down_ref, lines_ref, vectors_ref, pre_ref, branch_ref = refs[6:12]
    normed_ref, hidden_ref, down_ref, sems, extra_sems, out_sems = refs[12:]
    own, width = normed_ref.shape
    wide = w_down_ref.shape[0]
    half, chunks = width // 2, wide // width
    chip, core = at_ref[0], at_ref[1]
    at, last = pl.program_id(0), pl.num_programs(0) - 1
    rows = pl.ds(pl.multiple_of(at * tile, tile), tile)
    groups = weight_copies(chips, direct, chip, core, sources, w_in_ref, w_down_ref, lines_ref)
    groups = with_sems(groups, sems)
    extra = [
        pltpu.make_async_copy(hidden_hbm, hidden_ref, extra_sems.at[0]),
        pltpu.make_async_copy(normed_hbm, normed_ref, extra_sems.at[1]),
    ]
    here = pl.ds(pl.multiple_of(core * half, 128), half)
    there = pl.ds(pl.multiple_of((1 - core) * half, 128), half)

    @pl.when(at == 0)
    def _():
        for copy in groups[2] + groups[1] + groups[0]:
            copy.start()
        for copy in extra:
            copy.start()
        sums_ref[...] = jnp.zeros_like(sums_ref)
        for copy in groups[2] + groups[1] + groups[0]:
            copy.wait()
        vectors_ref[...] = jnp.sum(lines_ref[...].astype(WIDE), 0)

    def add_sum(k, value):
        sums_ref[k : k + 1] += jnp.sum(value, 0, keepdims=True)

    grad = jnp.where(2 * at <= last, grad_first_ref[...], grad_last_ref[...]).astype(WIDE)
    unit_two = unit_two_ref[...]
    add_sum(4, grad * unit_two)
    add_sum(5, grad)
    grad_normed = norm_back(grad, unit_two, scales_ref[:, 64:65], vectors_ref[4:5])
    grad_down = grad_normed.astype(LOW)
    down_ref[rows] = grad_down
    add_sum(3, grad_down.astype(WIDE))
    for c in range(chunks):
        lanes = slice(width * c, width * c + width)
        grad_pre = dot(grad_down, w_down_ref[lanes], NT) * slope_ref[:, lanes].astype(WIDE)
        grad_pre = grad_pre.astype(LOW)
        pre_ref[rows, lanes] = grad_pre
        add_sum(6 + c, grad_pre.astype(WIDE))
        grad_normed = grad_normed + dot(grad_pre, w_in_ref[c], NT)
    unit_one = unit_one_ref[...]
    add_sum(1, grad_normed * unit_one)
    add_sum(2, grad_normed)
    grad_branch = norm_back(grad_normed, unit_one, scales_ref[:, 0:1], vectors_ref[1:2]).astype(LOW)
    first_ref[...] = grad_branch
    branch_ref[rows] = grad_branch
    add_sum(0, grad_branch.astype(WIDE))
    mine_ref[...] = dot(grad_branch, w_in_ref[chunks, here], NT).astype(LOW)
    theirs_ref[...] = dot(grad_branch, w_in_ref[chunks, there], NT).astype(LOW)

    @pl.when(at == last)
    def _():
        for copy in extra:
            copy.wait()
        moving = []
        span, span_ff = width // (2 * chips), wide // (2 * chips)
        first = span * (chunks + 1)

        def leave(pairs):
            for source, target in pairs:
                copy = pltpu.make_async_copy(source, target, out_sems.at[len(moving)])
                copy.start()
                moving.append(copy)

        def leave_rows(c):
            if not direct:
                return leave([(w_in_ref.at[c], grad_refs[0].at[c])])
            for k, target in enumerate(grad_refs):
                for q in range(chips):
                    place = 2 * q + (core if k == 0 else 1 - core)
                    source = w_in_ref.at[c, pl.ds(pl.multiple_of(place * span, span), span)]
                    leave([(source, target.at[q, span * c : span * c + span])])

        for c in range(chunks):
            lanes = slice(width * c, width * c + width)
            w_down_ref[lanes] = dot(hidden_ref[:, lanes], down_ref[...], TN).astype(LOW)
            if direct:
                for k, target in enumerate(grad_refs):
                    place = 2 * c + (core if k == 0 else 1 - core)
                    source = w_down_ref.at[pl.ds(pl.multiple_of(place * span_ff, span_ff), span_ff)]
                    leave([(source, target.at[c, first : first + span_ff])])
            else:
                leave([(w_down_ref.at[lanes], grad_refs[1].at[lanes])])
            w_in_ref[c] = dot(normed_ref[...], pre_ref[:, lanes], TN).astype(LOW)
            leave_rows(c)
        w_in_ref[chunks, here] = dot(mixed_ref[...], branch_ref[...], TN).astype(LOW)
        w_in_ref[chunks, there] = dot(other_ref[...], branch_ref[...], TN).astype(LOW)
        leave_rows(chunks)
        for copy in moving:
            copy.wait()


IN_SMEM = pl.BlockSpec(memory_space=pltpu.SMEM)
IN_VMEM = pl.BlockSpec(memory_space=pltpu.VMEM)


IN_ANY = pl.BlockSpec(memory_space=pl.ANY)


TILE = 256


def tiles(width, first=0, many=None):
    if many is None:
        return pl.BlockSpec((TILE, width), lambda i: (i, 0))
    return pl.BlockSpec((TILE, width), lambda i: (jnp.clip(i - first, 0, many - 1), 0))


def project_tokens(at, pieces, b_qkv, weights, direct):
    length, width = 4 * pieces[0].shape[0], pieces[0].shape[1]
    half = width // 2
    chips = lax.axis_size("dp") // 2
    many = pieces[0].shape[0] // TILE

    def all_of(*shape):
        return pl.BlockSpec(shape, lambda i: (0, 0))

    return pl.pallas_call(
        partial(project_kernel, chips, direct),
        grid=(length // TILE,),
        out_shape=(
            jax.ShapeDtypeStruct((length, 3 * half), LOW),
            jax.ShapeDtypeStruct((length, width), LOW),
            jax.ShapeDtypeStruct((width, 3 * half), LOW),
        ),
        in_specs=[IN_SMEM]
        + [tiles(width, many * k, many) for k in range(4)]
        + [all_of(1, 3 * half)]
        + [IN_ANY] * len(weights),
        out_specs=(tiles(3 * half), tiles(width), all_of(width, 3 * half)),
        scratch_shapes=[pltpu.SemaphoreType.DMA((2 * chips,))],
        compiler_params=pltpu.CompilerParams(vmem_limit_bytes=48 << 20),
        cost_estimate=pl.CostEstimate(flops=1, bytes_accessed=1, transcendentals=0),
        name="project",
    )(at, *pieces, b_qkv, *weights)


def attend(near, rand, globs, bias, qkv):
    length, width = qkv.shape
    pairs, blocks = width // 384, length // BLOCK
    return pl.pallas_call(
        partial(attend_kernel, pairs, blocks, 4),
        out_shape=(
            jax.ShapeDtypeStruct((length, 128 * pairs), LOW),
            jax.ShapeDtypeStruct((blocks, 8, 128), WIDE),
        ),
        in_specs=[IN_SMEM] * 3 + [IN_VMEM] * 2,
        out_specs=(IN_VMEM,) * 2,
        compiler_params=pltpu.CompilerParams(vmem_limit_bytes=48 << 20),
        cost_estimate=pl.CostEstimate(flops=1, bytes_accessed=1, transcendentals=0),
        name="attend",
    )(near, rand, globs, bias, qkv)


def attend_back(near, rand, globs, bias, log_total, qkv, mine, come, w_qkv, grad_first):
    length, (wide, width) = qkv.shape[0], w_qkv.shape
    pairs, blocks = width // 384, length // BLOCK
    rows = jax.ShapeDtypeStruct((length // 2, wide), LOW)
    return pl.pallas_call(
        partial(attend_back_kernel, blocks, 2),
        out_shape=(
            jax.ShapeDtypeStruct((length, width), LOW),
            rows,
            rows,
            jax.ShapeDtypeStruct((1, width), WIDE),
        ),
        in_specs=[IN_SMEM] * 3 + [IN_VMEM] * 7,
        out_specs=(IN_VMEM,) * 4,
        scratch_shapes=[
            pltpu.VMEM((length, 128 * pairs), LOW),
            pltpu.VMEM((length, 256 * pairs), WIDE),
        ],
        compiler_params=pltpu.CompilerParams(vmem_limit_bytes=56 << 20),
        cost_estimate=pl.CostEstimate(flops=1, bytes_accessed=1, transcendentals=0),
        name="attend_back",
    )(near, rand, globs, bias, log_total, qkv, mine, come, w_qkv, grad_first)


def pack_columns(at, shard, near, mirror, rows_in):
    two, rows, width = shard.shape
    rows = 4 * rows_in + 2 * (rows - rows_in)
    return pl.pallas_call(
        partial(pack_columns_kernel, 4, rows_in),
        out_shape=jax.ShapeDtypeStruct((two, rows, width), LOW),
        in_specs=[IN_SMEM] + [IN_VMEM] * 3,
        out_specs=IN_VMEM,
        cost_estimate=pl.CostEstimate(flops=1, bytes_accessed=1, transcendentals=0),
        name="pack_columns",
    )(at, shard, near, mirror)


def pack_rows(at, shard, near, mirror, chunks, cut):
    rows, width = 4 * (shard.shape[0] - 16) + 16, shard.shape[1]
    return pl.pallas_call(
        partial(pack_kernel, 4, chunks, cut),
        out_shape=(
            jax.ShapeDtypeStruct((cut, width), LOW),
            jax.ShapeDtypeStruct((rows - cut, width), LOW),
        ),
        in_specs=[IN_SMEM] + [IN_VMEM] * 3,
        out_specs=(IN_VMEM, IN_VMEM),
        cost_estimate=pl.CostEstimate(flops=1, bytes_accessed=1, transcendentals=0),
        name="pack",
    )(at, shard, near, mirror)


def weight_space(chips, direct, chunks, width):
    return [
        pltpu.VMEM((chunks + 1, width, width), LOW),
        pltpu.VMEM((chunks * width, width), LOW),
        pltpu.VMEM((2 * chips if direct else 1, 16, width), LOW),
    ]


def unpack_rows(at, upper, lower, chunks):
    rows, width = upper[0].shape[0] + lower[0].shape[0], upper[0].shape[1]
    like = jax.ShapeDtypeStruct((2, rows // 4, width), LOW)
    return pl.pallas_call(
        partial(unpack_kernel, 4, chunks, len(upper)),
        out_shape=(like, like),
        in_specs=[IN_SMEM] + [IN_VMEM] * (len(upper) + len(lower)),
        out_specs=(IN_VMEM, IN_VMEM),
        cost_estimate=pl.CostEstimate(flops=1, bytes_accessed=1, transcendentals=0),
        name="unpack",
    )(at, *upper, *lower)


def layer_forward(at, mixed, other, tokens, weights, direct, chunks):
    own, width = other.shape[0], tokens.shape[1]
    chips, wide = lax.axis_size("dp") // 2, chunks * width

    def rows(width, kind=LOW):
        return jax.ShapeDtypeStruct((own, width), kind)

    return pl.pallas_call(
        partial(forward_kernel, chips, direct),
        grid=(own // TILE,),
        out_shape=(rows(width), rows(wide), rows(wide), rows(width))
        + (rows(width, WIDE), rows(width, WIDE), rows(128, WIDE)),
        in_specs=[IN_SMEM]
        + [tiles(p.shape[1]) for p in (mixed, other, tokens)]
        + [IN_ANY] * len(weights),
        out_specs=tuple(tiles(w) for w in (width, wide, wide, width, width, width, 128)),
        scratch_shapes=weight_space(chips, direct, chunks, width)
        + [pltpu.SemaphoreType.DMA((2 * chips * (chunks + 4),))],
        compiler_params=pltpu.CompilerParams(vmem_limit_bytes=58 << 20),
        cost_estimate=pl.CostEstimate(flops=1, bytes_accessed=1, transcendentals=0),
        name="layer_forward",
    )(at, mixed, other, tokens, *weights)


def layer_backward(at, mixed, other, grads, slope, units, scales, hidden, normed, weights, direct):
    own, width = normed.shape
    wide = slope.shape[1]
    half, chunks = width // 2, wide // width
    chips = lax.axis_size("dp") // 2
    many = own // TILE // 2
    whole = pl.BlockSpec((own, half), lambda i: (0, 0))
    if direct:
        rows = ((chunks + 1) * width + wide) // (2 * chips)
        grads_like = (jax.ShapeDtypeStruct((chips, rows, width), LOW),) * 2
    else:
        grads_like = (
            jax.ShapeDtypeStruct((chunks + 1, width, width), LOW),
            jax.ShapeDtypeStruct((wide, width), LOW),
        )
    return pl.pallas_call(
        partial(backward_kernel, TILE, chips, direct),
        grid=(own // TILE,),
        out_shape=(
            jax.ShapeDtypeStruct((own, width), LOW),
            jax.ShapeDtypeStruct((own, half), LOW),
            jax.ShapeDtypeStruct((own, half), LOW),
            jax.ShapeDtypeStruct((16, width), WIDE),
        )
        + grads_like,
        in_specs=[IN_SMEM]
        + [whole, whole]
        + [tiles(width, 0, many), tiles(width, many, many)]
        + [tiles(wide), tiles(width), tiles(width), tiles(128)]
        + [IN_ANY] * (2 + len(weights)),
        out_specs=(tiles(width), tiles(half), tiles(half))
        + (pl.BlockSpec((16, width), lambda i: (0, 0)),)
        + (IN_ANY,) * 2,
        scratch_shapes=weight_space(chips, direct, chunks, width)
        + [
            pltpu.VMEM((16, width), WIDE),
            pltpu.VMEM((own, wide), LOW),
            pltpu.VMEM((own, width), LOW),
            pltpu.VMEM((own, width), LOW),
            pltpu.VMEM((own, wide), LOW),
            pltpu.VMEM((own, width), LOW),
            pltpu.SemaphoreType.DMA((2 * chips * (chunks + 4),)),
            pltpu.SemaphoreType.DMA((2,)),
            pltpu.SemaphoreType.DMA((2 * chips * (chunks + 1) + 2 * chunks,)),
        ],
        compiler_params=pltpu.CompilerParams(vmem_limit_bytes=58 << 20),
        cost_estimate=pl.CostEstimate(flops=1, bytes_accessed=1, transcendentals=0),
        name="layer_backward",
    )(at, mixed, other, *grads, slope, *units, scales, hidden, normed, *weights)


def place_of(block, core, z, blocks):
    quarter, row = block // (blocks // 4), block % (blocks // 4)
    a = (quarter & 1) ^ (z & 1)
    return ((quarter >> 1) ^ core) * (blocks // 2) + a * (blocks // 4) + row


def block_at(place, core, z, blocks):
    quarter = 2 * ((place // (blocks // 2)) ^ core) + ((place % (blocks // 2)) // (blocks // 4) ^ (z & 1))
    return quarter * (blocks // 4) + place % (blocks // 4)


def tables(rand, globs, blocks):
    core = lax.axis_index("dp") & 1
    z = lax.axis_index("seq")
    here = block_at(jnp.arange(blocks, dtype=jnp.int32), core, z, blocks)
    heads = rand.shape[0]
    one, two = globs[0], globs[1]

    def near(block):
        return jnp.abs(block - here) <= 1

    every = jnp.ones((heads, blocks), bool)
    ok = [every & (here > 0), every, every & (here < blocks - 1)]
    ok += [every & ~near(one), every & ~near(two) & (one != two)]
    seen = []
    for r in range(3):
        block = rand[:, :, r]
        good = ~near(block) & (block != one) & (block != two)
        for before in seen:
            good = good & (block != before)
        seen.append(block)
        ok.append(good)
    whole_row = (here == one) | (here == two)
    ok = jnp.stack(ok, -1) & ~whole_row[None, :, None]
    bias = jnp.where(ok, 0.0, NEG).astype(WIDE)
    bias = bias.reshape(heads // 2, 2, blocks, SLOTS).transpose(2, 0, 3, 1)
    bias = jnp.repeat(bias, HEAD, axis=3)
    put = partial(place_of, core=core, z=z, blocks=blocks)
    sides = jnp.concatenate([put(jnp.maximum(here - 1, 0)), put(jnp.minimum(here + 1, blocks - 1))])
    return sides, put(rand).reshape(-1), put(globs), bias


def shards(
    inputs,
    cotangent,
    rand_blocks,
    global_blocks,
    w_query,
    b_query,
    w_key,
    w_value,
    b_value,
    w_out,
    b_out,
    gain_one,
    shift_one,
    w_up,
    b_up,
    w_down,
    b_down,
    gain_two,
    shift_two,
):
    n_dp, n_seq = lax.axis_size("dp"), lax.axis_size("seq")
    chips, devices = n_dp // 2, n_dp * n_seq
    core = lax.axis_index("dp") & 1
    z = lax.axis_index("seq")
    device = lax.axis_index("dp") * n_seq + z
    rows_in, width = w_query.shape
    rows_ff, wide = w_down.shape[0], w_up.shape[1]
    chunks = wide // width
    half_width = width // 2
    _, quarter, _ = inputs.shape
    length = quarter * n_seq
    blocks = length // BLOCK
    own = length // 2
    own_heads = HEADS // 2
    span, span_ff = n_seq * rows_in, n_seq * rows_ff
    direct = span % 16 == 0 and chips == chunks

    here = jnp.arange(devices, dtype=jnp.int32)[:, None] == device

    def placed(vector):
        return jnp.where(here, vector[None], jnp.zeros((), LOW)).reshape(-1, width)

    q_line, v_line = placed(b_query), placed(b_value)

    pairs = half_width // 128

    def side(at):
        no_line = jnp.zeros((1, width), LOW)
        parts = []
        for pair in range(pairs):
            first = at * half_width + 128 * pair
            lanes = slice(first, first + 128)
            for w, line in ((w_query, q_line), (w_key, no_line), (w_value, v_line)):
                parts.append(jnp.concatenate([w[:, lanes], line[:, lanes]], 0))
        return jnp.pad(jnp.concatenate(parts, 1), ((0, 7), (0, 0)))

    left, right = side(0), side(1)
    keep = jnp.where(core == 0, left, right)
    come = swap(jnp.where(core == 0, right, left))
    shard = jnp.stack([jnp.where(core == 0, keep, come), jnp.where(core == 0, come, keep)])
    def numbers_of(s):
        numbers = pick(rand_blocks, s, 0).reshape(-1)
        numbers = jnp.concatenate([numbers, pick(global_blocks, s, 0).reshape(-1)])
        return jnp.pad(numbers, (0, -numbers.shape[0] % 128))

    numbers = jnp.stack(bring(numbers_of))
    qkv_z = gather_seq(tie(shard, numbers))

    packed = jnp.concatenate(
        [w_up[:, width * c : width * c + width] for c in range(chunks)]
        + [w_out, w_down]
        + [placed(v) for v in (b_out, gain_one, shift_one, b_down, gain_two, shift_two, b_up)]
        + [jnp.zeros((16 - 6 - chunks, width), LOW)],
        0,
    )
    wide_z = gather_seq(tie(packed, shard), qkv_z[2])
    at = jnp.stack([lax.axis_index("dp") >> 1, core, z]).astype(jnp.int32)

    direct = span % 16 == 0 and chips == chunks
    if direct:
        whole = pack_columns(at, *qkv_z, rows_in)
    else:
        qkv_z = in_seq_order(*qkv_z)
        whole = []
        for k in range(2):
            lines = sum(p[k, rows_in:].astype(WIDE) for p in qkv_z).astype(LOW)
            whole += [p[k, :rows_in] for p in qkv_z] + [lines, jnp.zeros_like(lines)]
        whole = jnp.concatenate(whole, 0).reshape(2, span + 16, 3 * half_width)
    qkv_parts = gather_chips(whole)
    numbers = tie(numbers, whole)
    numbers = jnp.concatenate([numbers, swap(numbers)], 0)
    local_blocks = rand_blocks.shape[2]
    count = HEADS * local_blocks * 3
    globs = numbers[0, count : count + 2]
    rand = numbers[:, :count].reshape(4, HEADS, local_blocks, 3)
    rand = lax.dynamic_slice_in_dim(rand, core * own_heads, own_heads, 1)
    rand = rand.transpose(1, 0, 2, 3).reshape(own_heads, blocks, 3)
    sides, rand, glob_at, bias = tables(rand, globs, blocks)


    tied_inputs = tie(inputs, qkv_z[2])
    pieces = bring(lambda s: pick(tied_inputs, s, 0)[0])

    if direct:
        cut = chunks * span + span // 2
        near, pieces[0], bias, sides, rand, glob_at, *qkv_parts = join(
            wide_z[1], pieces[0], bias, sides, rand, glob_at, *qkv_parts
        )
        whole = pack_rows(at, wide_z[0], near, wide_z[2], chunks + 1, cut)
    else:
        wide_z = in_seq_order(*wide_z)
        rows_a = (chunks + 1) * rows_in
        rows = []
        for c in range(chunks + 1):
            rows += [p[c * rows_in : (c + 1) * rows_in] for p in wide_z]
        rows += [p[rows_a : rows_a + rows_ff] for p in wide_z]
        rows.append(sum(p[rows_a + rows_ff :].astype(WIDE) for p in wide_z).astype(LOW))
        whole = jnp.concatenate(rows, 0)
    if direct:
        lines = sum(jnp.sum(p[:, span].astype(WIDE), 0, keepdims=True) for p in qkv_parts)
        *parts, lines, pieces[0], pieces[1] = join(*gather_quads(*whole), lines, *pieces)
    else:
        parts = gather_chips(tie(whole, qkv_parts))
        lines = sum(jnp.sum(p[:, span].astype(WIDE), 0, keepdims=True) for p in qkv_parts)
    pieces = [*pieces, *(swap(p) for p in pieces)]
    rows_a, rows_b = (chunks + 1) * span, (chunks + 1) * span + span_ff
    if direct:
        qkv_weights = tuple(qkv_parts)
    else:
        ordered = in_chip_order(qkv_parts)
        qkv_weights = (jnp.concatenate([p[k, :span] for p in ordered for k in range(2)], 0),)

    if direct:
        upper, lower = jnp.stack(parts[:2]), jnp.stack(parts[2:])
        parts = [upper, flip_chip(upper, 2), lower, flip_chip(lower, 1)]
        other_parts = [swap(upper), None, swap(lower), None]
    qkv, tokens, w_qkv = project_tokens(at, pieces, lines, qkv_weights, direct)
    mixed, log_total = attend(sides, rand, glob_at, bias, qkv)
    tied = tie(cotangent, qkv)
    first_grads = bring_round(lambda s: pick(tied, s, 0)[0], 0)
    mixed, log_total, first_grads, *parts = join(mixed, log_total, first_grads, *parts)
    other = swap(mixed[own:])
    if direct:
        other_parts[1], other_parts[3] = swap(parts[1]), swap(parts[3])
    else:
        other_parts = [swap(p) for p in parts]
    if direct:
        weights = tuple(parts + other_parts)
    else:
        weights = (
            jnp.stack(
                [
                    in_device_order(
                        *([p[span * c : span * c + span] for p in ps] for ps in (parts, other_parts))
                    )
                    for c in range(chunks + 1)
                ]
            ),
            in_device_order(*([p[rows_a:rows_b] for p in ps] for ps in (parts, other_parts))),
            sum(p[rows_b:].astype(WIDE) for p in parts + other_parts).astype(LOW)[None],
        )
    tied = tie(cotangent, mixed)
    grad_result = first_grads, bring_round(lambda s: pick(tied, s, 0)[0], 1)
    forward = layer_forward(at, mixed, other, tokens, weights, direct, chunks)
    forward, grad_result = join(forward, grad_result)
    result, hidden, slope, normed, unit_one, unit_two, scales = forward
    output = send_back(result)
    backward = layer_backward(
        at,
        mixed,
        other,
        grad_result,
        slope,
        (unit_one, unit_two),
        scales,
        hidden,
        normed,
        weights,
        direct,
    )
    backward, output = join(backward, output)
    grad_first, mine, theirs, in_sums, grad_in, grad_down = backward

    come = swap(theirs)
    if direct:
        chip = lax.axis_index("dp") >> 1
        x, y = chip & 1, chip >> 1
        grad_other, come = join(swap(grad_down), come)
        cut = chunks * span + span // 2
        both = [p.reshape(2, 2, -1, width) for p in (grad_in, grad_other)]
        moves = [
            added(*(pick(p[:, :, rows], which, axis) for p in both))
            for rows, axis, own_side in ((slice(0, cut), 1, x), (slice(cut, None), 0, y))
            for which in (own_side, 1 - own_side)
        ]
        mine, come, *moves = join(mine, come, *moves)
        moves[1], moves[3] = flip_chip(moves[1], 1), flip_chip(moves[3], 2)
    grad_qkv, grad_own, grad_theirs, sums = attend_back(
        sides,
        rand,
        glob_at,
        bias,
        log_total,
        qkv,
        mine,
        come,
        w_qkv,
        grad_first,
    )
    if direct:
        grad_qkv, grad_own, grad_theirs, sums, *moves = join(grad_qkv, grad_own, grad_theirs, sums, *moves)
    come_rows = swap(grad_theirs)
    if direct:
        moves = [
            added(*(pick(p, which, axis) for p in pair))
            for pair, axis, own_side in ((moves[:2], 0, y), (moves[2:], 1, x))
            for which in (own_side, 1 - own_side)
        ]
        grad_own, *moves = join(grad_own, *(move.reshape(-1, width) for move in moves))
        moves[1], moves[3] = flip_chip(moves[1], 2), flip_chip(moves[3], 1)
    grad_inputs = [added(*pair) for pair in zip(start_back(grad_own), start_back(come_rows))]
    grad_inputs, grad_qkv = join(grad_inputs, grad_qkv)
    first_back = finish_back(grad_inputs, 0)
    grad_w_qkv = dot(tokens, grad_qkv, TN).astype(LOW)
    vectors = in_sums[: 6 + chunks].reshape(-1)
    vectors = jnp.pad(vectors, (0, -vectors.shape[0] % (3 * half_width))).reshape(-1, 3 * half_width)
    lines = jnp.concatenate([sums, vectors], 0).astype(LOW)
    lines = jnp.broadcast_to(lines, (chips, 2, n_seq) + lines.shape)
    parts = jnp.concatenate(
        [grad_w_qkv.reshape(chips, 2, n_seq, rows_in, 3 * half_width), lines], 3
    )
    keep, come = (pick(parts, which, 1)[:, 0] for which in (core, 1 - core))
    come = swap(come)
    parts = jnp.stack([keep, come], 1)
    if direct:
        first_back, *moves = join(first_back, *moves)
        near_sums, keep_sums = unpack_rows(at, moves[:2], moves[2:], chunks + 1)
    else:
        rows = lax.psum_scatter(grad_in, "dp", scatter_dimension=1, tiled=True)
        rows = rows.reshape((chunks + 1) * span, width)
        down = lax.psum_scatter(grad_down, "dp", scatter_dimension=0, tiled=True)
        near_sums, keep_sums = unpack_rows(at, [rows], [down], chunks + 1)
    grad_inputs = first_back, finish_back(grad_inputs, 1)
    near_sums = flip_seq(near_sums, 1)
    parts = reduce_chips(parts)
    parts, near_sums = join(parts, near_sums)
    own_qkv = reduce_seq(parts.transpose(1, 0, 2, 3))
    keep, come = own_qkv[0], own_qkv[1]
    left, right = jnp.where(core == 0, keep, come), jnp.where(core == 0, come, keep)

    mirror = flip_seq(added(keep_sums[1], near_sums[1]), 3)
    own_sums = sum(p.astype(WIDE) for p in (keep_sums[0], near_sums[0], mirror))
    rows_a = (chunks + 1) * rows_in
    own_up = jnp.concatenate(
        [own_sums[c * rows_in : (c + 1) * rows_in] for c in range(chunks)], 1
    )
    small = (keep + come)[rows_in + 1 :].reshape(-1)[: (6 + chunks) * width].reshape(-1, width)

    def joined(k, rows):
        lanes = [lanes_of(k, pair) for pair in range(pairs)]
        return jnp.concatenate([one[rows, at] for one in (left, right) for at in lanes], 1)

    def own_part(vector, size):
        return lax.dynamic_slice_in_dim(vector.reshape(-1), device * size, size, 0)

    six = lax.dynamic_slice_in_dim(small[:6], device * rows_in, rows_in, 1)

    matrix_rows, line = slice(0, rows_in), slice(rows_in, rows_in + 1)
    return (
        in_sequences(output),
        in_sequences(grad_inputs),
        joined(0, matrix_rows),
        own_part(joined(0, line), rows_in),
        joined(1, matrix_rows),
        joined(2, matrix_rows),
        own_part(joined(2, line), rows_in),
        own_sums[chunks * rows_in : rows_a],
        six[0],
        six[1],
        six[2],
        own_up,
        own_part(small[6 : 6 + chunks], rows_ff),
        own_sums[rows_a : rows_a + rows_ff],
        six[3],
        six[4],
        six[5],
    )


def solution(mesh):
    both = ("dp", "seq")
    matrix, vector = P(both, None), P(both)
    tokens = P("dp", "seq", None)
    return jax.shard_map(
        shards,
        mesh=mesh,
        in_specs=(tokens, tokens, P("dp", None, "seq", None), P("dp", None))
        + (matrix, vector, matrix, matrix, vector, matrix, vector, vector, vector)
        + (matrix, vector, matrix, vector, vector, vector),
        out_specs=(tokens, tokens)
        + (matrix, vector, matrix, matrix, vector, matrix, vector, vector, vector)
        + (matrix, vector, matrix, vector, vector, vector),
        check_vma=False,
    )
```

```python
from functools import partial

import jax
import jax.numpy as jnp
from jax import lax
from jax.experimental import pallas as pl
from jax.experimental.pallas import tpu as pltpu
from jax.sharding import PartitionSpec as P

HEADS = 12
HEAD = 64
BLOCK = 64
SLOTS = 8
EPS = 1e-06
NEG = -1e30
LOW = jnp.bfloat16
WIDE = jnp.float32

NT = (((1,), (1,)), ((), ()))
TN = (((0,), (0,)), ((), ()))
NN = (((1,), (0,)), ((), ()))


def dot(left, right, dims):
    return lax.dot_general(left, right, dims, preferred_element_type=WIDE)


def swap(array):
    size = lax.axis_size("dp")
    return lax.ppermute(array, "dp", [(i, i ^ 1) for i in range(size)])


def flip_seq(array, k):
    size = lax.axis_size("seq")
    return lax.ppermute(array, "seq", [(i, i ^ k) for i in range(size)])


def rounds():
    dp, seq = lax.axis_size("dp"), lax.axis_size("seq")
    for a in range(2):
        pairs = []
        for d in range(dp):
            for z in range(seq):
                to_dp = (d & ~1) | (z >> 1)
                to_seq = 2 * (d & 1) + (a ^ (z & 1))
                pairs.append((d * seq + z, to_dp * seq + to_seq))
        yield a, pairs


def bring_round(piece_of, which):
    a, pairs = list(rounds())[which]
    z = lax.axis_index("seq")
    return lax.ppermute(piece_of(a ^ (z & 1)), ("dp", "seq"), pairs)


def bring(piece_of):
    return [bring_round(piece_of, which) for which in range(2)]


def start_back(rows):
    size = rows.shape[0] // 2
    return [rows[size * a : size * a + size] for a in range(2)]


def finish_back(parts, which):
    a, pairs = list(rounds())[which]
    return lax.ppermute(parts[a], ("dp", "seq"), [(t, s) for s, t in pairs])


def send_back(rows):
    parts = start_back(rows)
    return [finish_back(parts, a) for a in range(2)]


def in_sequences(got):
    odd = (lax.axis_index("seq") & 1) == 1
    return jnp.stack([jnp.where(odd, got[1], got[0]), jnp.where(odd, got[0], got[1])])


def pick(array, index, axis):
    return lax.dynamic_slice_in_dim(array, index, 1, axis)


def gather_seq(shard, before=None):
    mirror = flip_seq(shard, 3)
    pair = jnp.stack([shard, mirror])
    if before is not None:
        pair = tie(pair, before)
    return shard, flip_seq(pair, 1), mirror


def in_seq_order(shard, near, mirror):
    z = lax.axis_index("seq")
    pieces = [shard, near[0], near[1], mirror]
    for bit in range(2):
        set_bit = ((z >> bit) & 1) == 1
        pieces = [
            jnp.where(set_bit, pieces[i ^ (1 << bit)], pieces[i]) for i in range(len(pieces))
        ]
    return pieces


def chip_groups():
    count = (lax.axis_size("dp") // 2).bit_length() - 1
    return [(bit, min(2, count - bit)) for bit in range(0, count, 2)]


def flip_chip(array, away):
    size = lax.axis_size("dp")
    return lax.ppermute(array, "dp", [(i, i ^ (2 * away)) for i in range(size)])


def gather_chips(part):
    parts = [part]
    for bit, bits in chip_groups():
        parts = parts + [flip_chip(p, k << bit) for k in range(1, 1 << bits) for p in parts]
    return parts


def in_chip_order(parts):
    chip = lax.axis_index("dp") >> 1
    parts = jnp.stack(parts)
    return [pick(parts, q ^ chip, 0)[0] for q in range(parts.shape[0])]


def in_device_order(mine, theirs):
    core = lax.axis_index("dp") & 1
    parts = []
    for own, other in zip(in_chip_order(mine), in_chip_order(theirs)):
        parts += [jnp.where(core == 0, own, other), jnp.where(core == 0, other, own)]
    return jnp.concatenate(parts, 0)


def join(*values):
    return lax.optimization_barrier(values)


def gather_quads(upper, lower):
    return [upper, flip_chip(upper, 1), lower, flip_chip(lower, 2)]


def tie(values, *others):
    return lax.optimization_barrier((values, others))[0]


def added(*arrays):
    return sum(array.astype(WIDE) for array in arrays).astype(LOW)


def reduce_chips(parts):
    chip = lax.axis_index("dp") >> 1
    for bit, bits in chip_groups():
        ways = 1 << bits
        parts = parts.reshape((-1, ways) + parts.shape[1:])
        mine = (chip >> bit) & (ways - 1)
        others = [flip_chip(pick(parts, mine ^ k, 1)[:, 0], k << bit) for k in range(1, ways)]
        parts = added(pick(parts, mine, 1)[:, 0], *others)
    return parts[0]


def reduce_seq(parts):
    z = lax.axis_index("seq")
    near = flip_seq(jnp.concatenate([pick(parts, z ^ 1, 0), pick(parts, z ^ 2, 0)], 0), 1)
    mirror = added(pick(parts, z ^ 3, 0)[0], near[1])
    return pick(parts, z, 0)[0].astype(WIDE) + near[0].astype(WIDE) + flip_seq(mirror, 3).astype(WIDE)


def norm_parts(summed):
    center = summed - jnp.mean(summed, -1, keepdims=True)
    spread = jnp.mean(center * center, -1, keepdims=True)
    scale = lax.rsqrt(spread + EPS)
    return center * scale, scale


def norm_back(grad, unit, scale, gain):
    grad_unit = grad * gain
    mean_one = jnp.mean(grad_unit, -1, keepdims=True)
    mean_two = jnp.mean(grad_unit * unit, -1, keepdims=True)
    return scale * (grad_unit - mean_one - unit * mean_two)


def gelu_parts(x):
    size = jnp.abs(x)
    t = 1.0 / (1.0 + (0.3275911 * 0.5**0.5) * size)
    bell = jnp.exp(-0.5 * x * x)
    series = 0.5 * 1.061405429
    for factor in (-1.453152027, 1.421413741, -0.284496736, 0.254829592):
        series = series * t + 0.5 * factor
    tail = series * t * bell
    share = jnp.where(x >= 0, 1.0 - tail, tail)
    return x * share, share + x * bell * 0.3989422804014327


def block_rows(ref, block, lanes):
    return ref[pl.ds(pl.multiple_of(block * BLOCK, BLOCK), BLOCK), lanes]


def diagonal(pair_rows, low):
    zero = jnp.zeros_like(pair_rows)
    return jnp.concatenate(
        [jnp.where(low, pair_rows, zero), jnp.where(low, zero, pair_rows)], axis=0
    )


def gather_blocks(ref, ids, lanes, low):
    parts = []
    for one, two in ids:
        if two is None:
            parts.append(block_rows(ref, one, lanes))
        else:
            parts.append(
                jnp.where(low, block_rows(ref, one, lanes), block_rows(ref, two, lanes))
            )
    return jnp.concatenate(parts, axis=0)


def slot_ids(near_ref, rand_ref, globs, i, head, blocks):
    ids = [(near_ref[i], None), (i, None), (near_ref[blocks + i], None)]
    ids += [(globs[0], None), (globs[1], None)]
    for r in range(3):
        ids.append(
            (
                rand_ref[(head * blocks + i) * 3 + r],
                rand_ref[((head + 1) * blocks + i) * 3 + r],
            )
        )
    return ids


def lanes_of(part, pair):
    first = 128 * (3 * pair + part)
    return slice(first, first + 128)


def flat_lanes(pair):
    return slice(128 * pair, 128 * pair + 128)


def start_copies(copies, sems):
    started = [
        pltpu.make_async_copy(source, target, sems.at[k])
        for k, (source, target) in enumerate(copies)
    ]
    for copy in started:
        copy.start()
    return started


def project_kernel(chips, direct, at_ref, *refs):
    pieces, b_ref = refs[:4], refs[4]
    sources, (qkv_ref, tokens_ref, w_ref, sems) = refs[5:-4], refs[-4:]
    if direct:
        span = w_ref.shape[0] // (2 * chips)
        copies = [
            (
                sources[away].at[k, :span],
                w_ref.at[pl.ds(pl.multiple_of((2 * (at_ref[0] ^ away) + k) * span, span), span)],
            )
            for away in range(chips)
            for k in range(2)
        ]
    else:
        copies = [(sources[0], w_ref)]

    @pl.when(pl.program_id(0) == 0)
    def _():
        for copy in start_copies(copies, sems):
            copy.wait()

    lane = lax.broadcasted_iota(jnp.int32, (1, w_ref.shape[1]), 1)
    scale = jnp.where(lane % 384 < 128, HEAD ** (-0.5), 1.0)
    at = pl.program_id(0) * len(pieces) // pl.num_programs(0)
    rows = pieces[0][...]
    for k in range(1, len(pieces)):
        rows = jnp.where(at == k, pieces[k][...], rows)
    tokens_ref[...] = rows
    values = (dot(rows, w_ref[...], NN) + b_ref[...]).astype(LOW).astype(WIDE)
    qkv_ref[...] = (values * scale).astype(LOW)


def with_sems(groups, sems):
    done, copies = 0, []
    for group in groups:
        copies.append([pltpu.make_async_copy(*pair, sems.at[done + k]) for k, pair in enumerate(group)])
        done += len(group)
    return copies


def attend_kernel(
    pairs, blocks, step, near_ref, rand_ref, glob_ref, bias_ref, qkv_ref, out_ref, log_ref
):
    low = lax.broadcasted_iota(jnp.int32, (1, 2 * HEAD), 1) < HEAD
    globs = (glob_ref[0], glob_ref[1])

    def scores_of(i, pair):
        ids = slot_ids(near_ref, rand_ref, globs, i, 2 * pair, blocks)
        queries = diagonal(block_rows(qkv_ref, i, lanes_of(0, pair)), low)
        return dot(gather_blocks(qkv_ref, ids, lanes_of(1, pair), low), queries, NT)

    def softmax_of(i, pair, scores):
        highest = jnp.max(scores, axis=0, keepdims=True)
        weights = jnp.exp(scores - highest)
        total = jnp.sum(weights, axis=0, keepdims=True)
        log_ref[i, pair : pair + 1] = highest + jnp.log(total)
        return (weights * (1.0 / total)).astype(LOW)

    def put(i, pair, mixed):
        at = pl.ds(pl.multiple_of(i * BLOCK, BLOCK), BLOCK)
        out_ref[at, flat_lanes(pair)] = jnp.where(low, mixed[:BLOCK], mixed[BLOCK:]).astype(LOW)

    def body(at, carry):
        units = [(at * step + d, pair) for d in range(step) for pair in range(pairs)]
        scores = [scores_of(*unit) for unit in units]
        probs = []
        for (i, pair), score in zip(units, scores):
            bias = bias_ref[i, pair]
            score = jnp.concatenate(
                [score[BLOCK * j : BLOCK * j + BLOCK] + bias[j : j + 1] for j in range(SLOTS)],
                axis=0,
            )
            probs.append(softmax_of(i, pair, score))
        for (i, pair), prob in zip(units, probs):
            ids = slot_ids(near_ref, rand_ref, globs, i, 2 * pair, blocks)
            values = gather_blocks(qkv_ref, ids, lanes_of(2, pair), low)
            put(i, pair, dot(prob, values, TN))
        return carry

    lax.fori_loop(0, blocks // step, body, 0)

    def whole_row(n, carry):
        i = glob_ref[n]
        scores = []
        for pair in range(pairs):
            queries = diagonal(block_rows(qkv_ref, i, lanes_of(0, pair)), low)
            scores.append(dot(qkv_ref[:, lanes_of(1, pair)], queries, NT))
        probs = [softmax_of(i, pair, scores[pair]) for pair in range(pairs)]
        for pair in range(pairs):
            put(i, pair, dot(probs[pair], qkv_ref[:, lanes_of(2, pair)], TN))
        return carry

    lax.fori_loop(0, 2, whole_row, 0)


def attend_back_kernel(
    blocks,
    step,
    near_ref,
    rand_ref,
    glob_ref,
    bias_ref,
    log_ref,
    qkv_ref,
    mine_ref,
    come_ref,
    w_ref,
    grad_first_ref,
    tokens_ref,
    weights_ref,
    rows_own_ref,
    rows_other_ref,
    sums_ref,
    out_ref,
    grad_ref,
    acc_ref,
):
    low = lax.broadcasted_iota(jnp.int32, (1, 2 * HEAD), 1) < HEAD
    globs = (glob_ref[0], glob_ref[1])
    acc_ref[...] = jnp.zeros_like(acc_ref)
    half = mine_ref.shape[0]
    grad_ref[:half] = mine_ref[...]
    grad_ref[half:] = come_ref[...]
    pairs = mine_ref.shape[1] // 128

    def source(pair, part):
        return qkv_ref.at[:, lanes_of(part, pair)]

    def log_of(i, pair):
        return log_ref[i, pair : pair + 1]

    every = slice(None)

    def add(part, pair, block, value):
        at = pl.ds(pl.multiple_of(block * BLOCK, BLOCK), BLOCK)
        lanes = flat_lanes(2 * pair + part)
        acc_ref[at, lanes] = acc_ref[at, lanes] + value

    def operands(i, pair):
        queries = diagonal(block_rows(source(pair, 0), i, every), low)
        grads = diagonal(block_rows(grad_ref, i, flat_lanes(pair)), low)
        return queries, grads

    def softmax_back(prob, grad_prob):
        scaled = prob * grad_prob
        inner = jnp.sum(scaled, axis=0, keepdims=True)
        return prob.astype(LOW), (scaled - prob * inner).astype(LOW)

    def put(i, pair, mixed):
        at = pl.ds(pl.multiple_of(i * BLOCK, BLOCK), BLOCK)
        out_ref[at, lanes_of(0, pair)] = (
            jnp.where(low, mixed[:BLOCK], mixed[BLOCK:]) * HEAD ** (-0.5)
        ).astype(LOW)

    def body(at, carry):
        units = [(at * step + d, pair) for d in range(step) for pair in range(pairs)]
        first = []
        for i, pair in units:
            ids = slot_ids(near_ref, rand_ref, globs, i, 2 * pair, blocks)
            queries, grads = operands(i, pair)
            first.append(
                (
                    dot(gather_blocks(source(pair, 1), ids, every, low), queries, NT),
                    dot(gather_blocks(source(pair, 2), ids, every, low), grads, NT),
                )
            )
        second = []
        for (i, pair), (score, grad_prob) in zip(units, first):
            shift = bias_ref[i, pair] - log_of(i, pair)
            prob = jnp.concatenate(
                [
                    jnp.exp(score[BLOCK * j : BLOCK * j + BLOCK] + shift[j : j + 1])
                    for j in range(SLOTS)
                ],
                axis=0,
            )
            second.append(softmax_back(prob, grad_prob))
        third = []
        for (i, pair), (prob, grad_score) in zip(units, second):
            ids = slot_ids(near_ref, rand_ref, globs, i, 2 * pair, blocks)
            queries, grads = operands(i, pair)
            keys = gather_blocks(source(pair, 1), ids, every, low)
            put(i, pair, dot(grad_score, keys, TN))
            third.append((dot(grad_score, queries, NN), dot(prob, grads, NN)))
        for (i, pair), values in zip(units, third):
            ids = slot_ids(near_ref, rand_ref, globs, i, 2 * pair, blocks)
            for j, (one, two) in enumerate(ids):
                for part, value in enumerate(values):
                    value = value[BLOCK * j : BLOCK * j + BLOCK]
                    if two is None:
                        add(part, pair, one, value)
                    else:
                        add(part, pair, one, jnp.where(low, value, 0.0))
                        add(part, pair, two, jnp.where(low, 0.0, value))
        return carry

    lax.fori_loop(0, blocks // step, body, 0)

    def whole_row(n, carry):
        i = glob_ref[n]
        first = []
        for pair in range(pairs):
            queries, grads = operands(i, pair)
            first.append(
                (
                    dot(source(pair, 1)[...], queries, NT),
                    dot(source(pair, 2)[...], grads, NT),
                )
            )
        second = []
        for pair, (score, grad_prob) in enumerate(first):
            prob = jnp.exp(score - log_of(i, pair))
            second.append(softmax_back(prob, grad_prob))
        for pair, (prob, grad_score) in enumerate(second):
            queries, grads = operands(i, pair)
            acc_ref[:, flat_lanes(2 * pair)] += dot(grad_score, queries, NN)
            acc_ref[:, flat_lanes(2 * pair + 1)] += dot(prob, grads, NN)
            put(i, pair, dot(grad_score, source(pair, 1)[...], TN))
        return carry

    lax.fori_loop(0, jnp.where(globs[0] == globs[1], 1, 2), whole_row, 0)
    for pair in range(pairs):
        out_ref[:, 384 * pair + 128 : 384 * pair + 384] = acc_ref[
            :, 256 * pair : 256 * pair + 256
        ].astype(LOW)

    sums_ref[...] = jnp.zeros_like(sums_ref)
    tile = 512
    for side, rows_ref in enumerate((rows_own_ref, rows_other_ref)):

        def token_rows(at, carry, side=side, rows_ref=rows_ref):
            grads = out_ref[pl.ds(pl.multiple_of(side * half + at * tile, tile), tile)]
            sums_ref[...] += jnp.sum(grads.astype(WIDE), 0, keepdims=True)
            rows = pl.ds(pl.multiple_of(at * tile, tile), tile)
            total = dot(grads, w_ref[...], NT)
            if side == 0:
                total = total + grad_first_ref[rows].astype(WIDE)
            rows_ref[rows] = total.astype(LOW)
            return carry

        lax.fori_loop(0, half // tile, token_rows, 0)
    for pair in range(pairs):
        lanes = slice(384 * pair, 384 * pair + 384)
        weights_ref[:, lanes] = dot(tokens_ref[...], out_ref[:, lanes], TN).astype(LOW)


def pack_kernel(seq, chunks, cut, at_ref, shard_ref, near_ref, mirror_ref, upper_ref, lower_ref):
    rows = shard_ref.shape[0] - 16
    rows_in = rows // (chunks + 4)
    rows_ff = rows - chunks * rows_in
    pieces = [shard_ref, near_ref.at[0], near_ref.at[1], mirror_ref]
    total = sum(piece[rows:].astype(WIDE) for piece in pieces)

    def put(first, value):
        target, first = (upper_ref, first) if first < cut else (lower_ref, first - cut)
        target[first : first + value.shape[0]] = value

    put(rows * seq, total.astype(LOW))
    for z in range(seq):

        @pl.when(at_ref[2] == z)
        def _(z=z):
            for k, piece in enumerate(pieces):
                for c in range(chunks):
                    put((c * seq + (z ^ k)) * rows_in, piece[c * rows_in : c * rows_in + rows_in])
                put(chunks * seq * rows_in + (z ^ k) * rows_ff, piece[chunks * rows_in : rows])


def pack_columns_kernel(seq, rows_in, at_ref, shard_ref, near_ref, mirror_ref, out_ref):
    pieces = [shard_ref, near_ref.at[0], near_ref.at[1], mirror_ref]
    total = sum(piece[:, rows_in:].astype(WIDE) for piece in pieces).astype(LOW)
    out_ref[:, seq * rows_in :] = jnp.concatenate([total, jnp.zeros_like(total)], 1)
    for z in range(seq):

        @pl.when(at_ref[2] == z)
        def _(z=z):
            for k, piece in enumerate(pieces):
                first = (z ^ k) * rows_in
                out_ref[:, first : first + rows_in] = piece[:, :rows_in]


def unpack_kernel(seq, chunks, many, at_ref, *refs):
    sources, (near_ref, keep_ref) = refs[:-2], refs[-2:]
    rows = near_ref.shape[1]
    rows_in = rows // (chunks + 4)
    rows_ff = rows - chunks * rows_in

    cut = sources[0].shape[0]

    def total(first, size):
        refs, first = (sources[:many], first) if first < cut else (sources[many:], first - cut)
        return sum(ref[first : first + size].astype(WIDE) for ref in refs).astype(LOW)

    for z in range(seq):

        @pl.when(at_ref[2] == z)
        def _(z=z):
            for k in range(seq):
                target = (keep_ref, near_ref)[k in (1, 2)].at[int(k > 1)]
                for c in range(chunks):
                    part = total((c * seq + (z ^ k)) * rows_in, rows_in)
                    target[c * rows_in : c * rows_in + rows_in] = part
                target[chunks * rows_in :] = total(chunks * seq * rows_in + (z ^ k) * rows_ff, rows_ff)


def weight_copies(chips, direct, chip, core, sources, w_in_ref, w_down_ref, lines_ref):
    if not direct:
        return [(sources[0], w_in_ref), (sources[2], lines_ref)], [], [(sources[1], w_down_ref)]
    wide, width = w_down_ref.shape
    chunks = wide // width
    span, span_ff = width // (2 * chips), wide // (2 * chips)
    cut = span // 2
    groups = [], [], []
    for k in range(2):
        for away in range(chips):
            place = 2 * (chip ^ away) + (core if k == 0 else 1 - core)
            upper = sources[4 * k + (away >> 1)].at[away & 1]
            lower = sources[4 * k + 2 + (away & 1)].at[away >> 1]
            rows = pl.ds(pl.multiple_of(place * span, span), span)
            groups[1].extend(
                (upper.at[span * c : span * c + span], w_in_ref.at[c, rows]) for c in range(chunks)
            )
            for half, source in enumerate((upper.at[span * chunks :], lower.at[:cut])):
                rows = pl.ds(pl.multiple_of(place * span + half * cut, cut), cut)
                groups[0].append((source, w_in_ref.at[chunks, rows]))
            rows = pl.ds(pl.multiple_of(place * span_ff, span_ff), span_ff)
            groups[2].append((lower.at[cut : cut + span_ff], w_down_ref.at[rows]))
            groups[0].append((lower.at[cut + span_ff :], lines_ref.at[k * chips + away]))
    return groups


def forward_kernel(
    chips,
    direct,
    at_ref,
    mixed_ref,
    other_ref,
    tokens_ref,
    *refs,
):
    sources, refs = refs[:-11], refs[-11:]
    output_ref, hidden_ref, slope_ref, normed_ref, unit_one_ref, unit_two_ref, scales_ref = refs[:7]
    w_in_ref, w_down_ref, lines_ref, sems = refs[7:]
    wide, width = w_down_ref.shape
    half, chunks = width // 2, wide // width
    core = at_ref[1]
    groups = weight_copies(chips, direct, at_ref[0], core, sources, w_in_ref, w_down_ref, lines_ref)
    groups = with_sems(groups, sems)

    @pl.when(pl.program_id(0) == 0)
    def _():
        for copy in sum(groups, []):
            copy.start()
        for copy in groups[0]:
            copy.wait()

    vectors = jnp.sum(lines_ref[...].astype(WIDE), 0)
    b_out, gain_one, shift_one, b_down, gain_two, shift_two = (vectors[k : k + 1] for k in range(6))
    here = pl.ds(pl.multiple_of(core * half, 128), half)
    there = pl.ds(pl.multiple_of((1 - core) * half, 128), half)
    branch = dot(mixed_ref[...], w_in_ref[chunks, here], NN) + dot(other_ref[...], w_in_ref[chunks, there], NN)
    unit_one, scale_one = norm_parts(tokens_ref[...].astype(WIDE) + (branch + b_out))
    normed = unit_one * gain_one + shift_one
    normed_low = normed.astype(LOW)
    normed_ref[...] = normed_low
    unit_one_ref[...] = unit_one

    @pl.when(pl.program_id(0) == 0)
    def _():
        for copy in groups[1] + groups[2]:
            copy.wait()

    down = b_down
    for c in range(0, chunks, 2):
        lanes = slice(width * c, width * c + 2 * width)
        weights = jnp.concatenate([w_in_ref[c], w_in_ref[c + 1]], 1)
        bias = jnp.concatenate([vectors[6 + c : 7 + c], vectors[7 + c : 8 + c]], 1)
        hidden, slope = gelu_parts(dot(normed_low, weights, NN) + bias)
        hidden = hidden.astype(LOW)
        hidden_ref[:, lanes] = hidden
        slope_ref[:, lanes] = slope.astype(LOW)
        down = down + dot(hidden, w_down_ref[lanes], NN)
    unit_two, scale_two = norm_parts(normed + down)
    output_ref[...] = (unit_two * gain_two + shift_two).astype(LOW)
    lane = lax.broadcasted_iota(jnp.int32, (1, 128), 1)
    scales_ref[...] = jnp.where(lane < 64, scale_one, scale_two)
    unit_two_ref[...] = unit_two


def backward_kernel(
    tile,
    chips,
    direct,
    at_ref,
    mixed_ref,
    other_ref,
    grad_first_ref,
    grad_last_ref,
    slope_ref,
    unit_one_ref,
    unit_two_ref,
    scales_ref,
    hidden_hbm,
    normed_hbm,
    *refs,
):
    sources, refs = refs[:-18], refs[-18:]
    first_ref, mine_ref, theirs_ref, sums_ref, *grad_refs = refs[:6]
    w_in_ref, w_down_ref, lines_ref, vectors_ref, pre_ref, branch_ref = refs[6:12]
    normed_ref, hidden_ref, down_ref, sems, extra_sems, out_sems = refs[12:]
    own, width = normed_ref.shape
    wide = w_down_ref.shape[0]
    half, chunks = width // 2, wide // width
    chip, core = at_ref[0], at_ref[1]
    at, last = pl.program_id(0), pl.num_programs(0) - 1
    rows = pl.ds(pl.multiple_of(at * tile, tile), tile)
    groups = weight_copies(chips, direct, chip, core, sources, w_in_ref, w_down_ref, lines_ref)
    groups = with_sems(groups, sems)
    extra = [
        pltpu.make_async_copy(hidden_hbm, hidden_ref, extra_sems.at[0]),
        pltpu.make_async_copy(normed_hbm, normed_ref, extra_sems.at[1]),
    ]
    here = pl.ds(pl.multiple_of(core * half, 128), half)
    there = pl.ds(pl.multiple_of((1 - core) * half, 128), half)

    @pl.when(at == 0)
    def _():
        for copy in groups[2] + groups[1] + groups[0]:
            copy.start()
        for copy in extra:
            copy.start()
        sums_ref[...] = jnp.zeros_like(sums_ref)
        for copy in groups[2] + groups[1] + groups[0]:
            copy.wait()
        vectors_ref[...] = jnp.sum(lines_ref[...].astype(WIDE), 0)

    def add_sum(k, value):
        sums_ref[k : k + 1] += jnp.sum(value, 0, keepdims=True)

    grad = jnp.where(2 * at <= last, grad_first_ref[...], grad_last_ref[...]).astype(WIDE)
    unit_two = unit_two_ref[...]
    add_sum(4, grad * unit_two)
    add_sum(5, grad)
    grad_normed = norm_back(grad, unit_two, scales_ref[:, 64:65], vectors_ref[4:5])
    grad_down = grad_normed.astype(LOW)
    down_ref[rows] = grad_down
    add_sum(3, grad_down.astype(WIDE))
    for c in range(chunks):
        lanes = slice(width * c, width * c + width)
        grad_pre = dot(grad_down, w_down_ref[lanes], NT) * slope_ref[:, lanes].astype(WIDE)
        grad_pre = grad_pre.astype(LOW)
        pre_ref[rows, lanes] = grad_pre
        add_sum(6 + c, grad_pre.astype(WIDE))
        grad_normed = grad_normed + dot(grad_pre, w_in_ref[c], NT)
    unit_one = unit_one_ref[...]
    add_sum(1, grad_normed * unit_one)
    add_sum(2, grad_normed)
    grad_branch = norm_back(grad_normed, unit_one, scales_ref[:, 0:1], vectors_ref[1:2]).astype(LOW)
    first_ref[...] = grad_branch
    branch_ref[rows] = grad_branch
    add_sum(0, grad_branch.astype(WIDE))
    mine_ref[...] = dot(grad_branch, w_in_ref[chunks, here], NT).astype(LOW)
    theirs_ref[...] = dot(grad_branch, w_in_ref[chunks, there], NT).astype(LOW)

    @pl.when(at == last)
    def _():
        for copy in extra:
            copy.wait()
        moving = []
        span, span_ff = width // (2 * chips), wide // (2 * chips)
        first = span * (chunks + 1)

        def leave(pairs):
            for source, target in pairs:
                copy = pltpu.make_async_copy(source, target, out_sems.at[len(moving)])
                copy.start()
                moving.append(copy)

        def leave_rows(c):
            if not direct:
                return leave([(w_in_ref.at[c], grad_refs[0].at[c])])
            for k, target in enumerate(grad_refs):
                for q in range(chips):
                    place = 2 * q + (core if k == 0 else 1 - core)
                    source = w_in_ref.at[c, pl.ds(pl.multiple_of(place * span, span), span)]
                    leave([(source, target.at[q, span * c : span * c + span])])

        for c in range(chunks):
            lanes = slice(width * c, width * c + width)
            w_down_ref[lanes] = dot(hidden_ref[:, lanes], down_ref[...], TN).astype(LOW)
            if direct:
                for k, target in enumerate(grad_refs):
                    place = 2 * c + (core if k == 0 else 1 - core)
                    source = w_down_ref.at[pl.ds(pl.multiple_of(place * span_ff, span_ff), span_ff)]
                    leave([(source, target.at[c, first : first + span_ff])])
            else:
                leave([(w_down_ref.at[lanes], grad_refs[1].at[lanes])])
            w_in_ref[c] = dot(normed_ref[...], pre_ref[:, lanes], TN).astype(LOW)
            leave_rows(c)
        w_in_ref[chunks, here] = dot(mixed_ref[...], branch_ref[...], TN).astype(LOW)
        w_in_ref[chunks, there] = dot(other_ref[...], branch_ref[...], TN).astype(LOW)
        leave_rows(chunks)
        for copy in moving:
            copy.wait()


IN_SMEM = pl.BlockSpec(memory_space=pltpu.SMEM)
IN_VMEM = pl.BlockSpec(memory_space=pltpu.VMEM)


IN_ANY = pl.BlockSpec(memory_space=pl.ANY)


TILE = 256


def tiles(width, first=0, many=None):
    if many is None:
        return pl.BlockSpec((TILE, width), lambda i: (i, 0))
    return pl.BlockSpec((TILE, width), lambda i: (jnp.clip(i - first, 0, many - 1), 0))


def project_tokens(at, pieces, b_qkv, weights, direct):
    length, width = 4 * pieces[0].shape[0], pieces[0].shape[1]
    half = width // 2
    chips = lax.axis_size("dp") // 2
    many = pieces[0].shape[0] // TILE

    def all_of(*shape):
        return pl.BlockSpec(shape, lambda i: (0, 0))

    return pl.pallas_call(
        partial(project_kernel, chips, direct),
        grid=(length // TILE,),
        out_shape=(
            jax.ShapeDtypeStruct((length, 3 * half), LOW),
            jax.ShapeDtypeStruct((length, width), LOW),
            jax.ShapeDtypeStruct((width, 3 * half), LOW),
        ),
        in_specs=[IN_SMEM]
        + [tiles(width, many * k, many) for k in range(4)]
        + [all_of(1, 3 * half)]
        + [IN_ANY] * len(weights),
        out_specs=(tiles(3 * half), tiles(width), all_of(width, 3 * half)),
        scratch_shapes=[pltpu.SemaphoreType.DMA((2 * chips,))],
        compiler_params=pltpu.CompilerParams(vmem_limit_bytes=48 << 20),
        cost_estimate=pl.CostEstimate(flops=1, bytes_accessed=1, transcendentals=0),
        name="project",
    )(at, *pieces, b_qkv, *weights)


def attend(near, rand, globs, bias, qkv):
    length, width = qkv.shape
    pairs, blocks = width // 384, length // BLOCK
    return pl.pallas_call(
        partial(attend_kernel, pairs, blocks, 4),
        out_shape=(
            jax.ShapeDtypeStruct((length, 128 * pairs), LOW),
            jax.ShapeDtypeStruct((blocks, 8, 128), WIDE),
        ),
        in_specs=[IN_SMEM] * 3 + [IN_VMEM] * 2,
        out_specs=(IN_VMEM,) * 2,
        compiler_params=pltpu.CompilerParams(vmem_limit_bytes=48 << 20),
        cost_estimate=pl.CostEstimate(flops=1, bytes_accessed=1, transcendentals=0),
        name="attend",
    )(near, rand, globs, bias, qkv)


def attend_back(near, rand, globs, bias, log_total, qkv, mine, come, w_qkv, grad_first, tokens):
    length, (wide, width) = qkv.shape[0], w_qkv.shape
    pairs, blocks = width // 384, length // BLOCK
    rows = jax.ShapeDtypeStruct((length // 2, wide), LOW)
    return pl.pallas_call(
        partial(attend_back_kernel, blocks, 2),
        out_shape=(
            jax.ShapeDtypeStruct((wide, width), LOW),
            rows,
            rows,
            jax.ShapeDtypeStruct((1, width), WIDE),
        ),
        in_specs=[IN_SMEM] * 3 + [IN_VMEM] * 8,
        out_specs=(IN_VMEM,) * 4,
        scratch_shapes=[
            pltpu.VMEM((length, width), LOW),
            pltpu.VMEM((length, 128 * pairs), LOW),
            pltpu.VMEM((length, 256 * pairs), WIDE),
        ],
        compiler_params=pltpu.CompilerParams(vmem_limit_bytes=56 << 20),
        cost_estimate=pl.CostEstimate(flops=1, bytes_accessed=1, transcendentals=0),
        name="attend_back",
    )(near, rand, globs, bias, log_total, qkv, mine, come, w_qkv, grad_first, tokens)


def pack_columns(at, shard, near, mirror, rows_in):
    two, rows, width = shard.shape
    rows = 4 * rows_in + 2 * (rows - rows_in)
    return pl.pallas_call(
        partial(pack_columns_kernel, 4, rows_in),
        out_shape=jax.ShapeDtypeStruct((two, rows, width), LOW),
        in_specs=[IN_SMEM] + [IN_VMEM] * 3,
        out_specs=IN_VMEM,
        cost_estimate=pl.CostEstimate(flops=1, bytes_accessed=1, transcendentals=0),
        name="pack_columns",
    )(at, shard, near, mirror)


def pack_rows(at, shard, near, mirror, chunks, cut):
    rows, width = 4 * (shard.shape[0] - 16) + 16, shard.shape[1]
    return pl.pallas_call(
        partial(pack_kernel, 4, chunks, cut),
        out_shape=(
            jax.ShapeDtypeStruct((cut, width), LOW),
            jax.ShapeDtypeStruct((rows - cut, width), LOW),
        ),
        in_specs=[IN_SMEM] + [IN_VMEM] * 3,
        out_specs=(IN_VMEM, IN_VMEM),
        cost_estimate=pl.CostEstimate(flops=1, bytes_accessed=1, transcendentals=0),
        name="pack",
    )(at, shard, near, mirror)


def weight_space(chips, direct, chunks, width):
    return [
        pltpu.VMEM((chunks + 1, width, width), LOW),
        pltpu.VMEM((chunks * width, width), LOW),
        pltpu.VMEM((2 * chips if direct else 1, 16, width), LOW),
    ]


def unpack_rows(at, upper, lower, chunks):
    rows, width = upper[0].shape[0] + lower[0].shape[0], upper[0].shape[1]
    like = jax.ShapeDtypeStruct((2, rows // 4, width), LOW)
    return pl.pallas_call(
        partial(unpack_kernel, 4, chunks, len(upper)),
        out_shape=(like, like),
        in_specs=[IN_SMEM] + [IN_VMEM] * (len(upper) + len(lower)),
        out_specs=(IN_VMEM, IN_VMEM),
        cost_estimate=pl.CostEstimate(flops=1, bytes_accessed=1, transcendentals=0),
        name="unpack",
    )(at, *upper, *lower)


def layer_forward(at, mixed, other, tokens, weights, direct, chunks):
    own, width = other.shape[0], tokens.shape[1]
    chips, wide = lax.axis_size("dp") // 2, chunks * width

    def rows(width, kind=LOW):
        return jax.ShapeDtypeStruct((own, width), kind)

    return pl.pallas_call(
        partial(forward_kernel, chips, direct),
        grid=(own // TILE,),
        out_shape=(rows(width), rows(wide), rows(wide), rows(width))
        + (rows(width, WIDE), rows(width, WIDE), rows(128, WIDE)),
        in_specs=[IN_SMEM]
        + [tiles(p.shape[1]) for p in (mixed, other, tokens)]
        + [IN_ANY] * len(weights),
        out_specs=tuple(tiles(w) for w in (width, wide, wide, width, width, width, 128)),
        scratch_shapes=weight_space(chips, direct, chunks, width)
        + [pltpu.SemaphoreType.DMA((2 * chips * (chunks + 4),))],
        compiler_params=pltpu.CompilerParams(vmem_limit_bytes=58 << 20),
        cost_estimate=pl.CostEstimate(flops=1, bytes_accessed=1, transcendentals=0),
        name="layer_forward",
    )(at, mixed, other, tokens, *weights)


def layer_backward(at, mixed, other, grads, slope, units, scales, hidden, normed, weights, direct):
    own, width = normed.shape
    wide = slope.shape[1]
    half, chunks = width // 2, wide // width
    chips = lax.axis_size("dp") // 2
    many = own // TILE // 2
    whole = pl.BlockSpec((own, half), lambda i: (0, 0))
    if direct:
        rows = ((chunks + 1) * width + wide) // (2 * chips)
        grads_like = (jax.ShapeDtypeStruct((chips, rows, width), LOW),) * 2
    else:
        grads_like = (
            jax.ShapeDtypeStruct((chunks + 1, width, width), LOW),
            jax.ShapeDtypeStruct((wide, width), LOW),
        )
    return pl.pallas_call(
        partial(backward_kernel, TILE, chips, direct),
        grid=(own // TILE,),
        out_shape=(
            jax.ShapeDtypeStruct((own, width), LOW),
            jax.ShapeDtypeStruct((own, half), LOW),
            jax.ShapeDtypeStruct((own, half), LOW),
            jax.ShapeDtypeStruct((16, width), WIDE),
        )
        + grads_like,
        in_specs=[IN_SMEM]
        + [whole, whole]
        + [tiles(width, 0, many), tiles(width, many, many)]
        + [tiles(wide), tiles(width), tiles(width), tiles(128)]
        + [IN_ANY] * (2 + len(weights)),
        out_specs=(tiles(width), tiles(half), tiles(half))
        + (pl.BlockSpec((16, width), lambda i: (0, 0)),)
        + (IN_ANY,) * 2,
        scratch_shapes=weight_space(chips, direct, chunks, width)
        + [
            pltpu.VMEM((16, width), WIDE),
            pltpu.VMEM((own, wide), LOW),
            pltpu.VMEM((own, width), LOW),
            pltpu.VMEM((own, width), LOW),
            pltpu.VMEM((own, wide), LOW),
            pltpu.VMEM((own, width), LOW),
            pltpu.SemaphoreType.DMA((2 * chips * (chunks + 4),)),
            pltpu.SemaphoreType.DMA((2,)),
            pltpu.SemaphoreType.DMA((2 * chips * (chunks + 1) + 2 * chunks,)),
        ],
        compiler_params=pltpu.CompilerParams(vmem_limit_bytes=58 << 20),
        cost_estimate=pl.CostEstimate(flops=1, bytes_accessed=1, transcendentals=0),
        name="layer_backward",
    )(at, mixed, other, *grads, slope, *units, scales, hidden, normed, *weights)


def place_of(block, core, z, blocks):
    quarter, row = block // (blocks // 4), block % (blocks // 4)
    a = (quarter & 1) ^ (z & 1)
    return ((quarter >> 1) ^ core) * (blocks // 2) + a * (blocks // 4) + row


def block_at(place, core, z, blocks):
    quarter = 2 * ((place // (blocks // 2)) ^ core) + ((place % (blocks // 2)) // (blocks // 4) ^ (z & 1))
    return quarter * (blocks // 4) + place % (blocks // 4)


def tables(rand, globs, blocks):
    core = lax.axis_index("dp") & 1
    z = lax.axis_index("seq")
    here = block_at(jnp.arange(blocks, dtype=jnp.int32), core, z, blocks)
    heads = rand.shape[0]
    one, two = globs[0], globs[1]

    def near(block):
        return jnp.abs(block - here) <= 1

    every = jnp.ones((heads, blocks), bool)
    ok = [every & (here > 0), every, every & (here < blocks - 1)]
    ok += [every & ~near(one), every & ~near(two) & (one != two)]
    seen = []
    for r in range(3):
        block = rand[:, :, r]
        good = ~near(block) & (block != one) & (block != two)
        for before in seen:
            good = good & (block != before)
        seen.append(block)
        ok.append(good)
    whole_row = (here == one) | (here == two)
    ok = jnp.stack(ok, -1) & ~whole_row[None, :, None]
    bias = jnp.where(ok, 0.0, NEG).astype(WIDE)
    bias = bias.reshape(heads // 2, 2, blocks, SLOTS).transpose(2, 0, 3, 1)
    bias = jnp.repeat(bias, HEAD, axis=3)
    put = partial(place_of, core=core, z=z, blocks=blocks)
    sides = jnp.concatenate([put(jnp.maximum(here - 1, 0)), put(jnp.minimum(here + 1, blocks - 1))])
    return sides, put(rand).reshape(-1), put(globs), bias


def shards(
    inputs,
    cotangent,
    rand_blocks,
    global_blocks,
    w_query,
    b_query,
    w_key,
    w_value,
    b_value,
    w_out,
    b_out,
    gain_one,
    shift_one,
    w_up,
    b_up,
    w_down,
    b_down,
    gain_two,
    shift_two,
):
    n_dp, n_seq = lax.axis_size("dp"), lax.axis_size("seq")
    chips, devices = n_dp // 2, n_dp * n_seq
    core = lax.axis_index("dp") & 1
    z = lax.axis_index("seq")
    device = lax.axis_index("dp") * n_seq + z
    rows_in, width = w_query.shape
    rows_ff, wide = w_down.shape[0], w_up.shape[1]
    chunks = wide // width
    half_width = width // 2
    _, quarter, _ = inputs.shape
    length = quarter * n_seq
    blocks = length // BLOCK
    own = length // 2
    own_heads = HEADS // 2
    span, span_ff = n_seq * rows_in, n_seq * rows_ff
    direct = span % 16 == 0 and chips == chunks

    here = jnp.arange(devices, dtype=jnp.int32)[:, None] == device

    def placed(vector):
        return jnp.where(here, vector[None], jnp.zeros((), LOW)).reshape(-1, width)

    q_line, v_line = placed(b_query), placed(b_value)

    pairs = half_width // 128

    def side(at):
        no_line = jnp.zeros((1, width), LOW)
        parts = []
        for pair in range(pairs):
            first = at * half_width + 128 * pair
            lanes = slice(first, first + 128)
            for w, line in ((w_query, q_line), (w_key, no_line), (w_value, v_line)):
                parts.append(jnp.concatenate([w[:, lanes], line[:, lanes]], 0))
        return jnp.pad(jnp.concatenate(parts, 1), ((0, 7), (0, 0)))

    left, right = side(0), side(1)
    keep = jnp.where(core == 0, left, right)
    come = swap(jnp.where(core == 0, right, left))
    shard = jnp.stack([jnp.where(core == 0, keep, come), jnp.where(core == 0, come, keep)])
    def numbers_of(s):
        numbers = pick(rand_blocks, s, 0).reshape(-1)
        numbers = jnp.concatenate([numbers, pick(global_blocks, s, 0).reshape(-1)])
        return jnp.pad(numbers, (0, -numbers.shape[0] % 128))

    numbers = jnp.stack(bring(numbers_of))
    qkv_z = gather_seq(tie(shard, numbers))

    packed = jnp.concatenate(
        [w_up[:, width * c : width * c + width] for c in range(chunks)]
        + [w_out, w_down]
        + [placed(v) for v in (b_out, gain_one, shift_one, b_down, gain_two, shift_two, b_up)]
        + [jnp.zeros((16 - 6 - chunks, width), LOW)],
        0,
    )
    wide_z = gather_seq(tie(packed, shard), qkv_z[2])
    at = jnp.stack([lax.axis_index("dp") >> 1, core, z]).astype(jnp.int32)

    direct = span % 16 == 0 and chips == chunks
    if direct:
        whole = pack_columns(at, *qkv_z, rows_in)
    else:
        qkv_z = in_seq_order(*qkv_z)
        whole = []
        for k in range(2):
            lines = sum(p[k, rows_in:].astype(WIDE) for p in qkv_z).astype(LOW)
            whole += [p[k, :rows_in] for p in qkv_z] + [lines, jnp.zeros_like(lines)]
        whole = jnp.concatenate(whole, 0).reshape(2, span + 16, 3 * half_width)
    qkv_parts = gather_chips(whole)
    numbers = tie(numbers, whole)
    numbers = jnp.concatenate([numbers, swap(numbers)], 0)
    local_blocks = rand_blocks.shape[2]
    count = HEADS * local_blocks * 3
    globs = numbers[0, count : count + 2]
    rand = numbers[:, :count].reshape(4, HEADS, local_blocks, 3)
    rand = lax.dynamic_slice_in_dim(rand, core * own_heads, own_heads, 1)
    rand = rand.transpose(1, 0, 2, 3).reshape(own_heads, blocks, 3)
    sides, rand, glob_at, bias = tables(rand, globs, blocks)


    tied_inputs = tie(inputs, qkv_z[2])
    pieces = bring(lambda s: pick(tied_inputs, s, 0)[0])

    if direct:
        cut = chunks * span + span // 2
        near, pieces[0], bias, sides, rand, glob_at, *qkv_parts = join(
            wide_z[1], pieces[0], bias, sides, rand, glob_at, *qkv_parts
        )
        whole = pack_rows(at, wide_z[0], near, wide_z[2], chunks + 1, cut)
    else:
        wide_z = in_seq_order(*wide_z)
        rows_a = (chunks + 1) * rows_in
        rows = []
        for c in range(chunks + 1):
            rows += [p[c * rows_in : (c + 1) * rows_in] for p in wide_z]
        rows += [p[rows_a : rows_a + rows_ff] for p in wide_z]
        rows.append(sum(p[rows_a + rows_ff :].astype(WIDE) for p in wide_z).astype(LOW))
        whole = jnp.concatenate(rows, 0)
    if direct:
        lines = sum(jnp.sum(p[:, span].astype(WIDE), 0, keepdims=True) for p in qkv_parts)
        *parts, lines, pieces[0], pieces[1] = join(*gather_quads(*whole), lines, *pieces)
    else:
        parts = gather_chips(tie(whole, qkv_parts))
        lines = sum(jnp.sum(p[:, span].astype(WIDE), 0, keepdims=True) for p in qkv_parts)
    pieces = [*pieces, *(swap(p) for p in pieces)]
    rows_a, rows_b = (chunks + 1) * span, (chunks + 1) * span + span_ff
    if direct:
        qkv_weights = tuple(qkv_parts)
    else:
        ordered = in_chip_order(qkv_parts)
        qkv_weights = (jnp.concatenate([p[k, :span] for p in ordered for k in range(2)], 0),)

    if direct:
        upper, lower = jnp.stack(parts[:2]), jnp.stack(parts[2:])
        parts = [upper, flip_chip(upper, 2), lower, flip_chip(lower, 1)]
        other_parts = [swap(upper), None, swap(lower), None]
    qkv, tokens, w_qkv = project_tokens(at, pieces, lines, qkv_weights, direct)
    mixed, log_total = attend(sides, rand, glob_at, bias, qkv)
    tied = tie(cotangent, qkv)
    first_grads = bring_round(lambda s: pick(tied, s, 0)[0], 0)
    mixed, log_total, first_grads, *parts = join(mixed, log_total, first_grads, *parts)
    other = swap(mixed[own:])
    if direct:
        other_parts[1], other_parts[3] = swap(parts[1]), swap(parts[3])
    else:
        other_parts = [swap(p) for p in parts]
    if direct:
        weights = tuple(parts + other_parts)
    else:
        weights = (
            jnp.stack(
                [
                    in_device_order(
                        *([p[span * c : span * c + span] for p in ps] for ps in (parts, other_parts))
                    )
                    for c in range(chunks + 1)
                ]
            ),
            in_device_order(*([p[rows_a:rows_b] for p in ps] for ps in (parts, other_parts))),
            sum(p[rows_b:].astype(WIDE) for p in parts + other_parts).astype(LOW)[None],
        )
    tied = tie(cotangent, mixed)
    grad_result = first_grads, bring_round(lambda s: pick(tied, s, 0)[0], 1)
    forward = layer_forward(at, mixed, other, tokens, weights, direct, chunks)
    forward, grad_result = join(forward, grad_result)
    result, hidden, slope, normed, unit_one, unit_two, scales = forward
    output = send_back(result)
    backward = layer_backward(
        at,
        mixed,
        other,
        grad_result,
        slope,
        (unit_one, unit_two),
        scales,
        hidden,
        normed,
        weights,
        direct,
    )
    backward, output = join(backward, output)
    grad_first, mine, theirs, in_sums, grad_in, grad_down = backward

    come = swap(theirs)
    if direct:
        chip = lax.axis_index("dp") >> 1
        x, y = chip & 1, chip >> 1
        grad_other, come = join(swap(grad_down), come)
        cut = chunks * span + span // 2
        both = [p.reshape(2, 2, -1, width) for p in (grad_in, grad_other)]
        moves = [
            added(*(pick(p[:, :, rows], which, axis) for p in both))
            for rows, axis, own_side in ((slice(0, cut), 1, x), (slice(cut, None), 0, y))
            for which in (own_side, 1 - own_side)
        ]
        mine, come, *moves = join(mine, come, *moves)
        moves[1], moves[3] = flip_chip(moves[1], 1), flip_chip(moves[3], 2)
    grad_w_qkv, grad_own, grad_theirs, sums = attend_back(
        sides,
        rand,
        glob_at,
        bias,
        log_total,
        qkv,
        mine,
        come,
        w_qkv,
        grad_first,
        tokens,
    )
    if direct:
        grad_w_qkv, grad_own, grad_theirs, sums, *moves = join(
            grad_w_qkv, grad_own, grad_theirs, sums, *moves
        )
    come_rows = swap(grad_theirs)
    if direct:
        moves = [
            added(*(pick(p, which, axis) for p in pair))
            for pair, axis, own_side in ((moves[:2], 0, y), (moves[2:], 1, x))
            for which in (own_side, 1 - own_side)
        ]
        grad_own, *moves = join(grad_own, *(move.reshape(-1, width) for move in moves))
        moves[1], moves[3] = flip_chip(moves[1], 2), flip_chip(moves[3], 1)
    grad_inputs = [added(*pair) for pair in zip(start_back(grad_own), start_back(come_rows))]
    first_back = finish_back(grad_inputs, 0)
    vectors = in_sums[: 6 + chunks].reshape(-1)
    vectors = jnp.pad(vectors, (0, -vectors.shape[0] % (3 * half_width))).reshape(-1, 3 * half_width)
    lines = jnp.concatenate([sums, vectors], 0).astype(LOW)
    lines = jnp.broadcast_to(lines, (chips, 2, n_seq) + lines.shape)
    parts = jnp.concatenate(
        [grad_w_qkv.reshape(chips, 2, n_seq, rows_in, 3 * half_width), lines], 3
    )
    keep, come = (pick(parts, which, 1)[:, 0] for which in (core, 1 - core))
    come = swap(come)
    parts = jnp.stack([keep, come], 1)
    if direct:
        first_back, *moves = join(first_back, *moves)
        near_sums, keep_sums = unpack_rows(at, moves[:2], moves[2:], chunks + 1)
    else:
        rows = lax.psum_scatter(grad_in, "dp", scatter_dimension=1, tiled=True)
        rows = rows.reshape((chunks + 1) * span, width)
        down = lax.psum_scatter(grad_down, "dp", scatter_dimension=0, tiled=True)
        near_sums, keep_sums = unpack_rows(at, [rows], [down], chunks + 1)
    grad_inputs = first_back, finish_back(grad_inputs, 1)
    near_sums = flip_seq(near_sums, 1)
    parts = reduce_chips(parts)
    parts, near_sums = join(parts, near_sums)
    own_qkv = reduce_seq(parts.transpose(1, 0, 2, 3))
    keep, come = own_qkv[0], own_qkv[1]
    left, right = jnp.where(core == 0, keep, come), jnp.where(core == 0, come, keep)

    mirror = flip_seq(added(keep_sums[1], near_sums[1]), 3)
    own_sums = sum(p.astype(WIDE) for p in (keep_sums[0], near_sums[0], mirror))
    rows_a = (chunks + 1) * rows_in
    own_up = jnp.concatenate(
        [own_sums[c * rows_in : (c + 1) * rows_in] for c in range(chunks)], 1
    )
    small = (keep + come)[rows_in + 1 :].reshape(-1)[: (6 + chunks) * width].reshape(-1, width)

    def joined(k, rows):
        lanes = [lanes_of(k, pair) for pair in range(pairs)]
        return jnp.concatenate([one[rows, at] for one in (left, right) for at in lanes], 1)

    def own_part(vector, size):
        return lax.dynamic_slice_in_dim(vector.reshape(-1), device * size, size, 0)

    six = lax.dynamic_slice_in_dim(small[:6], device * rows_in, rows_in, 1)

    matrix_rows, line = slice(0, rows_in), slice(rows_in, rows_in + 1)
    return (
        in_sequences(output),
        in_sequences(grad_inputs),
        joined(0, matrix_rows),
        own_part(joined(0, line), rows_in),
        joined(1, matrix_rows),
        joined(2, matrix_rows),
        own_part(joined(2, line), rows_in),
        own_sums[chunks * rows_in : rows_a],
        six[0],
        six[1],
        six[2],
        own_up,
        own_part(small[6 : 6 + chunks], rows_ff),
        own_sums[rows_a : rows_a + rows_ff],
        six[3],
        six[4],
        six[5],
    )


def solution(mesh):
    both = ("dp", "seq")
    matrix, vector = P(both, None), P(both)
    tokens = P("dp", "seq", None)
    return jax.shard_map(
        shards,
        mesh=mesh,
        in_specs=(tokens, tokens, P("dp", None, "seq", None), P("dp", None))
        + (matrix, vector, matrix, matrix, vector, matrix, vector, vector, vector)
        + (matrix, vector, matrix, vector, vector, vector),
        out_specs=(tokens, tokens)
        + (matrix, vector, matrix, matrix, vector, matrix, vector, vector, vector)
        + (matrix, vector, matrix, vector, vector, vector),
        check_vma=False,
    )
```
